32 devices in a mesh: grp: 4 (over x, core), inner: 8 (over z, y).
Axes of the slice: x: 2, y: 2, z: 4, core: 2. Of those that a mesh axis runs over, the one named last changes fastest.
Arguments:
- electric: float32 [3, 16, 128, 512], P(None, None, 'inner', 'grp'), may hold values from -6 to 6
- magnetic: float32 [3, 16, 128, 512], P(None, None, 'inner', 'grp'), may hold values from -6 to 6
- material_ids: int32 [16, 128, 512], P(None, 'inner', 'grp'), may hold values from 0 to 7
- update_ca: float32 [8], replicated, may hold values from 0.6 to 1
- update_cb: float32 [8], replicated, may hold values from 0.12 to 0.45
- face_ranges: int32 [8, 4, 4], P('inner', 'grp'), may hold values from 0 to 128, as said below
- band_table: int32 [32], replicated, may hold values from 0 to 31, each once
Outputs:
- electric_out: float32 [3, 16, 128, 512], P(None, None, 'inner', 'grp')
- magnetic_out: float32 [3, 16, 128, 512], P(None, None, 'inner', 'grp')
- far_field: float32 [32, 8, 128], P(('grp', 'inner'))
The draws below stay inside these ranges and needn't reach their ends.
Inputs may be any that keep to these rules, and one draw needn't show every extreme that they name: `face_ranges`: one box [x0, x1) x [y0, y1) with x0 <= 32, x1 >= 96, y0 <= 128, y1 >= 384 is clipped to each tile: entries are (clip(x0 - i * 16), clip(x1 - i * 16), clip(y0 - j * 128), clip(y1 - j * 128)), each clip into [0, tile width].
All inputs are finite; a program needn't handle non-finite values.
Results may differ from the reference program's by a relative error of at most 0.0003.
Values sent between devices are 32-bit elements; how exact they have to be, the bound alone decides.
A program may use at most 64 MiB of HBM per device.

```python
import math
import jax
import jax.numpy as jnp
from jax import lax

CX = 16
CY = 128
NZ = 16
STEPS = 8
FREQS = 32
ANG_BAND = 4
NMAT = 8
ZF = 8
NX = 128
NY = 512
BANDS = 32


def draw_face_ranges(key, part):
    keys = jax.random.split(key, 4)
    x_low = jax.random.randint(keys[0], (), 0, NX // 4 + 1)
    x_high = jax.random.randint(keys[1], (), NX - NX // 4, NX + 1)
    y_low = jax.random.randint(keys[2], (), 0, NY // 4 + 1)
    y_high = jax.random.randint(keys[3], (), NY - NY // 4, NY + 1)
    start_x = jnp.arange(NX // CX, dtype=jnp.int32) * CX
    start_y = jnp.arange(NY // CY, dtype=jnp.int32) * CY
    low_x = jnp.clip(x_low - start_x, 0, CX)
    high_x = jnp.clip(x_high - start_x, 0, CX)
    low_y = jnp.clip(y_low - start_y, 0, CY)
    high_y = jnp.clip(y_high - start_y, 0, CY)
    grid_shape = (NX // CX, NY // CY)
    return jnp.stack([jnp.broadcast_to(low_x[:, None], grid_shape), jnp.broadcast_to(high_x[:, None], grid_shape), jnp.broadcast_to(low_y[None, :], grid_shape), jnp.broadcast_to(high_y[None, :], grid_shape)], axis=-1).astype(jnp.int32)


def set_ends(drawn, key, least, largest):
    spot = [jax.random.randint(jax.random.fold_in(key, axis), (), 0, length) for axis, length in enumerate(drawn.shape)]
    widest = drawn.shape.index(max(drawn.shape))
    next_to = spot[:widest] + [(spot[widest] + 1) % drawn.shape[widest]] + spot[widest + 1:]
    return drawn.at[tuple(spot)].set(least).at[tuple(next_to)].set(largest)


def steps_of(stream_key, shape, shards, low, high):
    level, own = 1.0, jax.random.fold_in(stream_key, 6)
    for dim, parts in shards:
        heights = jnp.exp(jax.random.uniform(jax.random.fold_in(own, dim), (parts,), jnp.float32, low / len(shards), high / len(shards)))
        level = level * jnp.repeat(heights, shape[dim] // parts).reshape([-1 if axis == dim else 1 for axis in range(len(shape))])
    return level


def normal_values(key, extent, deviation, limit, cuts=(), kind=jnp.bfloat16):
    gain = steps_of(key, extent, cuts, -0.22, 0.18) if cuts else 1.0
    result = jax.random.normal(key, extent, jnp.float32) * deviation * gain
    return jnp.minimum(jnp.maximum(result, -limit), limit).astype(kind)


def setup_inputs(seed: int = 0) -> dict:
    seeds = jax.random.split(jax.random.key(seed), 8)
    electric = normal_values(seeds[0], (3, NZ, NX, NY), 1.0, 6.0, ((2, 8), (3, 4)), jnp.float32)
    magnetic = normal_values(seeds[1], (3, NZ, NX, NY), 1.0, 6.0, ((2, 8), (3, 4)), jnp.float32)
    material_ids = set_ends(jax.random.randint(seeds[2], (NZ, NX, NY), 0, NMAT), jax.random.fold_in(seeds[2], 1), 0, NMAT - 1).astype(jnp.int32)
    update_ca = jnp.clip(jax.random.uniform(seeds[3], (NMAT,), jnp.float32, 0.6, 1.0), 0.6, 1.0)
    update_cb = jnp.clip(jnp.exp(jax.random.uniform(seeds[4], (NMAT,), jnp.float32, math.log(0.12), math.log(0.45))), 0.12, 0.45)
    face_ranges = draw_face_ranges(jax.random.fold_in(seeds[7], 71), 0)
    band_table = jax.random.permutation(seeds[6], BANDS).astype(jnp.int32)
    return {"electric": electric, "magnetic": magnetic, "material_ids": material_ids, "update_ca": update_ca, "update_cb": update_cb, "face_ranges": face_ranges, "band_table": band_table}


def forward_diff(field, axis):
    size = field.shape[axis]
    rest = lax.slice_in_dim(field, 1, size, axis=axis)
    edge = jnp.zeros_like(lax.slice_in_dim(field, 0, 1, axis=axis))
    return jnp.concatenate([rest, edge], axis) - field

def backward_diff(field, axis):
    size = field.shape[axis]
    rest = lax.slice_in_dim(field, 0, size - 1, axis=axis)
    edge = jnp.zeros_like(lax.slice_in_dim(field, 0, 1, axis=axis))
    return field - jnp.concatenate([edge, rest], axis)

def curl_with(field, diff):
    curl_x = diff(field[2], 2) - diff(field[1], 0)
    curl_y = diff(field[0], 0) - diff(field[2], 1)
    curl_z = diff(field[1], 1) - diff(field[0], 2)
    return jnp.stack([curl_x, curl_y, curl_z])

def reference(electric, magnetic, material_ids, update_ca, update_cb, face_ranges, band_table):
    highest = lax.Precision.HIGHEST
    coef_a = update_ca[material_ids]
    coef_b = update_cb[material_ids]
    xcells = jnp.arange(NX, dtype=jnp.int32)
    ycells = jnp.arange(NY, dtype=jnp.int32)
    tile_x = (xcells // CX)[:, None]
    tile_y = (ycells // CY)[None, :]
    local_x = (xcells % CX)[:, None]
    local_y = (ycells % CY)[None, :]
    face_mask = (local_x >= face_ranges[tile_x, tile_y, 0]) & (local_x < face_ranges[tile_x, tile_y, 1]) & (local_y >= face_ranges[tile_x, tile_y, 2]) & (local_y < face_ranges[tile_x, tile_y, 3])
    face_mask = face_mask.astype(jnp.float32)
    recorded = []
    for iteration in range(STEPS):
        magnetic = magnetic - 0.5 * curl_with(electric, forward_diff)
        electric = coef_a * electric + coef_b * curl_with(magnetic, backward_diff)
        recorded.append(jnp.stack([electric[0, ZF], electric[1, ZF], magnetic[0, ZF], magnetic[1, ZF]]) * face_mask)
    samples = jnp.stack(recorded)
    times = jnp.arange(STEPS, dtype=jnp.int32)
    ones_f = jnp.arange(FREQS, dtype=jnp.int32) + 1
    turns = ones_f[:, None] * times[None, :] % 128
    dft_angle = turns.astype(jnp.float32) * jnp.float32(2.0 * math.pi / 128.0)
    dft_cos = jnp.cos(dft_angle)
    dft_sin = jnp.sin(dft_angle)
    b_dirs = jnp.arange(ANG_BAND, dtype=jnp.int32) * 33 // ANG_BAND - 16
    a_dirs = band_table.astype(jnp.int32) - BANDS // 2
    scale = 1.0 / math.sqrt(NX * NY)

    def one_freq(freq_idx):
        mult = freq_idx + 1
        cur_re = jnp.einsum('n,ncxy->cxy', dft_cos[freq_idx], samples, precision=highest)
        cur_im = -jnp.einsum('n,ncxy->cxy', dft_sin[freq_idx], samples, precision=highest)
        turn_y = mult * ycells[:, None] * b_dirs[None, :] % 4096
        ang_y = turn_y.astype(jnp.float32) * jnp.float32(2.0 * math.pi / 4096.0)
        cos_y = jnp.cos(ang_y)
        sin_y = jnp.sin(ang_y)
        col_re = jnp.einsum('cxy,yq->cxq', cur_re, cos_y, precision=highest) - jnp.einsum('cxy,yq->cxq', cur_im, sin_y, precision=highest)
        col_im = jnp.einsum('cxy,yq->cxq', cur_re, sin_y, precision=highest) + jnp.einsum('cxy,yq->cxq', cur_im, cos_y, precision=highest)
        turn_x = mult * a_dirs[:, None] * xcells[None, :] % 4096
        ang_x = turn_x.astype(jnp.float32) * jnp.float32(2.0 * math.pi / 4096.0)
        cos_x = jnp.cos(ang_x)
        sin_x = jnp.sin(ang_x)
        far_re = jnp.einsum('px,cxq->pcq', cos_x, col_re, precision=highest) - jnp.einsum('px,cxq->pcq', sin_x, col_im, precision=highest)
        far_im = jnp.einsum('px,cxq->pcq', sin_x, col_re, precision=highest) + jnp.einsum('px,cxq->pcq', cos_x, col_im, precision=highest)
        return (far_re, far_im)
    far_re, far_im = lax.map(one_freq, jnp.arange(FREQS, dtype=jnp.int32))
    joined = jnp.concatenate([far_re, far_im], axis=2)
    joined = jnp.transpose(joined, (1, 2, 3, 0)).reshape(BANDS, 8, ANG_BAND * FREQS)
    return (electric, magnetic, joined * scale)
```

```python
import functools
import math

import jax
import jax.numpy as jnp
import numpy as np
from jax import lax
from jax.experimental import pallas as pl
from jax.experimental.pallas import tpu as pltpu
from jax.sharding import PartitionSpec as P

STEPS = 8
FREQS = 32
ANG_BAND = 4
NMAT = 8
ZF = 8
NZ = 16
CX = 16
CY = 128
PAD = 8
HALO = 8
ROWS = CX + 2 * HALO
PITCH = ROWS + 2 * PAD
GROUPS = ROWS // 8
OWN = (1, 2)
HALF = NZ // 2
SIDE = CY // 4
MESH = pl.DeviceIdType.MESH


def tables(bands, groups):
    f = np.tile(np.arange(FREQS, dtype=np.int64) + 1, ANG_BAND)
    b = np.repeat(np.arange(ANG_BAND, dtype=np.int64) * 33 // ANG_BAND - 16, FREQS)
    a = np.arange(bands, dtype=np.int64) - bands // 2

    def both(turns, period):
        angle = (turns % period) * (2.0 * math.pi / period)
        return np.cos(angle).astype(np.float32), np.sin(angle).astype(np.float32)

    y = np.arange(CY, dtype=np.int64)[:, None]
    proj = np.concatenate(both(f * b * y, 4096), axis=1)
    time = np.stack(both(f * np.arange(STEPS, dtype=np.int64)[:, None], 128))
    y_start = np.stack(both(f * b * CY * np.arange(groups, dtype=np.int64)[:, None], 4096))
    cell = np.stack(both(f * a[:, None], 4096))
    block = np.stack(both(f * a[:, None] * CX, 4096))
    flat = [proj[:, :CY], proj[:, CY:]] + [part for table in (time, y_start, cell, block) for part in table]
    starts = np.cumsum([0] + [-(-part.shape[0] // 8) * 8 for part in flat])
    packed = np.zeros((starts[-1], CY), np.float32)
    for start, part in zip(starts, flat):
        packed[start : start + part.shape[0]] = part
    return packed, tuple(int(start) for start in starts[:-1])


class Rows:
    def __init__(self, ref, starts):
        self.ref, self.starts = ref, starts

    def at(self, part, first, count):
        return self.ref[pl.ds(self.starts[part] + first, count), :]


def kernel(
    ny, nx, scale, starts,
    e_hbm, h_hbm, ids_hbm, ca_hbm, cb_hbm, face_hbm, bands_hbm, table_hbm,
    e_out, h_out, far_out,
    ef, hf, ids, ca, cb, face, bands, table, in_sem,
    coef_a, coef_b, se, sh, strip_a, strip_b,
    edge_r, edge_l, from_l, from_r,
    sample, acc, cols, phase, f_send, f_recv,
    send_sem, recv_sem, f_send_sem, f_recv_sem, out_sem,
):
    iy = lax.axis_index("grp")
    ix = lax.axis_index("inner")
    total = ny * nx
    me = iy * nx + ix
    f32 = jnp.float32
    lane = lax.broadcasted_iota(jnp.int32, (8, CY), 1)
    row = lax.broadcasted_iota(jnp.int32, (8, CY), 0)
    own_rows = pl.ds(PAD + HALO, CX)

    loads = [
        pltpu.make_async_copy(src, dst, in_sem.at[i])
        for i, (src, dst) in enumerate(
            (
                (e_hbm, ef.at[:, :, own_rows]),
                (h_hbm, hf.at[:, :, own_rows]),
                (ids_hbm, ids.at[:, pl.ds(HALO, CX)]),
                (ca_hbm, ca),
                (cb_hbm, cb),
                (face_hbm, face),
                (bands_hbm, bands),
                (table_hbm, table),
            )
        )
    ]
    for load in loads:
        load.start()
    time, y_start, cell, block = (Rows(table, starts[i : i + 2]) for i in (2, 4, 6, 8))

    barrier = pltpu.get_barrier_semaphore()

    def greet(k, carry):
        other = lax.rem(me + k, total)
        pl.semaphore_signal(
            barrier, inc=1, device_id=(lax.div(other, nx), lax.rem(other, nx)), device_id_type=MESH
        )
        return carry

    lax.fori_loop(1, total, greet, 0)

    has_xr, has_xl = ix < nx - 1, ix > 0
    has_yr, has_yl = iy < ny - 1, iy > 0
    low, high = pl.ds(0, 8), pl.ds(8, 8)
    every = (
        (has_yr, has_yl, edge_r, from_l.at[:, pl.ds(HALO, CX)], (iy + 1, ix)),
        (has_yr & has_xr, has_yl & has_xl, edge_r.at[:, high], from_l.at[:, low], (iy + 1, ix + 1)),
        (has_yr & has_xl, has_yl & has_xr, edge_r.at[:, low], from_l.at[:, pl.ds(24, 8)], (iy + 1, ix - 1)),
        (has_yl, has_yr, edge_l, from_r.at[:, pl.ds(HALO, CX)], (iy - 1, ix)),
        (has_yl & has_xr, has_yr & has_xl, edge_l.at[:, high], from_r.at[:, low], (iy - 1, ix + 1)),
        (has_yl & has_xl, has_yr & has_xr, edge_l.at[:, low], from_r.at[:, pl.ds(24, 8)], (iy - 1, ix - 1)),
        (has_xr, has_xl, e_hbm.at[:, :, high], ef.at[:, :, pl.ds(PAD, 8)], (iy, ix + 1)),
        (has_xl, has_xr, e_hbm.at[:, :, low], ef.at[:, :, pl.ds(PAD + 24, 8)], (iy, ix - 1)),
        (has_xr, has_xl, h_hbm.at[:, :, high], hf.at[:, :, pl.ds(PAD, 8)], (iy, ix + 1)),
        (has_xl, has_xr, h_hbm.at[:, :, low], hf.at[:, :, pl.ds(PAD + 24, 8)], (iy, ix - 1)),
        (has_xr, has_xl, ids_hbm.at[:, high], ids.at[:, low], (iy, ix + 1)),
        (has_xl, has_xr, ids_hbm.at[:, low], ids.at[:, pl.ds(24, 8)], (iy, ix - 1)),
    )

    def remote(i, src, dst, device):
        return pltpu.make_async_remote_copy(
            src_ref=src,
            dst_ref=dst,
            send_sem=send_sem.at[i],
            recv_sem=recv_sem.at[i],
            device_id=device,
            device_id_type=MESH,
        )

    def start_copies(which):
        for i in which:
            sends, _, src, dst, device = every[i]

            @pl.when(sends)
            def _(i=i, src=src, dst=dst, device=device):
                remote(i, src, dst, device).start()

    def await_copies(which):
        for i in which:
            _, receives, src, dst, _ = every[i]

            @pl.when(receives)
            def _(i=i, src=src, dst=dst):
                remote(i, src, dst, (iy, ix)).wait_recv()

    y_copies, x_copies = range(6), range(6, 12)

    for missing, rows in (
        (jnp.logical_not(has_xl), 0),
        (jnp.logical_not(has_xr), 24),
    ):
        @pl.when(missing)
        def _(rows=rows):
            def fill(z, carry):
                for c in range(3):
                    ef[c, z, pl.ds(PAD + rows, 8), :] = jnp.zeros((8, CY), f32)
                    hf[c, z, pl.ds(PAD + rows, 8), :] = jnp.zeros((8, CY), f32)
                ids[z, pl.ds(rows, 8), :] = jnp.full((8, CY), NMAT, jnp.int32)
                return carry

            lax.fori_loop(0, NZ, fill, 0)

    for edge, side in ((from_l, has_yl), (from_r, has_yr)):
        for given, rows, count in ((side, 8, 16), (side & has_xl, 0, 8), (side & has_xr, 24, 8)):
            @pl.when(jnp.logical_not(given))
            def _(edge=edge, rows=rows, count=count):
                edge[pl.ds(0, 6), pl.ds(rows, count), :] = jnp.zeros((6, count, CY), f32)
                edge[6, pl.ds(rows, count), :] = jnp.full((count, CY), float(NMAT), f32)

    def clear(z, carry):
        for c in range(3):
            for rows in (0, PAD + ROWS):
                ef[c, z, pl.ds(rows, PAD), :] = jnp.zeros((PAD, CY), f32)
                hf[c, z, pl.ds(rows, PAD), :] = jnp.zeros((PAD, CY), f32)
        return carry

    lax.fori_loop(0, NZ, clear, 0)
    for field in (se, sh):
        for c in range(3):
            for j in range(HALF):
                for rows in (0, PAD + ROWS):
                    field[c, j, pl.ds(rows, PAD), :] = jnp.zeros((PAD, CY), f32)
    sample[...] = jnp.zeros(sample.shape, f32)
    acc[...] = jnp.zeros(acc.shape, f32)

    pl.semaphore_wait(barrier, total - 1)
    start_copies(x_copies)
    for load in loads:
        load.wait()

    for i in range(7):
        for g in range(2):
            right = jnp.zeros((8, CY), f32)
            left = jnp.zeros((8, CY), f32)
            for z in range(NZ):
                rows = pl.ds(8 * g + PAD + HALO, 8)
                if i < 6:
                    value = (ef, hf)[i // 3][i % 3, z, rows, :]
                else:
                    value = ids[z, pl.ds(8 * g + HALO, 8), :].astype(f32)
                here = (lane >= 8 * z) & (lane < 8 * z + 8)
                right = jnp.where(here, pltpu.roll(value, (8 * z - 120) % CY, 1) if z < 15 else value, right)
                left = jnp.where(here, pltpu.roll(value, 8 * z, 1) if z else value, left)
            edge_r[i, pl.ds(8 * g, 8), :] = right
            edge_l[i, pl.ds(8 * g, 8), :] = left
    start_copies(y_copies)

    def lookup(here):
        va = jnp.zeros((8, CY), f32)
        vb = jnp.zeros((8, CY), f32)
        for m in range(NMAT):
            chosen = here == m
            va = jnp.where(chosen, ca[m], va)
            vb = jnp.where(chosen, cb[m], vb)
        return va, vb

    def coefficients(groups):
        def one(z, carry):
            for g in groups:
                va, vb = lookup(ids[z, pl.ds(8 * g, 8), :])
                coef_a[z, pl.ds(8 * g, 8), :] = va
                coef_b[z, pl.ds(8 * g, 8), :] = vb
            return carry

        lax.fori_loop(0, NZ, one, 0)

    in_half = lax.rem(lane, CY // 2)

    def strips(groups):
        spots = (
            (0, 8, (lane >= 8) & (lane < 24)),
            (0, 48, (lane >= 32) & (lane < 48)),
            (1, 72, (lane >= 72) & (lane < 88)),
            (1, 112, (lane >= 96) & (lane < 112)),
        )

        def pack(j, values, i, rows, base):
            out = jnp.full((8, CY), base, f32)
            for half, shift, mask in spots:
                out = jnp.where(mask, pltpu.roll(values[half], shift, 1), out)
            before, after = from_l[i, rows, :], from_r[i, rows, :]
            out = jnp.where(in_half < 8, pltpu.roll(before, (CY - 8 * j) % CY, 1) if j else before, out)
            return jnp.where((in_half >= 48) & (in_half < 56), pltpu.roll(after, (CY + 48 - 8 * j) % CY, 1), out)

        for g in groups:
            rows = pl.ds(8 * g, 8)
            padded = pl.ds(PAD + 8 * g, 8)
            for j in range(HALF):
                for i in range(6):
                    source, target = ((ef, se), (hf, sh))[i // 3]
                    values = [source[i % 3, j + HALF * half, padded, :] for half in range(2)]
                    target[i % 3, j, padded, :] = pack(j, values, i, rows, 0.0)
                values = [ids[j + HALF * half, rows, :].astype(f32) for half in range(2)]
                va, vb = lookup(pack(j, values, 6, rows, float(NMAT)))
                strip_a[j, rows, :] = va
                strip_b[j, rows, :] = vb

    def power(bit, carry):
        pr, pi, br, bi = carry
        take = lax.rem(lax.shift_right_logical(ix, bit), 2) == 1
        nr = pr * br - pi * bi
        ni = pr * bi + pi * br
        return (
            jnp.where(take, nr, pr),
            jnp.where(take, ni, pi),
            br * br - bi * bi,
            2.0 * br * bi,
        )

    coefficients(OWN)
    rows_at_once = 8
    for start in range(0, total, rows_at_once):
        part = pl.ds(start, rows_at_once)
        carry = (
            jnp.full((rows_at_once, CY), scale, jnp.float32),
            jnp.zeros((rows_at_once, CY), jnp.float32),
            block.at(0, start, rows_at_once),
            block.at(1, start, rows_at_once),
        )
        for bit in range(max(1, (nx - 1).bit_length())):
            carry = power(bit, carry)
        phase[part, :] = carry[0]
        phase[pl.ds(total + start, rows_at_once), :] = carry[1]
    start_phase = Rows(phase, (0, total))

    await_copies(y_copies)
    strips(OWN)
    await_copies(x_copies)
    strips((0, 3))
    coefficients((0, 3))

    half_x = jnp.where(ix > 0, 0.5, 0.0).astype(f32)
    half_y = jnp.where((in_half < 8) & (iy == 0), 0.0, 0.5).astype(f32)
    on_face = [
        (row + 8 * g >= face[0]) & (row + 8 * g < face[1]) & (lane >= face[2]) & (lane < face[3])
        for g in range(2)
    ]

    def add_sample(n):
        g_re, g_im = (
            jnp.dot(
                sample[...],
                table[pl.ds(starts[part], CY), :],
                precision=lax.Precision.HIGHEST,
                preferred_element_type=jnp.float32,
            )
            for part in range(2)
        )
        ct, st = time.at(0, n, 1), time.at(1, n, 1)
        acc[0] += ct * g_re + st * g_im
        acc[1] += ct * g_im - st * g_re

    def at(g, shift=0):
        return pl.ds(PAD + 8 * g + shift, 8)

    every_group = range(GROUPS)

    def new_magnetic(e, h, z, here, above, factor):
        out = []
        for g in every_group:
            ex, ey, ez = here[g]
            ex_z, ey_z = above[g]
            ey_x, ez_x = e[1, z, at(g, 1), :], e[2, z, at(g, 1), :]
            ex_y, ez_y = pltpu.roll(ex, CY - 1, 1), pltpu.roll(ez, CY - 1, 1)
            hx = h[0, z, at(g), :] - factor[g] * ((ez_y - ez) - (ey_z - ey))
            hy = h[1, z, at(g), :] - factor[g] * ((ex_z - ex) - (ez_x - ez))
            hz = h[2, z, at(g), :] - factor[g] * ((ey_x - ey) - (ex_y - ex))
            h[0, z, at(g), :] = hx
            h[1, z, at(g), :] = hy
            h[2, z, at(g), :] = hz
            out.append((hx, hy, hz))
        return out

    def new_electric(e, h, a, b, z, here, now, below):
        out = []
        for g in every_group:
            ex, ey, ez = here[g]
            hx, hy, hz = now[g]
            hx_z, hy_z = below[g]
            hy_x, hz_x = h[1, z, at(g, -1), :], h[2, z, at(g, -1), :]
            hx_y, hz_y = pltpu.roll(hx, 1, 1), pltpu.roll(hz, 1, 1)
            va, vb = a[z, pl.ds(8 * g, 8), :], b[z, pl.ds(8 * g, 8), :]
            ex = va * ex + vb * ((hz - hz_y) - (hy - hy_z))
            ey = va * ey + vb * ((hx - hx_z) - (hz - hz_x))
            ez = va * ez + vb * ((hy - hy_x) - (hx - hx_y))
            e[0, z, at(g), :] = ex
            e[1, z, at(g), :] = ey
            e[2, z, at(g), :] = ez
            out.append((ex, ey))
        return out

    def plane(e, z):
        return [tuple(e[c, z, at(g), :] for c in range(3)) for g in every_group]

    zero = jnp.zeros((8, CY), f32)
    low_half = lane < CY // 2

    def step(n, carry):
        add_sample(jnp.maximum(n - 1, 0))

        factor = [half_y * (half_x * 2.0)] + [half_y] * 3
        here = first = plane(se, 0)
        below = None
        for j in range(HALF):
            if j < HALF - 1:
                ahead = plane(se, j + 1)
                above = [v[:2] for v in ahead]
            else:
                ahead = None
                above = [
                    tuple(jnp.where(low_half, pltpu.roll(v, CY // 2, 1), 0.0) for v in group[:2]) for group in first
                ]
            now = new_magnetic(se, sh, j, here, above, factor)
            if j:
                new_electric(se, sh, strip_a, strip_b, j, here, now, below)
            else:
                start = now
            below = [v[:2] for v in now]
            here = ahead
        below = [tuple(jnp.where(low_half, 0.0, pltpu.roll(v, CY // 2, 1)) for v in group) for group in below]
        ends = new_electric(se, sh, strip_a, strip_b, 0, plane(se, 0), start, below)
        ends = [ends[g] + start[g][:2] for g in OWN]

        factor = [jnp.full((8, CY), half_x, f32)] + [0.5] * 3
        here = plane(ef, 0)
        below = [(zero, zero)] * GROUPS
        for z in range(NZ):
            if z < NZ - 1:
                ahead = plane(ef, z + 1)
                above = [v[:2] for v in ahead]
            else:
                ahead, above = None, [(zero, zero)] * GROUPS
            now = new_magnetic(ef, hf, z, here, above, factor)
            values = new_electric(ef, hf, coef_a, coef_b, z, here, now, below)
            below = [v[:2] for v in now]
            here = ahead
            if z == ZF:
                for k, g in enumerate(OWN):
                    for c, value in enumerate(values[g] + below[g]):
                        end = ends[k][c]
                        value = jnp.where(lane < 8, pltpu.roll(end, 56, 1), value)
                        value = jnp.where(lane >= CY - 8, pltpu.roll(end, 16, 1), value)
                        sample[pl.ds(c * CX + 8 * k, 8), :] = jnp.where(on_face[k], value, 0.0)
        return carry

    lax.fori_loop(0, STEPS, step, 0)

    add_sample(STEPS - 1)
    outs = []
    for f, (field, strip, out) in enumerate(((ef, se, e_out), (hf, sh, h_out))):
        for c in range(3):
            for z in range(NZ):
                half, j = z // HALF, z % HALF
                for g in OWN:
                    end = strip[c, j, at(g), :]
                    value = field[c, z, at(g), :]
                    value = jnp.where(lane < 8, pltpu.roll(end, (CY - 64 * half - 8) % CY, 1), value)
                    value = jnp.where(lane >= CY - 8, pltpu.roll(end, 80 - 64 * half, 1), value)
                    field[c, z, at(g), :] = value
        copy = pltpu.make_async_copy(field.at[:, :, own_rows], out, out_sem.at[f])
        copy.start()
        outs.append(copy)

    yr, yi = y_start.at(0, iy, 1), y_start.at(1, iy, 1)
    col_re = acc[0] * yr - acc[1] * yi
    acc[1] = acc[0] * yi + acc[1] * yr
    acc[0] = col_re
    for part in range(2):
        for x in range(CX):
            four = acc[part, pl.ds(x, 4, stride=CX), :]
            cols[part, x, pl.ds(0, 4), :] = four
            cols[part, x, pl.ds(4, 4), :] = four

    upper = lax.broadcasted_iota(jnp.int32, (8, CY), 0) < 4
    at_once = min(8, total)

    def send_far(k):
        other = lax.rem(me + k, total)
        return pltpu.make_async_remote_copy(
            src_ref=f_send.at[k],
            dst_ref=f_recv.at[k - 1],
            send_sem=f_send_sem,
            recv_sem=f_recv_sem,
            device_id=(lax.div(other, nx), lax.rem(other, nx)),
            device_id_type=MESH,
        )

    def project(trip, carry):
        k0 = trip * at_once
        picked = [bands[lax.rem(me + k0 + j, total)] for j in range(at_once)]

        def pair(rows, part, j):
            return jnp.where(upper, rows.at(part, picked[j], 1), rows.at(part, picked[j + 1], 1))

        pairs = range(0, at_once, 2)
        wr = [pair(cell, 0, j) for j in pairs]
        wi = [pair(cell, 1, j) for j in pairs]
        c_re, c_im = cols[0, CX - 1], cols[1, CX - 1]
        re = [c_re for _ in pairs]
        im = [c_im for _ in pairs]
        for x in range(CX - 2, -1, -1):
            c_re, c_im = cols[0, x], cols[1, x]
            re, im = (
                [r * a - i * b + c_re for r, i, a, b in zip(re, im, wr, wi)],
                [r * b + i * a + c_im for r, i, a, b in zip(re, im, wr, wi)],
            )
        for t, j in enumerate(pairs):
            pr, pi = pair(start_phase, 0, j), pair(start_phase, 1, j)
            far_re = re[t] * pr - im[t] * pi
            far_im = re[t] * pi + im[t] * pr
            f_send[k0 + j] = jnp.where(upper, far_re, pltpu.roll(far_im, 4, 0))
            f_send[k0 + j + 1] = jnp.where(upper, pltpu.roll(far_re, 4, 0), far_im)
        for j in range(at_once):
            @pl.when(k0 + j > 0)
            def _(j=j):
                send_far(k0 + j).start()
        return carry

    lax.fori_loop(0, total // at_once, project, 0)

    pltpu.make_async_copy(f_recv, f_recv, f_recv_sem).wait()
    if total <= 64:
        terms = [f_send[0]] + [f_recv[k] for k in range(total - 1)]
        while len(terms) > 1:
            terms = [a + b for a, b in zip(terms[::2], terms[1::2])]
        far_out[...] = terms[0]
    else:
        far_out[...] = lax.fori_loop(0, total - 1, lambda k, t: t + f_recv[k], f_send[0])
    pltpu.make_async_copy(f_recv, f_recv, f_send_sem).wait()
    for i, (sends, _, src, dst, device) in enumerate(every):
        @pl.when(sends)
        def _(i=i, src=src, dst=dst, device=device):
            remote(i, src, dst, device).wait_send()
    for copy in outs:
        copy.wait()


def local(ny, nx, electric, magnetic, material_ids, update_ca, update_cb, face_ranges, band_table):
    total = ny * nx
    bands = band_table.shape[0]
    assert bands == total and electric.shape == (3, NZ, CX, CY)
    scale = 1.0 / math.sqrt(CX * nx * CY * ny)
    f32 = jnp.float32
    vmem = pl.BlockSpec(memory_space=pltpu.VMEM)
    hbm = pl.BlockSpec(memory_space=pltpu.HBM)
    packed, starts = tables(bands, ny)
    e_out, h_out, far = pl.pallas_call(
        functools.partial(kernel, ny, nx, scale, starts),
        out_shape=(
            jax.ShapeDtypeStruct(electric.shape, f32),
            jax.ShapeDtypeStruct(electric.shape, f32),
            jax.ShapeDtypeStruct((8, CY), f32),
        ),
        in_specs=[hbm] * 8,
        out_specs=(hbm, hbm, vmem),
        scratch_shapes=[
            pltpu.VMEM((3, NZ, PITCH, CY), f32),
            pltpu.VMEM((3, NZ, PITCH, CY), f32),
            pltpu.VMEM((NZ, ROWS, CY), jnp.int32),
            pltpu.SMEM((NMAT,), f32),
            pltpu.SMEM((NMAT,), f32),
            pltpu.SMEM((4,), jnp.int32),
            pltpu.SMEM((bands,), jnp.int32),
            pltpu.VMEM(packed.shape, f32),
            pltpu.SemaphoreType.DMA((8,)),
            pltpu.VMEM((NZ, ROWS, CY), f32),
            pltpu.VMEM((NZ, ROWS, CY), f32),
            pltpu.VMEM((3, HALF, PITCH, CY), f32),
            pltpu.VMEM((3, HALF, PITCH, CY), f32),
            pltpu.VMEM((HALF, ROWS, CY), f32),
            pltpu.VMEM((HALF, ROWS, CY), f32),
            pltpu.VMEM((7, CX, CY), f32),
            pltpu.VMEM((7, CX, CY), f32),
            pltpu.VMEM((7, ROWS, CY), f32),
            pltpu.VMEM((7, ROWS, CY), f32),
            pltpu.VMEM((4 * CX, CY), f32),
            pltpu.VMEM((2, 4 * CX, CY), f32),
            pltpu.VMEM((2, CX, 8, CY), f32),
            pltpu.VMEM((2 * total, CY), f32),
            pltpu.VMEM((total, 8, CY), f32),
            pltpu.VMEM((total - 1, 8, CY), f32),
            pltpu.SemaphoreType.DMA((12,)),
            pltpu.SemaphoreType.DMA((12,)),
            pltpu.SemaphoreType.DMA,
            pltpu.SemaphoreType.DMA,
            pltpu.SemaphoreType.DMA((2,)),
        ],
        compiler_params=pltpu.CompilerParams(
            collective_id=0, has_side_effects=True, vmem_limit_bytes=62 * 1024 * 1024
        ),
        name="fdtd",
    )(
        electric,
        magnetic,
        material_ids,
        update_ca,
        update_cb,
        face_ranges.reshape(4),
        band_table,
        packed,
    )
    return e_out, h_out, far.reshape(1, 8, CY)


def solution(mesh):
    in_specs = (
        P(None, None, "inner", "grp"),
        P(None, None, "inner", "grp"),
        P(None, "inner", "grp"),
        P(),
        P(),
        P("inner", "grp", None),
        P(),
    )
    out_specs = (
        P(None, None, "inner", "grp"),
        P(None, None, "inner", "grp"),
        P(("grp", "inner"), None, None),
    )
    body = functools.partial(local, mesh.shape["grp"], mesh.shape["inner"])
    return jax.shard_map(body, mesh=mesh, in_specs=in_specs, out_specs=out_specs, check_vma=False)
```

```python
import functools
import math

import jax
import jax.numpy as jnp
import numpy as np
from jax import lax
from jax.experimental import pallas as pl
from jax.experimental.pallas import tpu as pltpu
from jax.sharding import PartitionSpec as P

STEPS = 8
FREQS = 32
ANG_BAND = 4
NMAT = 8
ZF = 8
NZ = 16
CX = 16
CY = 128
PAD = 8
HALO = 8
ROWS = CX + 2 * HALO
GHOST = 4
PITCH = CX + 2 * PAD
WIDE = CX + 2 * GHOST + 2 * PAD
OWN = (1, 2)
HALF = NZ // 2
MESH = pl.DeviceIdType.MESH


def tables(bands, groups):
    f = np.tile(np.arange(FREQS, dtype=np.int64) + 1, ANG_BAND)
    b = np.repeat(np.arange(ANG_BAND, dtype=np.int64) * 33 // ANG_BAND - 16, FREQS)
    a = np.arange(bands, dtype=np.int64) - bands // 2

    def both(turns, period):
        angle = (turns % period) * (2.0 * math.pi / period)
        return np.cos(angle).astype(np.float32), np.sin(angle).astype(np.float32)

    y = np.arange(CY, dtype=np.int64)[:, None]
    proj = np.concatenate(both(f * b * y, 4096), axis=1)
    time = np.stack(both(f * np.arange(STEPS, dtype=np.int64)[:, None], 128))
    y_start = np.stack(both(f * b * CY * np.arange(groups, dtype=np.int64)[:, None], 4096))
    cell = np.stack(both(f * a[:, None], 4096))
    block = np.stack(both(f * a[:, None] * CX, 4096))
    flat = [proj[:, :CY], proj[:, CY:]] + [part for table in (time, y_start, cell, block) for part in table]
    starts = np.cumsum([0] + [-(-part.shape[0] // 8) * 8 for part in flat])
    packed = np.zeros((starts[-1], CY), np.float32)
    for start, part in zip(starts, flat):
        packed[start : start + part.shape[0]] = part
    return packed, tuple(int(start) for start in starts[:-1])


class Rows:
    def __init__(self, ref, starts):
        self.ref, self.starts = ref, starts

    def at(self, part, first, count):
        return self.ref[pl.ds(self.starts[part] + first, count), :]


def kernel(
    ny, nx, scale, starts,
    e_hbm, h_hbm, ids_hbm, ca_hbm, cb_hbm, face_hbm, bands_hbm, table_hbm,
    e_out, h_out, far_out,
    ef, hf, ids, ca, cb, face, bands, table, e_in, h_in, in_sem,
    coef_a, coef_b, se, sh, strip_a, strip_b, ce, ch, de, dh,
    edge_r, edge_l, from_l, from_r,
    own_h, own_e, left_h, right_e, strip_own_h, strip_own_e, strip_left_h, strip_right_e,
    samples, strip_samples, sample, acc, cols, phase, f_send, f_recv,
    send_sem, recv_sem, trace_send, trace_recv, f_send_sem, f_recv_sem, out_sem,
):
    iy = lax.axis_index("grp")
    ix = lax.axis_index("inner")
    total = ny * nx
    me = iy * nx + ix
    f32 = jnp.float32
    lane = lax.broadcasted_iota(jnp.int32, (8, CY), 1)
    row = lax.broadcasted_iota(jnp.int32, (8, CY), 0)
    own_rows = pl.ds(PAD, CX)

    loads = [
        pltpu.make_async_copy(src, dst, in_sem.at[i])
        for i, (src, dst) in enumerate(
            (
                (e_hbm, ef.at[:, :, own_rows]),
                (h_hbm, hf.at[:, :, own_rows]),
                (ids_hbm, ids.at[:, pl.ds(HALO, CX)]),
                (ca_hbm, ca),
                (cb_hbm, cb),
                (face_hbm, face),
                (bands_hbm, bands),
                (table_hbm, table),
                (e_hbm, e_in),
                (h_hbm, h_in),
            )
        )
    ]
    for load in loads:
        load.start()
    time, y_start, cell, block = (Rows(table, starts[i : i + 2]) for i in (2, 4, 6, 8))

    barrier = pltpu.get_barrier_semaphore()

    def greet(k, carry):
        other = lax.rem(me + k, total)
        pl.semaphore_signal(
            barrier, inc=1, device_id=(lax.div(other, nx), lax.rem(other, nx)), device_id_type=MESH
        )
        return carry

    lax.fori_loop(1, total, greet, 0)

    has_xr, has_xl = ix < nx - 1, ix > 0
    has_yr, has_yl = iy < ny - 1, iy > 0
    low, high = pl.ds(0, 8), pl.ds(8, 8)
    every = (
        (has_yr, has_yl, edge_r, from_l.at[:, pl.ds(HALO, CX)], (iy + 1, ix)),
        (has_yl, has_yr, edge_l, from_r.at[:, pl.ds(HALO, CX)], (iy - 1, ix)),
        (has_yr & has_xr, has_yl & has_xl, edge_r.at[6, high], from_l.at[6, low], (iy + 1, ix + 1)),
        (has_yr & has_xl, has_yl & has_xr, edge_r.at[6, low], from_l.at[6, pl.ds(24, 8)], (iy + 1, ix - 1)),
        (has_yl & has_xr, has_yr & has_xl, edge_l.at[6, high], from_r.at[6, low], (iy - 1, ix + 1)),
        (has_yl & has_xl, has_yr & has_xr, edge_l.at[6, low], from_r.at[6, pl.ds(24, 8)], (iy - 1, ix - 1)),
        (has_xr, has_xl, ids_hbm.at[:, high], ids.at[:, low], (iy, ix + 1)),
        (has_xl, has_xr, ids_hbm.at[:, low], ids.at[:, pl.ds(24, 8)], (iy, ix - 1)),
    )
    traces = (
        (has_xr, has_xl, own_h, left_h, (iy, ix + 1)),
        (has_xl, has_xr, own_e, right_e, (iy, ix - 1)),
        (has_xr, has_xl, strip_own_h, strip_left_h, (iy, ix + 1)),
        (has_xl, has_xr, strip_own_e, strip_right_e, (iy, ix - 1)),
    )

    def trace(n, k):
        _, _, src, dst, device = traces[k]
        return pltpu.make_async_remote_copy(
            src_ref=src.at[n],
            dst_ref=dst.at[n],
            send_sem=trace_send.at[n, k],
            recv_sem=trace_recv.at[n, k],
            device_id=device,
            device_id_type=MESH,
        )

    def send_trace(n, k):
        @pl.when(traces[k][0])
        def _():
            trace(n, k).start()

    def await_trace(n, k):
        @pl.when(traces[k][1])
        def _():
            trace(n, k).wait_recv()

    def remote(i, src, dst, device):
        return pltpu.make_async_remote_copy(
            src_ref=src,
            dst_ref=dst,
            send_sem=send_sem.at[i],
            recv_sem=recv_sem.at[i],
            device_id=device,
            device_id_type=MESH,
        )

    def start_copies(which):
        for i in which:
            sends, _, src, dst, device = every[i]

            @pl.when(sends)
            def _(i=i, src=src, dst=dst, device=device):
                remote(i, src, dst, device).start()

    def await_copies(which):
        for i in which:
            _, receives, src, dst, _ = every[i]

            @pl.when(receives)
            def _(i=i, src=src, dst=dst):
                remote(i, src, dst, (iy, ix)).wait_recv()

    y_copies, x_copies = range(6), range(6, 8)

    for given, rows, arrived in ((has_xl, 0, (left_h, strip_left_h)), (has_xr, 24, (right_e, strip_right_e))):
        @pl.when(jnp.logical_not(given))
        def _(rows=rows, arrived=arrived):
            for buf in arrived:
                buf[...] = jnp.zeros(buf.shape, f32)
            ids[:, pl.ds(rows, 8), :] = jnp.full((NZ, 8, CY), NMAT, jnp.int32)

    for edge, side in ((from_l, has_yl), (from_r, has_yr)):
        @pl.when(jnp.logical_not(side))
        def _(edge=edge):
            edge[pl.ds(0, 6), pl.ds(HALO, CX), :] = jnp.zeros((6, CX, CY), f32)

        for given, rows, count in ((side, 8, 16), (side & has_xl, 0, 8), (side & has_xr, 24, 8)):
            @pl.when(jnp.logical_not(given))
            def _(edge=edge, rows=rows, count=count):
                edge[6, pl.ds(rows, count), :] = jnp.full((count, CY), float(NMAT), f32)

    for fields in ((ef, hf), (se, sh)):
        for field in fields:
            for c in range(3):
                for z in range(field.shape[1]):
                    for rows in (0, PAD + CX):
                        field[c, z, pl.ds(rows, PAD), :] = jnp.zeros((PAD, CY), f32)
    for field in (ce, ch, de, dh):
        field[...] = jnp.zeros(field.shape, f32)
    sample[...] = jnp.zeros(sample.shape, f32)
    acc[...] = jnp.zeros(acc.shape, f32)

    pl.semaphore_wait(barrier, total - 1)
    start_copies(x_copies)
    for load in loads:
        load.wait()

    for i in range(7):
        for g in range(2):
            right = jnp.zeros((8, CY), f32)
            left = jnp.zeros((8, CY), f32)
            for z in range(NZ):
                rows = pl.ds(8 * g + PAD, 8)
                if i < 6:
                    value = (ef, hf)[i // 3][i % 3, z, rows, :]
                else:
                    value = ids[z, pl.ds(8 * g + HALO, 8), :].astype(f32)
                here = (lane >= 8 * z) & (lane < 8 * z + 8)
                right = jnp.where(here, pltpu.roll(value, (8 * z - 120) % CY, 1) if z < 15 else value, right)
                left = jnp.where(here, pltpu.roll(value, 8 * z, 1) if z else value, left)
            edge_r[i, pl.ds(8 * g, 8), :] = right
            edge_l[i, pl.ds(8 * g, 8), :] = left
    start_copies(y_copies)

    def lookup(here):
        va = jnp.zeros((8, CY), f32)
        vb = jnp.zeros((8, CY), f32)
        for m in range(NMAT):
            chosen = here == m
            va = jnp.where(chosen, ca[m], va)
            vb = jnp.where(chosen, cb[m], vb)
        return va, vb

    def coefficients(groups):
        def one(z, carry):
            for g in groups:
                va, vb = lookup(ids[z, pl.ds(8 * g, 8), :])
                coef_a[z, pl.ds(8 * g, 8), :] = va
                coef_b[z, pl.ds(8 * g, 8), :] = vb
            return carry

        lax.fori_loop(0, NZ, one, 0)

    in_half = lax.rem(lane, CY // 2)

    def strips(groups):
        spots = (
            (0, 8, (lane >= 8) & (lane < 24)),
            (0, 48, (lane >= 32) & (lane < 48)),
            (1, 72, (lane >= 72) & (lane < 88)),
            (1, 112, (lane >= 96) & (lane < 112)),
        )

        def pack(j, values, i, rows, base):
            out = jnp.full((8, CY), base, f32)
            for half, shift, mask in spots:
                out = jnp.where(mask, pltpu.roll(values[half], shift, 1), out)
            before, after = from_l[i, rows, :], from_r[i, rows, :]
            out = jnp.where(in_half < 8, pltpu.roll(before, (CY - 8 * j) % CY, 1) if j else before, out)
            return jnp.where((in_half >= 48) & (in_half < 56), pltpu.roll(after, (CY + 48 - 8 * j) % CY, 1), out)

        for g in groups:
            rows = pl.ds(8 * g, 8)
            padded = pl.ds(PAD + 8 * g - HALO, 8)
            for j in range(HALF):
                for i in range(6 if g in OWN else 0):
                    source, target = ((e_in, se), (h_in, sh))[i // 3]
                    values = [source[i % 3, j + HALF * half, pl.ds(8 * g - HALO, 8), :] for half in range(2)]
                    target[i % 3, j, padded, :] = pack(j, values, i, rows, 0.0)
                values = [ids[j + HALF * half, rows, :].astype(f32) for half in range(2)]
                va, vb = lookup(pack(j, values, 6, rows, float(NMAT)))
                strip_a[j, rows, :] = va
                strip_b[j, rows, :] = vb

    def power(bit, carry):
        pr, pi, br, bi = carry
        take = lax.rem(lax.shift_right_logical(ix, bit), 2) == 1
        nr = pr * br - pi * bi
        ni = pr * bi + pi * br
        return (
            jnp.where(take, nr, pr),
            jnp.where(take, ni, pi),
            br * br - bi * bi,
            2.0 * br * bi,
        )

    coefficients(OWN)
    rows_at_once = 8
    for start in range(0, total, rows_at_once):
        part = pl.ds(start, rows_at_once)
        carry = (
            jnp.full((rows_at_once, CY), scale, jnp.float32),
            jnp.zeros((rows_at_once, CY), jnp.float32),
            block.at(0, start, rows_at_once),
            block.at(1, start, rows_at_once),
        )
        for bit in range(max(1, (nx - 1).bit_length())):
            carry = power(bit, carry)
        phase[part, :] = carry[0]
        phase[pl.ds(total + start, rows_at_once), :] = carry[1]
    start_phase = Rows(phase, (0, total))

    half_y = jnp.where((in_half < 8) & (iy == 0), 0.0, 0.5).astype(f32)
    on_face = [
        (row + 8 * g >= face[0]) & (row + 8 * g < face[1]) & (lane >= face[2]) & (lane < face[3])
        for g in range(2)
    ]

    def add_sample(n):
        g_re, g_im = (
            jnp.dot(
                sample[...],
                table[pl.ds(starts[part], CY), :],
                precision=lax.Precision.HIGHEST,
                preferred_element_type=jnp.float32,
            )
            for part in range(2)
        )
        ct, st = time.at(0, n, 1), time.at(1, n, 1)
        acc[0] += ct * g_re + st * g_im
        acc[1] += ct * g_im - st * g_re

    def at(g, shift=0):
        return pl.ds(PAD + 8 * g + shift, 8)

    zero = jnp.zeros((8, CY), f32)
    low_half = lane < CY // 2

    def new_magnetic(e, h, z, groups, here, above, factor, source):
        out = {}
        for g in groups:
            ex, ey, ez = here[g]
            ex_z, ey_z = above[g]
            ey_x, ez_x = e[1, z, at(g, 1), :], e[2, z, at(g, 1), :]
            if source is not None and g != 1:
                more_y, more_z = source(g, z)
                ey_x, ez_x = ey_x + more_y, ez_x + more_z
            ex_y, ez_y = pltpu.roll(ex, CY - 1, 1), pltpu.roll(ez, CY - 1, 1)
            hx = h[0, z, at(g), :] - factor * ((ez_y - ez) - (ey_z - ey))
            hy = h[1, z, at(g), :] - factor * ((ex_z - ex) - (ez_x - ez))
            hz = h[2, z, at(g), :] - factor * ((ey_x - ey) - (ex_y - ex))
            h[0, z, at(g), :] = hx
            h[1, z, at(g), :] = hy
            h[2, z, at(g), :] = hz
            out[g] = (hx, hy, hz)
        return out

    def new_electric(e, h, a, b, z, groups, base, here, now, below, source):
        out = {}
        for g in groups:
            ex, ey, ez = here[g]
            hx, hy, hz = now[g]
            hx_z, hy_z = below[g]
            hy_x, hz_x = h[1, z, at(g, -1), :], h[2, z, at(g, -1), :]
            if source is not None and g != 1:
                more_y, more_z = source(g, z)
                hy_x, hz_x = hy_x + more_y, hz_x + more_z
            hx_y, hz_y = pltpu.roll(hx, 1, 1), pltpu.roll(hz, 1, 1)
            va, vb = a[z, pl.ds(base + 8 * g, 8), :], b[z, pl.ds(base + 8 * g, 8), :]
            ex = va * ex + vb * ((hz - hz_y) - (hy - hy_z))
            ey = va * ey + vb * ((hx - hx_z) - (hz - hz_x))
            ez = va * ez + vb * ((hy - hy_x) - (hx - hx_y))
            e[0, z, at(g), :] = ex
            e[1, z, at(g), :] = ey
            e[2, z, at(g), :] = ez
            out[g] = (ex, ey)
        return out

    def plane(e, z, groups):
        return {g: tuple(e[c, z, at(g), :] for c in range(3)) for g in groups}

    def two(values):
        return {g: v[:2] for g, v in values.items()}

    def advance(e, h, groups, base, source_e=None, source_h=None):
        here = plane(e, 0, groups)
        nothing = {g: (zero, zero) for g in groups}
        below = nothing
        for z in range(NZ):
            ahead = plane(e, z + 1, groups) if z < NZ - 1 else None
            above = two(ahead) if ahead else nothing
            now = new_magnetic(e, h, z, groups, here, above, 0.5, source_e)
            new_electric(e, h, coef_a, coef_b, z, groups, base, here, now, below, source_h)
            below, here = two(now), ahead

    def advance_strips(e, h, groups, base, source_e=None, source_h=None):
        here = first = plane(e, 0, groups)
        for j in range(HALF):
            if j < HALF - 1:
                ahead = plane(e, j + 1, groups)
                above = two(ahead)
            else:
                ahead = None
                above = {
                    g: tuple(jnp.where(low_half, pltpu.roll(v, CY // 2, 1), 0.0) for v in first[g][:2]) for g in groups
                }
            now = new_magnetic(e, h, j, groups, here, above, half_y, source_e)
            if j:
                new_electric(e, h, strip_a, strip_b, j, groups, base, here, now, below, source_h)
            else:
                start = now
            below, here = two(now), ahead
        below = {g: tuple(jnp.where(low_half, 0.0, pltpu.roll(v, CY // 2, 1)) for v in below[g]) for g in groups}
        new_electric(e, h, strip_a, strip_b, 0, groups, base, plane(e, 0, groups), start, below, source_h)

    def borders(n, e, h, mine_e, mine_h, run, k):
        depth = e.shape[1]
        for c in (1, 2):
            mine_e[n, pl.ds((c - 1) * depth, depth), :] = e[c, :, PAD, :]
        send_trace(n, k + 1)
        run(e, h, (0, 1), HALO)
        for c in (1, 2):
            mine_h[n, pl.ds((c - 1) * depth, depth), :] = h[c, :, PAD + CX - 1, :]
        send_trace(n, k)

    def keep(n, e, h, z, kept, first_row, add):
        for c, (field, part) in enumerate(((e, 0), (e, 1), (h, 0), (h, 1))):
            for k in range(2):
                spot = pl.ds(c * CX + 8 * k, 8)
                value = field[part, z, pl.ds(first_row + 8 * k, 8), :]
                kept[n, spot, :] = kept[n, spot, :] + value if add else value

    def alone(n, carry):
        borders(n, ef, hf, own_e, own_h, advance, 0)
        keep(n, ef, hf, ZF, samples, PAD, False)
        return carry

    def alone_strips(n, carry):
        borders(n, se, sh, strip_own_e, strip_own_h, advance_strips, 2)
        keep(n, se, sh, 0, strip_samples, PAD, False)
        return carry

    def sources(n, left, right, spot, depth):
        masks = {0: (row == spot) & has_xl, 2: row == spot}

        def source(g, z):
            buf = left if g == 0 else right
            return tuple(
                jnp.where(masks[g], jnp.broadcast_to(buf[n, pl.ds(c * depth + z, 1), :], (8, CY)), 0.0) for c in range(2)
            )

        return source

    SHIFT = HALO - GHOST

    def correct(groups, n, carry):
        await_trace(n, 0)
        await_trace(n, 1)
        advance(
            ce, ch, groups, SHIFT,
            sources(n, own_e, right_e, GHOST - 1, NZ), sources(n, left_h, own_h, GHOST, NZ),
        )
        keep(n, ce, ch, ZF, samples, PAD + GHOST, True)
        return carry

    def correct_strips(groups, n, carry):
        add_sample(jnp.maximum(n - 1, 0))
        await_trace(n, 2)
        await_trace(n, 3)
        advance_strips(
            de, dh, groups, SHIFT,
            sources(n, strip_own_e, strip_right_e, GHOST - 1, HALF), sources(n, strip_left_h, strip_own_h, GHOST, HALF),
        )
        keep(n, de, dh, 0, strip_samples, PAD + GHOST, True)
        for c in range(4):
            for k in range(2):
                spot = pl.ds(c * CX + 8 * k, 8)
                end = strip_samples[n, spot, :]
                value = jnp.where(lane < 8, pltpu.roll(end, 56, 1), samples[n, spot, :])
                value = jnp.where(lane >= CY - 8, pltpu.roll(end, 16, 1), value)
                sample[spot, :] = jnp.where(on_face[k], value, 0.0)
        return carry

    lax.fori_loop(0, STEPS, alone, 0)
    await_copies(y_copies)
    strips(OWN)
    lax.fori_loop(0, STEPS, alone_strips, 0)
    await_copies(x_copies)
    strips((0, 3))
    coefficients((0, 3))
    lax.fori_loop(0, STEPS // 2, functools.partial(correct, (0, 2)), 0)
    lax.fori_loop(STEPS // 2, STEPS, functools.partial(correct, (0, 1, 2)), 0)
    lax.fori_loop(0, STEPS // 2, functools.partial(correct_strips, (0, 2)), 0)
    lax.fori_loop(STEPS // 2, STEPS, functools.partial(correct_strips, (0, 1, 2)), 0)

    add_sample(STEPS - 1)
    outs = []
    for f, (field, strip, more, strip_more, out) in enumerate(((ef, se, ce, de, e_out), (hf, sh, ch, dh, h_out))):
        for c in range(3):
            for z in range(NZ):
                half, j = z // HALF, z % HALF
                for g in range(2):
                    end = strip[c, j, at(g), :] + strip_more[c, j, at(g, GHOST), :]
                    value = field[c, z, at(g), :] + more[c, z, at(g, GHOST), :]
                    value = jnp.where(lane < 8, pltpu.roll(end, (CY - 64 * half - 8) % CY, 1), value)
                    value = jnp.where(lane >= CY - 8, pltpu.roll(end, 80 - 64 * half, 1), value)
                    field[c, z, at(g), :] = value
        copy = pltpu.make_async_copy(field.at[:, :, own_rows], out, out_sem.at[f])
        copy.start()
        outs.append(copy)

    yr, yi = y_start.at(0, iy, 1), y_start.at(1, iy, 1)
    col_re = acc[0] * yr - acc[1] * yi
    acc[1] = acc[0] * yi + acc[1] * yr
    acc[0] = col_re
    for part in range(2):
        for x in range(CX):
            four = acc[part, pl.ds(x, 4, stride=CX), :]
            cols[part, x, pl.ds(0, 4), :] = four
            cols[part, x, pl.ds(4, 4), :] = four

    upper = lax.broadcasted_iota(jnp.int32, (8, CY), 0) < 4
    at_once = min(8, total)

    def send_far(k):
        other = lax.rem(me + k, total)
        return pltpu.make_async_remote_copy(
            src_ref=f_send.at[k],
            dst_ref=f_recv.at[k - 1],
            send_sem=f_send_sem,
            recv_sem=f_recv_sem,
            device_id=(lax.div(other, nx), lax.rem(other, nx)),
            device_id_type=MESH,
        )

    def project(trip, carry):
        k0 = trip * at_once
        picked = [bands[lax.rem(me + k0 + j, total)] for j in range(at_once)]

        def pair(rows, part, j):
            return jnp.where(upper, rows.at(part, picked[j], 1), rows.at(part, picked[j + 1], 1))

        pairs = range(0, at_once, 2)
        wr = [pair(cell, 0, j) for j in pairs]
        wi = [pair(cell, 1, j) for j in pairs]
        c_re, c_im = cols[0, CX - 1], cols[1, CX - 1]
        re = [c_re for _ in pairs]
        im = [c_im for _ in pairs]
        for x in range(CX - 2, -1, -1):
            c_re, c_im = cols[0, x], cols[1, x]
            re, im = (
                [r * a - i * b + c_re for r, i, a, b in zip(re, im, wr, wi)],
                [r * b + i * a + c_im for r, i, a, b in zip(re, im, wr, wi)],
            )
        for t, j in enumerate(pairs):
            pr, pi = pair(start_phase, 0, j), pair(start_phase, 1, j)
            far_re = re[t] * pr - im[t] * pi
            far_im = re[t] * pi + im[t] * pr
            f_send[k0 + j] = jnp.where(upper, far_re, pltpu.roll(far_im, 4, 0))
            f_send[k0 + j + 1] = jnp.where(upper, pltpu.roll(far_re, 4, 0), far_im)
        for j in range(at_once):
            @pl.when(k0 + j > 0)
            def _(j=j):
                send_far(k0 + j).start()
        return carry

    lax.fori_loop(0, total // at_once, project, 0)

    pltpu.make_async_copy(f_recv, f_recv, f_recv_sem).wait()
    if total <= 64:
        terms = [f_send[0]] + [f_recv[k] for k in range(total - 1)]
        while len(terms) > 1:
            terms = [a + b for a, b in zip(terms[::2], terms[1::2])]
        far_out[...] = terms[0]
    else:
        far_out[...] = lax.fori_loop(0, total - 1, lambda k, t: t + f_recv[k], f_send[0])
    pltpu.make_async_copy(f_recv, f_recv, f_send_sem).wait()
    for i, (sends, _, src, dst, device) in enumerate(every):
        @pl.when(sends)
        def _(i=i, src=src, dst=dst, device=device):
            remote(i, src, dst, device).wait_send()

    def sent(n, carry):
        for k in range(4):
            @pl.when(traces[k][0])
            def _(k=k):
                trace(n, k).wait_send()
        return carry

    lax.fori_loop(0, STEPS, sent, 0)
    for copy in outs:
        copy.wait()


def local(ny, nx, electric, magnetic, material_ids, update_ca, update_cb, face_ranges, band_table):
    total = ny * nx
    bands = band_table.shape[0]
    assert bands == total and electric.shape == (3, NZ, CX, CY)
    scale = 1.0 / math.sqrt(CX * nx * CY * ny)
    f32 = jnp.float32
    vmem = pl.BlockSpec(memory_space=pltpu.VMEM)
    hbm = pl.BlockSpec(memory_space=pltpu.HBM)
    packed, starts = tables(bands, ny)
    e_out, h_out, far = pl.pallas_call(
        functools.partial(kernel, ny, nx, scale, starts),
        out_shape=(
            jax.ShapeDtypeStruct(electric.shape, f32),
            jax.ShapeDtypeStruct(electric.shape, f32),
            jax.ShapeDtypeStruct((8, CY), f32),
        ),
        in_specs=[hbm] * 8,
        out_specs=(hbm, hbm, vmem),
        scratch_shapes=[
            pltpu.VMEM((3, NZ, PITCH, CY), f32),
            pltpu.VMEM((3, NZ, PITCH, CY), f32),
            pltpu.VMEM((NZ, ROWS, CY), jnp.int32),
            pltpu.SMEM((NMAT,), f32),
            pltpu.SMEM((NMAT,), f32),
            pltpu.SMEM((4,), jnp.int32),
            pltpu.SMEM((bands,), jnp.int32),
            pltpu.VMEM(packed.shape, f32),
            pltpu.VMEM((3, NZ, CX, CY), f32),
            pltpu.VMEM((3, NZ, CX, CY), f32),
            pltpu.SemaphoreType.DMA((10,)),
            pltpu.VMEM((NZ, ROWS, CY), f32),
            pltpu.VMEM((NZ, ROWS, CY), f32),
            pltpu.VMEM((3, HALF, PITCH, CY), f32),
            pltpu.VMEM((3, HALF, PITCH, CY), f32),
            pltpu.VMEM((HALF, ROWS, CY), f32),
            pltpu.VMEM((HALF, ROWS, CY), f32),
            pltpu.VMEM((3, NZ, WIDE, CY), f32),
            pltpu.VMEM((3, NZ, WIDE, CY), f32),
            pltpu.VMEM((3, HALF, WIDE, CY), f32),
            pltpu.VMEM((3, HALF, WIDE, CY), f32),
            pltpu.VMEM((7, CX, CY), f32),
            pltpu.VMEM((7, CX, CY), f32),
            pltpu.VMEM((7, ROWS, CY), f32),
            pltpu.VMEM((7, ROWS, CY), f32),
            *[pltpu.VMEM((STEPS, 2 * NZ, CY), f32)] * 4,
            *[pltpu.VMEM((STEPS, 2 * HALF, CY), f32)] * 4,
            pltpu.VMEM((STEPS, 4 * CX, CY), f32),
            pltpu.VMEM((STEPS, 4 * CX, CY), f32),
            pltpu.VMEM((4 * CX, CY), f32),
            pltpu.VMEM((2, 4 * CX, CY), f32),
            pltpu.VMEM((2, CX, 8, CY), f32),
            pltpu.VMEM((2 * total, CY), f32),
            pltpu.VMEM((total, 8, CY), f32),
            pltpu.VMEM((total - 1, 8, CY), f32),
            pltpu.SemaphoreType.DMA((8,)),
            pltpu.SemaphoreType.DMA((8,)),
            pltpu.SemaphoreType.DMA((STEPS, 4)),
            pltpu.SemaphoreType.DMA((STEPS, 4)),
            pltpu.SemaphoreType.DMA,
            pltpu.SemaphoreType.DMA,
            pltpu.SemaphoreType.DMA((2,)),
        ],
        compiler_params=pltpu.CompilerParams(
            collective_id=0, has_side_effects=True, vmem_limit_bytes=62 * 1024 * 1024
        ),
        name="fdtd",
    )(
        electric,
        magnetic,
        material_ids,
        update_ca,
        update_cb,
        face_ranges.reshape(4),
        band_table,
        packed,
    )
    return e_out, h_out, far.reshape(1, 8, CY)


def solution(mesh):
    in_specs = (
        P(None, None, "inner", "grp"),
        P(None, None, "inner", "grp"),
        P(None, "inner", "grp"),
        P(),
        P(),
        P("inner", "grp", None),
        P(),
    )
    out_specs = (
        P(None, None, "inner", "grp"),
        P(None, None, "inner", "grp"),
        P(("grp", "inner"), None, None),
    )
    body = functools.partial(local, mesh.shape["grp"], mesh.shape["inner"])
    return jax.shard_map(body, mesh=mesh, in_specs=in_specs, out_specs=out_specs, check_vma=False)
```

```python
import functools
import math

import jax
import jax.numpy as jnp
import numpy as np
from jax import lax
from jax.experimental import pallas as pl
from jax.experimental.pallas import tpu as pltpu
from jax.sharding import PartitionSpec as P

STEPS = 8
FREQS = 32
ANG_BAND = 4
NMAT = 8
ZF = 8
NZ = 16
CX = 16
CY = 128
PAD = 8
HALO = 8
ROWS = CX + 2 * HALO
GHOST = 4
PITCH = CX + 2 * PAD
WIDE = CX + 2 * GHOST + 2 * PAD
OWN = (1, 2)
HALF = NZ // 2
MESH = pl.DeviceIdType.MESH


def tables(bands, groups):
    f = np.tile(np.arange(FREQS, dtype=np.int64) + 1, ANG_BAND)
    b = np.repeat(np.arange(ANG_BAND, dtype=np.int64) * 33 // ANG_BAND - 16, FREQS)
    a = np.arange(bands, dtype=np.int64) - bands // 2

    def both(turns, period):
        angle = (turns % period) * (2.0 * math.pi / period)
        return np.cos(angle).astype(np.float32), np.sin(angle).astype(np.float32)

    y = np.arange(CY, dtype=np.int64)[:, None]
    proj = np.concatenate(both(f * b * y, 4096), axis=1)
    time = np.stack(both(f * np.arange(STEPS, dtype=np.int64)[:, None], 128))
    y_start = np.stack(both(f * b * CY * np.arange(groups, dtype=np.int64)[:, None], 4096))
    cell = np.stack(both(f * a[:, None], 4096))
    block = np.stack(both(f * a[:, None] * CX, 4096))
    flat = [proj[:, :CY], proj[:, CY:]] + [part for table in (time, y_start, cell, block) for part in table]
    starts = np.cumsum([0] + [-(-part.shape[0] // 8) * 8 for part in flat])
    packed = np.zeros((starts[-1], CY), np.float32)
    for start, part in zip(starts, flat):
        packed[start : start + part.shape[0]] = part
    return packed, tuple(int(start) for start in starts[:-1])


def round_offsets(ny, nx):
    rounds, reach = [], 1
    while reach < max(ny, nx) - 1:
        rounds.append(
            [(0, s * reach) for s in (-1, 1) if reach < nx - 1] + [(s * reach, 0) for s in (-1, 1) if reach < ny - 1]
        )
        reach *= 2
    rounds.append([(s * d, 0) for d in range(1, ny) for s in (-1, 1)])
    return rounds


class Rows:
    def __init__(self, ref, starts):
        self.ref, self.starts = ref, starts

    def at(self, part, first, count):
        return self.ref[pl.ds(self.starts[part] + first, count), :]


def kernel(
    ny, nx, scale, starts,
    e_hbm, h_hbm, ids_hbm, ca_hbm, cb_hbm, face_hbm, bands_hbm, table_hbm,
    e_out, h_out, far_out,
    ef, hf, ids, ca, cb, face, bands, table, e_in, h_in, in_sem,
    coef_a, coef_b, se, sh, strip_a, strip_b, ce, ch, de, dh,
    edge_r, edge_l, from_l, from_r, last_ids, first_ids, left_ids, right_ids,
    own_h, own_e, left_h, right_e, strip_own_h, strip_own_e, strip_left_h, strip_right_e,
    samples, strip_samples, sample, turned, acc, cols, phase, f_send, f_recv,
    send_sem, recv_sem, trace_send, trace_recv, round_sem, f_send_sem, f_recv_sem, out_sem,
):
    iy = lax.axis_index("grp")
    ix = lax.axis_index("inner")
    total = ny * nx
    me = iy * nx + ix
    f32 = jnp.float32
    lane = lax.broadcasted_iota(jnp.int32, (8, CY), 1)
    row = lax.broadcasted_iota(jnp.int32, (8, CY), 0)
    own_rows = pl.ds(PAD, CX)

    loads = [
        pltpu.make_async_copy(src, dst, in_sem.at[i])
        for i, (src, dst) in enumerate(
            (
                (e_hbm, ef.at[:, :, own_rows]),
                (h_hbm, hf.at[:, :, own_rows]),
                (ids_hbm, ids.at[:, pl.ds(HALO, CX)]),
                (ca_hbm, ca),
                (cb_hbm, cb),
                (face_hbm, face),
                (bands_hbm, bands),
                (table_hbm, table),
                (e_hbm, e_in),
                (h_hbm, h_in),
            )
        )
    ]
    for load in loads:
        load.start()
    time, y_start, cell, block = (Rows(table, starts[i : i + 2]) for i in (2, 4, 6, 8))

    barrier = pltpu.get_barrier_semaphore()

    has_xr, has_xl = ix < nx - 1, ix > 0
    has_yr, has_yl = iy < ny - 1, iy > 0

    def within(y, x):
        return (y >= 0) & (y < ny) & (x >= 0) & (x < nx)

    def signal_all(sem, offsets):
        for dy, dx in offsets:
            @pl.when(within(iy + dy, ix + dx))
            def _(dy=dy, dx=dx):
                pl.semaphore_signal(sem, inc=1, device_id=(iy + dy, ix + dx), device_id_type=MESH)

    def partners(offsets):
        return sum(jnp.where(within(iy + dy, ix + dx), 1, 0) for dy, dx in offsets)

    around = [(dy, dx) for dy in (-1, 0, 1) for dx in (-1, 0, 1) if (dy, dx) != (0, 0)]
    signal_all(barrier, around)
    rounds = round_offsets(ny, nx)

    def begin_round(k):
        if k > 0:
            end_round(k - 1)
        signal_all(round_sem.at[k], rounds[k])

    def end_round(k):
        pl.semaphore_wait(round_sem.at[k], partners(rounds[k]))

    low, high = pl.ds(0, 8), pl.ds(8, 8)
    every = (
        (has_yr, has_yl, edge_r, from_l.at[:, pl.ds(HALO, CX)], (iy + 1, ix)),
        (has_yl, has_yr, edge_l, from_r.at[:, pl.ds(HALO, CX)], (iy - 1, ix)),
        (has_yr & has_xr, has_yl & has_xl, edge_r.at[6, high], from_l.at[6, low], (iy + 1, ix + 1)),
        (has_yr & has_xl, has_yl & has_xr, edge_r.at[6, low], from_l.at[6, pl.ds(24, 8)], (iy + 1, ix - 1)),
        (has_yl & has_xr, has_yr & has_xl, edge_l.at[6, high], from_r.at[6, low], (iy - 1, ix + 1)),
        (has_yl & has_xl, has_yr & has_xr, edge_l.at[6, low], from_r.at[6, pl.ds(24, 8)], (iy - 1, ix - 1)),
        (has_xr, has_xl, last_ids, left_ids, (iy, ix + 1)),
        (has_xl, has_xr, first_ids, right_ids, (iy, ix - 1)),
    )
    traces = (
        (has_xr, has_xl, own_h, left_h, (iy, ix + 1)),
        (has_xl, has_xr, own_e, right_e, (iy, ix - 1)),
        (has_xr, has_xl, strip_own_h, strip_left_h, (iy, ix + 1)),
        (has_xl, has_xr, strip_own_e, strip_right_e, (iy, ix - 1)),
    )

    def trace(n, k):
        _, _, src, dst, device = traces[k]
        return pltpu.make_async_remote_copy(
            src_ref=src.at[n],
            dst_ref=dst.at[n],
            send_sem=trace_send.at[n, k],
            recv_sem=trace_recv.at[n, k],
            device_id=device,
            device_id_type=MESH,
        )

    def send_trace(n, k):
        @pl.when(traces[k][0])
        def _():
            trace(n, k).start()

    def await_trace(n, k):
        @pl.when(traces[k][1])
        def _():
            trace(n, k).wait_recv()

    def remote(i, src, dst, device):
        return pltpu.make_async_remote_copy(
            src_ref=src,
            dst_ref=dst,
            send_sem=send_sem.at[i],
            recv_sem=recv_sem.at[i],
            device_id=device,
            device_id_type=MESH,
        )

    def start_copies(which):
        for i in which:
            sends, _, src, dst, device = every[i]

            @pl.when(sends)
            def _(i=i, src=src, dst=dst, device=device):
                remote(i, src, dst, device).start()

    def await_copies(which):
        for i in which:
            _, receives, src, dst, _ = every[i]

            @pl.when(receives)
            def _(i=i, src=src, dst=dst):
                remote(i, src, dst, (iy, ix)).wait_recv()

    y_copies, corner_copies, x_copies = range(2), range(2, 6), range(6, 8)

    for given, fresh, arrived in ((has_xl, left_ids, (left_h, strip_left_h)), (has_xr, right_ids, (right_e, strip_right_e))):
        @pl.when(jnp.logical_not(given))
        def _(fresh=fresh, arrived=arrived):
            for buf in arrived:
                buf[...] = jnp.zeros(buf.shape, f32)
            fresh[...] = jnp.full(fresh.shape, NMAT, jnp.int32)

    for edge, side in ((from_l, has_yl), (from_r, has_yr)):
        @pl.when(jnp.logical_not(side))
        def _(edge=edge):
            edge[pl.ds(0, 6), pl.ds(HALO, CX), :] = jnp.zeros((6, CX, CY), f32)

        for given, rows, count in ((side, 8, 16), (side & has_xl, 0, 8), (side & has_xr, 24, 8)):
            @pl.when(jnp.logical_not(given))
            def _(edge=edge, rows=rows, count=count):
                edge[6, pl.ds(rows, count), :] = jnp.full((count, CY), float(NMAT), f32)

    for fields in ((ef, hf), (se, sh)):
        for field in fields:
            for c in range(3):
                for z in range(field.shape[1]):
                    for rows in (0, PAD + CX):
                        field[c, z, pl.ds(rows, PAD), :] = jnp.zeros((PAD, CY), f32)
    ids[:, pl.ds(0, 8), :] = jnp.full((NZ, 8, CY), NMAT, jnp.int32)
    ids[:, pl.ds(HALO + CX, 8), :] = jnp.full((NZ, 8, CY), NMAT, jnp.int32)
    for field in (ce, ch, de, dh):
        field[...] = jnp.zeros(field.shape, f32)

    pl.semaphore_wait(barrier, partners(around))
    begin_round(0)
    for load in loads:
        load.wait()

    for z in range(NZ):
        spot = pl.ds(z * GHOST, GHOST)
        last_ids[spot, :] = ids[z, pl.ds(HALO + CX - GHOST, GHOST), :]
        first_ids[spot, :] = ids[z, pl.ds(HALO, GHOST), :]
    start_copies(x_copies)
    for i in range(7):
        for g in range(2):
            right = jnp.zeros((8, CY), f32)
            left = jnp.zeros((8, CY), f32)
            for z in range(NZ):
                rows = pl.ds(8 * g + PAD, 8)
                if i < 6:
                    value = (ef, hf)[i // 3][i % 3, z, rows, :]
                else:
                    value = ids[z, pl.ds(8 * g + HALO, 8), :].astype(f32)
                here = (lane >= 8 * z) & (lane < 8 * z + 8)
                right = jnp.where(here, pltpu.roll(value, (8 * z - 120) % CY, 1) if z < 15 else value, right)
                left = jnp.where(here, pltpu.roll(value, 8 * z, 1) if z else value, left)
            edge_r[i, pl.ds(8 * g, 8), :] = right
            edge_l[i, pl.ds(8 * g, 8), :] = left
    start_copies(y_copies)
    start_copies(corner_copies)

    def lookup(here):
        va = jnp.zeros((8, CY), f32)
        vb = jnp.zeros((8, CY), f32)
        for m in range(NMAT):
            chosen = here == m
            va = jnp.where(chosen, ca[m], va)
            vb = jnp.where(chosen, cb[m], vb)
        return va, vb

    def coefficients(groups):
        def one(z, carry):
            for g in groups:
                va, vb = lookup(ids[z, pl.ds(8 * g, 8), :])
                coef_a[z, pl.ds(8 * g, 8), :] = va
                coef_b[z, pl.ds(8 * g, 8), :] = vb
            return carry

        lax.fori_loop(0, NZ, one, 0)

    in_half = lax.rem(lane, CY // 2)

    def strips(groups):
        spots = (
            (0, 8, (lane >= 8) & (lane < 24)),
            (0, 48, (lane >= 32) & (lane < 48)),
            (1, 72, (lane >= 72) & (lane < 88)),
            (1, 112, (lane >= 96) & (lane < 112)),
        )

        def pack(j, values, i, rows, base):
            out = jnp.full((8, CY), base, f32)
            for half, shift, mask in spots:
                out = jnp.where(mask, pltpu.roll(values[half], shift, 1), out)
            before, after = from_l[i, rows, :], from_r[i, rows, :]
            out = jnp.where(in_half < 8, pltpu.roll(before, (CY - 8 * j) % CY, 1) if j else before, out)
            return jnp.where((in_half >= 48) & (in_half < 56), pltpu.roll(after, (CY + 48 - 8 * j) % CY, 1), out)

        for g in groups:
            rows = pl.ds(8 * g, 8)
            padded = pl.ds(PAD + 8 * g - HALO, 8)
            for j in range(HALF):
                for i in range(6 if g in OWN else 0):
                    source, target = ((e_in, se), (h_in, sh))[i // 3]
                    values = [source[i % 3, j + HALF * half, pl.ds(8 * g - HALO, 8), :] for half in range(2)]
                    target[i % 3, j, padded, :] = pack(j, values, i, rows, 0.0)
                values = [ids[j + HALF * half, rows, :].astype(f32) for half in range(2)]
                va, vb = lookup(pack(j, values, 6, rows, float(NMAT)))
                strip_a[j, rows, :] = va
                strip_b[j, rows, :] = vb

    def power(bit, carry):
        pr, pi, br, bi = carry
        take = lax.rem(lax.shift_right_logical(ix, bit), 2) == 1
        nr = pr * br - pi * bi
        ni = pr * bi + pi * br
        return (
            jnp.where(take, nr, pr),
            jnp.where(take, ni, pi),
            br * br - bi * bi,
            2.0 * br * bi,
        )

    coefficients(OWN)
    rows_at_once = 8
    for start in range(0, total, rows_at_once):
        part = pl.ds(start, rows_at_once)
        carry = (
            jnp.full((rows_at_once, CY), scale, jnp.float32),
            jnp.zeros((rows_at_once, CY), jnp.float32),
            block.at(0, start, rows_at_once),
            block.at(1, start, rows_at_once),
        )
        for bit in range(max(1, (nx - 1).bit_length())):
            carry = power(bit, carry)
        phase[part, :] = carry[0]
        phase[pl.ds(total + start, rows_at_once), :] = carry[1]
    start_phase = Rows(phase, (0, total))

    half_y = jnp.where((in_half < 8) & (iy == 0), 0.0, 0.5).astype(f32)
    on_face = [
        (row + 8 * g >= face[0]) & (row + 8 * g < face[1]) & (lane >= face[2]) & (lane < face[3])
        for g in range(2)
    ]

    def at(g, shift=0):
        return pl.ds(PAD + 8 * g + shift, 8)

    zero = jnp.zeros((8, CY), f32)
    low_half = lane < CY // 2

    def new_magnetic(e, h, z, groups, here, above, factor, source):
        out = {}
        for g in groups:
            ex, ey, ez = here[g]
            ex_z, ey_z = above[g]
            ey_x, ez_x = e[1, z, at(g, 1), :], e[2, z, at(g, 1), :]
            if source is not None and g != 1:
                more_y, more_z = source(g, z)
                ey_x, ez_x = ey_x + more_y, ez_x + more_z
            ex_y, ez_y = pltpu.roll(ex, CY - 1, 1), pltpu.roll(ez, CY - 1, 1)
            hx = h[0, z, at(g), :] - factor * ((ez_y - ez) - (ey_z - ey))
            hy = h[1, z, at(g), :] - factor * ((ex_z - ex) - (ez_x - ez))
            hz = h[2, z, at(g), :] - factor * ((ey_x - ey) - (ex_y - ex))
            h[0, z, at(g), :] = hx
            h[1, z, at(g), :] = hy
            h[2, z, at(g), :] = hz
            out[g] = (hx, hy, hz)
        return out

    def new_electric(e, h, a, b, z, groups, base, here, now, below, source):
        out = {}
        for g in groups:
            ex, ey, ez = here[g]
            hx, hy, hz = now[g]
            hx_z, hy_z = below[g]
            hy_x, hz_x = h[1, z, at(g, -1), :], h[2, z, at(g, -1), :]
            if source is not None and g != 1:
                more_y, more_z = source(g, z)
                hy_x, hz_x = hy_x + more_y, hz_x + more_z
            hx_y, hz_y = pltpu.roll(hx, 1, 1), pltpu.roll(hz, 1, 1)
            va, vb = a[z, pl.ds(base + 8 * g, 8), :], b[z, pl.ds(base + 8 * g, 8), :]
            ex = va * ex + vb * ((hz - hz_y) - (hy - hy_z))
            ey = va * ey + vb * ((hx - hx_z) - (hz - hz_x))
            ez = va * ez + vb * ((hy - hy_x) - (hx - hx_y))
            e[0, z, at(g), :] = ex
            e[1, z, at(g), :] = ey
            e[2, z, at(g), :] = ez
            out[g] = (ex, ey)
        return out

    def plane(e, z, groups):
        return {g: tuple(e[c, z, at(g), :] for c in range(3)) for g in groups}

    def two(values):
        return {g: v[:2] for g, v in values.items()}

    def advance(e, h, groups, base, source_e=None, source_h=None):
        here = plane(e, 0, groups)
        nothing = {g: (zero, zero) for g in groups}
        below = nothing
        for z in range(NZ):
            ahead = plane(e, z + 1, groups) if z < NZ - 1 else None
            above = two(ahead) if ahead else nothing
            now = new_magnetic(e, h, z, groups, here, above, 0.5, source_e)
            new_electric(e, h, coef_a, coef_b, z, groups, base, here, now, below, source_h)
            below, here = two(now), ahead

    def advance_strips(e, h, groups, base, source_e=None, source_h=None):
        here = first = plane(e, 0, groups)
        for j in range(HALF):
            if j < HALF - 1:
                ahead = plane(e, j + 1, groups)
                above = two(ahead)
            else:
                ahead = None
                above = {
                    g: tuple(jnp.where(low_half, pltpu.roll(v, CY // 2, 1), 0.0) for v in first[g][:2]) for g in groups
                }
            now = new_magnetic(e, h, j, groups, here, above, half_y, source_e)
            if j:
                new_electric(e, h, strip_a, strip_b, j, groups, base, here, now, below, source_h)
            else:
                start = now
            below, here = two(now), ahead
        below = {g: tuple(jnp.where(low_half, 0.0, pltpu.roll(v, CY // 2, 1)) for v in below[g]) for g in groups}
        new_electric(e, h, strip_a, strip_b, 0, groups, base, plane(e, 0, groups), start, below, source_h)

    def borders(n, e, h, mine_e, mine_h, run, k):
        depth = e.shape[1]
        for c in (1, 2):
            mine_e[n, pl.ds((c - 1) * depth, depth), :] = e[c, :, PAD, :]
        send_trace(n, k + 1)
        run(e, h, (0, 1), HALO)
        for c in (1, 2):
            mine_h[n, pl.ds((c - 1) * depth, depth), :] = h[c, :, PAD + CX - 1, :]
        send_trace(n, k)

    def keep(n, e, h, z, kept, first_row, add):
        for c, (field, part) in enumerate(((e, 0), (e, 1), (h, 0), (h, 1))):
            for k in range(2):
                spot = pl.ds(c * CX + 8 * k, 8)
                value = field[part, z, pl.ds(first_row + 8 * k, 8), :]
                kept[n, spot, :] = kept[n, spot, :] + value if add else value

    def alone(n, carry):
        borders(n, ef, hf, own_e, own_h, advance, 0)
        keep(n, ef, hf, ZF, samples, PAD, False)
        return carry

    def alone_strips(n, carry):
        borders(n, se, sh, strip_own_e, strip_own_h, advance_strips, 2)
        keep(n, se, sh, 0, strip_samples, PAD, False)
        return carry

    def sources(n, left, right, spot, depth):
        masks = {0: (row == spot) & has_xl, 2: row == spot}

        def source(g, z):
            buf = left if g == 0 else right
            return tuple(
                jnp.where(masks[g], jnp.broadcast_to(buf[n, pl.ds(c * depth + z, 1), :], (8, CY)), 0.0) for c in range(2)
            )

        return source

    SHIFT = HALO - GHOST

    def correct(groups, n, carry):
        await_trace(n, 0)
        await_trace(n, 1)
        advance(
            ce, ch, groups, SHIFT,
            sources(n, own_e, right_e, GHOST - 1, NZ), sources(n, left_h, own_h, GHOST, NZ),
        )
        keep(n, ce, ch, ZF, samples, PAD + GHOST, True)
        return carry

    def correct_strips(groups, n):
        advance_strips(
            de, dh, groups, SHIFT,
            sources(n, strip_own_e, strip_right_e, GHOST - 1, HALF), sources(n, strip_left_h, strip_own_h, GHOST, HALF),
        )
        keep(n, de, dh, 0, strip_samples, PAD + GHOST, True)

    def correct_both(strip_groups, i, carry):
        n = STEPS // 2 + i
        await_trace(2 * i, 2)
        await_trace(2 * i, 3)
        await_trace(2 * i + 1, 2)
        await_trace(2 * i + 1, 3)
        correct((0, 1, 2), n, carry)
        correct_strips(strip_groups, 2 * i)
        correct_strips(strip_groups, 2 * i + 1)
        return carry

    lax.fori_loop(0, STEPS, alone, 0)
    begin_round(1)
    await_copies(y_copies)
    strips(OWN)
    lax.fori_loop(0, STEPS, alone_strips, 0)
    begin_round(2)
    await_copies(x_copies)
    await_copies(corner_copies)
    for z in range(NZ):
        spot = pl.ds(z * GHOST, GHOST)
        ids[z, pl.ds(HALO - GHOST, GHOST), :] = left_ids[spot, :]
        ids[z, pl.ds(HALO + CX, GHOST), :] = right_ids[spot, :]
    strips((0, 3))
    coefficients((0, 3))
    lax.fori_loop(0, STEPS // 2, functools.partial(correct, (0, 2)), 0)
    lax.fori_loop(0, STEPS // 4, functools.partial(correct_both, (0, 2)), 0)
    begin_round(3)
    lax.fori_loop(STEPS // 4, STEPS // 2, functools.partial(correct_both, (0, 1, 2)), 0)

    for k in range(4, len(rounds)):
        begin_round(k)
    for n in range(STEPS):
        for c in range(4):
            for k in range(2):
                spot = pl.ds(c * CX + 8 * k, 8)
                end = strip_samples[n, spot, :]
                value = jnp.where(lane < 8, pltpu.roll(end, 56, 1), samples[n, spot, :])
                value = jnp.where(lane >= CY - 8, pltpu.roll(end, 16, 1), value)
                sample[pl.ds(n * 4 * CX + c * CX + 8 * k, 8), :] = jnp.where(on_face[k], value, 0.0)
    for part in range(2):
        turned[part] = jnp.dot(
            sample[...],
            table[pl.ds(starts[part], CY), :],
            precision=lax.Precision.HIGHEST,
            preferred_element_type=f32,
        )
    for first in range(0, 4 * CX, 8):
        re, im = zero, zero
        for n in range(STEPS):
            g_re, g_im = (turned[part, pl.ds(n * 4 * CX + first, 8), :] for part in range(2))
            ct, st = time.at(0, n, 1), time.at(1, n, 1)
            re += ct * g_re + st * g_im
            im += ct * g_im - st * g_re
        acc[0, pl.ds(first, 8), :] = re
        acc[1, pl.ds(first, 8), :] = im

    end_round(len(rounds) - 1)
    yr, yi = y_start.at(0, iy, 1), y_start.at(1, iy, 1)
    col_re = acc[0] * yr - acc[1] * yi
    acc[1] = acc[0] * yi + acc[1] * yr
    acc[0] = col_re
    for part in range(2):
        for x in range(CX):
            four = acc[part, pl.ds(x, 4, stride=CX), :]
            cols[part, x, pl.ds(0, 4), :] = four
            cols[part, x, pl.ds(4, 4), :] = four

    upper = lax.broadcasted_iota(jnp.int32, (8, CY), 0) < 4
    at_once = min(8, total)

    def send_far(k):
        other = lax.rem(me + k, total)
        return pltpu.make_async_remote_copy(
            src_ref=f_send.at[k],
            dst_ref=f_recv.at[k - 1],
            send_sem=f_send_sem,
            recv_sem=f_recv_sem,
            device_id=(lax.div(other, nx), lax.rem(other, nx)),
            device_id_type=MESH,
        )

    def project(trip, carry):
        k0 = trip * at_once
        picked = [bands[lax.rem(me + k0 + j, total)] for j in range(at_once)]

        def pair(rows, part, j):
            return jnp.where(upper, rows.at(part, picked[j], 1), rows.at(part, picked[j + 1], 1))

        pairs = range(0, at_once, 2)
        wr = [pair(cell, 0, j) for j in pairs]
        wi = [pair(cell, 1, j) for j in pairs]
        c_re, c_im = cols[0, CX - 1], cols[1, CX - 1]
        re = [c_re for _ in pairs]
        im = [c_im for _ in pairs]
        for x in range(CX - 2, -1, -1):
            c_re, c_im = cols[0, x], cols[1, x]
            re, im = (
                [r * a - i * b + c_re for r, i, a, b in zip(re, im, wr, wi)],
                [r * b + i * a + c_im for r, i, a, b in zip(re, im, wr, wi)],
            )
        for t, j in enumerate(pairs):
            pr, pi = pair(start_phase, 0, j), pair(start_phase, 1, j)
            far_re = re[t] * pr - im[t] * pi
            far_im = re[t] * pi + im[t] * pr
            f_send[k0 + j] = jnp.where(upper, far_re, pltpu.roll(far_im, 4, 0))
            f_send[k0 + j + 1] = jnp.where(upper, pltpu.roll(far_re, 4, 0), far_im)
        for j in range(at_once):
            @pl.when(k0 + j > 0)
            def _(j=j):
                send_far(k0 + j).start()
        return carry

    lax.fori_loop(0, total // at_once, project, 0)

    outs = []
    for f, (field, strip, more, strip_more, out) in enumerate(((ef, se, ce, de, e_out), (hf, sh, ch, dh, h_out))):
        for c in range(3):
            for z in range(NZ):
                half, j = z // HALF, z % HALF
                for g in range(2):
                    end = strip[c, j, at(g), :] + strip_more[c, j, at(g, GHOST), :]
                    value = field[c, z, at(g), :] + more[c, z, at(g, GHOST), :]
                    value = jnp.where(lane < 8, pltpu.roll(end, (CY - 64 * half - 8) % CY, 1), value)
                    value = jnp.where(lane >= CY - 8, pltpu.roll(end, 80 - 64 * half, 1), value)
                    field[c, z, at(g), :] = value
        copy = pltpu.make_async_copy(field.at[:, :, own_rows], out, out_sem.at[f])
        copy.start()
        outs.append(copy)

    pltpu.make_async_copy(f_recv, f_recv, f_recv_sem).wait()
    if total <= 64:
        terms = [f_send[0]] + [f_recv[k] for k in range(total - 1)]
        while len(terms) > 1:
            terms = [a + b for a, b in zip(terms[::2], terms[1::2])]
        far_out[...] = terms[0]
    else:
        far_out[...] = lax.fori_loop(0, total - 1, lambda k, t: t + f_recv[k], f_send[0])
    pltpu.make_async_copy(f_recv, f_recv, f_send_sem).wait()
    for i, (sends, _, src, dst, device) in enumerate(every):
        @pl.when(sends)
        def _(i=i, src=src, dst=dst, device=device):
            remote(i, src, dst, device).wait_send()

    def sent(n, carry):
        for k in range(4):
            @pl.when(traces[k][0])
            def _(k=k):
                trace(n, k).wait_send()
        return carry

    lax.fori_loop(0, STEPS, sent, 0)
    for copy in outs:
        copy.wait()


def local(ny, nx, electric, magnetic, material_ids, update_ca, update_cb, face_ranges, band_table):
    total = ny * nx
    bands = band_table.shape[0]
    assert bands == total and electric.shape == (3, NZ, CX, CY)
    scale = 1.0 / math.sqrt(CX * nx * CY * ny)
    f32 = jnp.float32
    vmem = pl.BlockSpec(memory_space=pltpu.VMEM)
    hbm = pl.BlockSpec(memory_space=pltpu.HBM)
    packed, starts = tables(bands, ny)
    e_out, h_out, far = pl.pallas_call(
        functools.partial(kernel, ny, nx, scale, starts),
        out_shape=(
            jax.ShapeDtypeStruct(electric.shape, f32),
            jax.ShapeDtypeStruct(electric.shape, f32),
            jax.ShapeDtypeStruct((8, CY), f32),
        ),
        in_specs=[hbm] * 8,
        out_specs=(hbm, hbm, vmem),
        scratch_shapes=[
            pltpu.VMEM((3, NZ, PITCH, CY), f32),
            pltpu.VMEM((3, NZ, PITCH, CY), f32),
            pltpu.VMEM((NZ, ROWS, CY), jnp.int32),
            pltpu.SMEM((NMAT,), f32),
            pltpu.SMEM((NMAT,), f32),
            pltpu.SMEM((4,), jnp.int32),
            pltpu.SMEM((bands,), jnp.int32),
            pltpu.VMEM(packed.shape, f32),
            pltpu.VMEM((3, NZ, CX, CY), f32),
            pltpu.VMEM((3, NZ, CX, CY), f32),
            pltpu.SemaphoreType.DMA((10,)),
            pltpu.VMEM((NZ, ROWS, CY), f32),
            pltpu.VMEM((NZ, ROWS, CY), f32),
            pltpu.VMEM((3, HALF, PITCH, CY), f32),
            pltpu.VMEM((3, HALF, PITCH, CY), f32),
            pltpu.VMEM((HALF, ROWS, CY), f32),
            pltpu.VMEM((HALF, ROWS, CY), f32),
            pltpu.VMEM((3, NZ, WIDE, CY), f32),
            pltpu.VMEM((3, NZ, WIDE, CY), f32),
            pltpu.VMEM((3, HALF, WIDE, CY), f32),
            pltpu.VMEM((3, HALF, WIDE, CY), f32),
            pltpu.VMEM((7, CX, CY), f32),
            pltpu.VMEM((7, CX, CY), f32),
            pltpu.VMEM((7, ROWS, CY), f32),
            pltpu.VMEM((7, ROWS, CY), f32),
            *[pltpu.VMEM((NZ * GHOST, CY), jnp.int32)] * 4,
            *[pltpu.VMEM((STEPS, 2 * NZ, CY), f32)] * 4,
            *[pltpu.VMEM((STEPS, 2 * HALF, CY), f32)] * 4,
            pltpu.VMEM((STEPS, 4 * CX, CY), f32),
            pltpu.VMEM((STEPS, 4 * CX, CY), f32),
            pltpu.VMEM((STEPS * 4 * CX, CY), f32),
            pltpu.VMEM((2, STEPS * 4 * CX, CY), f32),
            pltpu.VMEM((2, 4 * CX, CY), f32),
            pltpu.VMEM((2, CX, 8, CY), f32),
            pltpu.VMEM((2 * total, CY), f32),
            pltpu.VMEM((total, 8, CY), f32),
            pltpu.VMEM((total - 1, 8, CY), f32),
            pltpu.SemaphoreType.DMA((8,)),
            pltpu.SemaphoreType.DMA((8,)),
            pltpu.SemaphoreType.DMA((STEPS, 4)),
            pltpu.SemaphoreType.DMA((STEPS, 4)),
            pltpu.SemaphoreType.REGULAR((len(round_offsets(ny, nx)),)),
            pltpu.SemaphoreType.DMA,
            pltpu.SemaphoreType.DMA,
            pltpu.SemaphoreType.DMA((2,)),
        ],
        compiler_params=pltpu.CompilerParams(
            collective_id=0, has_side_effects=True, vmem_limit_bytes=62 * 1024 * 1024
        ),
        name="fdtd",
    )(
        electric,
        magnetic,
        material_ids,
        update_ca,
        update_cb,
        face_ranges.reshape(4),
        band_table,
        packed,
    )
    return e_out, h_out, far.reshape(1, 8, CY)


def solution(mesh):
    in_specs = (
        P(None, None, "inner", "grp"),
        P(None, None, "inner", "grp"),
        P(None, "inner", "grp"),
        P(),
        P(),
        P("inner", "grp", None),
        P(),
    )
    out_specs = (
        P(None, None, "inner", "grp"),
        P(None, None, "inner", "grp"),
        P(("grp", "inner"), None, None),
    )
    body = functools.partial(local, mesh.shape["grp"], mesh.shape["inner"])
    return jax.shard_map(body, mesh=mesh, in_specs=in_specs, out_specs=out_specs, check_vma=False)
```

```python
import functools
import math

import jax
import jax.numpy as jnp
import numpy as np
from jax import lax
from jax.experimental import pallas as pl
from jax.experimental.pallas import tpu as pltpu
from jax.sharding import PartitionSpec as P

STEPS = 8
FREQS = 32
ANG_BAND = 4
NMAT = 8
ZF = 8
NZ = 16
CX = 16
CY = 128
PAD = 8
HALO = 8
ROWS = CX + 2 * HALO
GHOST = 4
PITCH = CX + 2 * PAD
WIDE = CX + 2 * GHOST + 2 * PAD
OWN = (1, 2)
HALF = NZ // 2
MESH = pl.DeviceIdType.MESH


def tables(bands, groups):
    f = np.tile(np.arange(FREQS, dtype=np.int64) + 1, ANG_BAND)
    b = np.repeat(np.arange(ANG_BAND, dtype=np.int64) * 33 // ANG_BAND - 16, FREQS)
    a = np.arange(bands, dtype=np.int64) - bands // 2

    def both(turns, period):
        angle = (turns % period) * (2.0 * math.pi / period)
        return np.cos(angle).astype(np.float32), np.sin(angle).astype(np.float32)

    y = np.arange(CY, dtype=np.int64)[:, None]
    proj = np.concatenate(both(f * b * y, 4096), axis=1)
    time = np.stack(both(f * np.arange(STEPS, dtype=np.int64)[:, None], 128))
    y_start = np.stack(both(f * b * CY * np.arange(groups, dtype=np.int64)[:, None], 4096))
    cell = np.stack(both(f * a[:, None], 4096))
    block = np.stack(both(f * a[:, None] * CX, 4096))
    flat = [proj[:, :CY], proj[:, CY:]] + [part for table in (time, y_start, cell, block) for part in table]
    starts = np.cumsum([0] + [-(-part.shape[0] // 8) * 8 for part in flat])
    packed = np.zeros((starts[-1], CY), np.float32)
    for start, part in zip(starts, flat):
        packed[start : start + part.shape[0]] = part
    return packed, tuple(int(start) for start in starts[:-1])


def round_offsets(ny, nx):
    rounds, reach = [], 1
    while reach < max(ny, nx) - 1:
        rounds.append(
            [(0, s * reach) for s in (-1, 1) if reach < nx - 1] + [(s * reach, 0) for s in (-1, 1) if reach < ny - 1]
        )
        reach *= 2
    rounds.append([(s * d, 0) for d in range(1, ny) for s in (-1, 1)])
    return rounds


class Rows:
    def __init__(self, ref, starts):
        self.ref, self.starts = ref, starts

    def at(self, part, first, count):
        return self.ref[pl.ds(self.starts[part] + first, count), :]


def kernel(
    ny, nx, scale, starts,
    e_hbm, h_hbm, ids_hbm, ca_hbm, cb_hbm, face_hbm, bands_hbm, table_hbm,
    e_out, h_out, far_out,
    ef, hf, ids, ca, cb, face, bands, table, e_in, h_in, in_sem,
    coef_a, coef_b, se, sh, strip_a, strip_b, ce, ch, de, dh,
    edge_r, edge_l, from_l, from_r, last_ids, first_ids, left_ids, right_ids,
    own_h, own_e, left_h, right_e, strip_own_h, strip_own_e, strip_left_h, strip_right_e,
    samples, strip_samples, sample, turned, acc, cols, phase, f_send, f_recv,
    send_sem, recv_sem, trace_send, trace_recv, round_sem, f_send_sem, f_recv_sem,
):
    iy = lax.axis_index("grp")
    ix = lax.axis_index("inner")
    total = ny * nx
    me = iy * nx + ix
    f32 = jnp.float32
    lane = lax.broadcasted_iota(jnp.int32, (8, CY), 1)
    row = lax.broadcasted_iota(jnp.int32, (8, CY), 0)
    own_rows = pl.ds(PAD, CX)

    loads = [
        pltpu.make_async_copy(src, dst, in_sem.at[i])
        for i, (src, dst) in enumerate(
            (
                (e_hbm, ef.at[:, :, own_rows]),
                (h_hbm, hf.at[:, :, own_rows]),
                (ids_hbm, ids.at[:, pl.ds(HALO, CX)]),
                (ca_hbm, ca),
                (cb_hbm, cb),
                (face_hbm, face),
                (bands_hbm, bands),
                (table_hbm, table),
                (e_hbm, e_in),
                (h_hbm, h_in),
            )
        )
    ]
    for load in loads:
        load.start()
    time, y_start, cell, block = (Rows(table, starts[i : i + 2]) for i in (2, 4, 6, 8))

    barrier = pltpu.get_barrier_semaphore()

    has_xr, has_xl = ix < nx - 1, ix > 0
    has_yr, has_yl = iy < ny - 1, iy > 0

    def within(y, x):
        return (y >= 0) & (y < ny) & (x >= 0) & (x < nx)

    def signal_all(sem, offsets):
        for dy, dx in offsets:
            @pl.when(within(iy + dy, ix + dx))
            def _(dy=dy, dx=dx):
                pl.semaphore_signal(sem, inc=1, device_id=(iy + dy, ix + dx), device_id_type=MESH)

    def partners(offsets):
        return sum(jnp.where(within(iy + dy, ix + dx), 1, 0) for dy, dx in offsets)

    around = [(dy, dx) for dy in (-1, 0, 1) for dx in (-1, 0, 1) if (dy, dx) != (0, 0)]
    signal_all(barrier, around)
    rounds = round_offsets(ny, nx)

    def begin_round(k):
        if k > 0:
            end_round(k - 1)
        signal_all(round_sem.at[k], rounds[k])

    def end_round(k):
        pl.semaphore_wait(round_sem.at[k], partners(rounds[k]))

    low, high = pl.ds(0, 8), pl.ds(8, 8)
    every = (
        (has_yr, has_yl, edge_r, from_l.at[:, pl.ds(HALO, CX)], (iy + 1, ix)),
        (has_yl, has_yr, edge_l, from_r.at[:, pl.ds(HALO, CX)], (iy - 1, ix)),
        (has_yr & has_xr, has_yl & has_xl, edge_r.at[6, high], from_l.at[6, low], (iy + 1, ix + 1)),
        (has_yr & has_xl, has_yl & has_xr, edge_r.at[6, low], from_l.at[6, pl.ds(24, 8)], (iy + 1, ix - 1)),
        (has_yl & has_xr, has_yr & has_xl, edge_l.at[6, high], from_r.at[6, low], (iy - 1, ix + 1)),
        (has_yl & has_xl, has_yr & has_xr, edge_l.at[6, low], from_r.at[6, pl.ds(24, 8)], (iy - 1, ix - 1)),
        (has_xr, has_xl, last_ids, left_ids, (iy, ix + 1)),
        (has_xl, has_xr, first_ids, right_ids, (iy, ix - 1)),
    )
    traces = (
        (has_xr, has_xl, own_h, left_h, (iy, ix + 1)),
        (has_xl, has_xr, own_e, right_e, (iy, ix - 1)),
        (has_xr, has_xl, strip_own_h, strip_left_h, (iy, ix + 1)),
        (has_xl, has_xr, strip_own_e, strip_right_e, (iy, ix - 1)),
    )

    def trace(n, k):
        _, _, src, dst, device = traces[k]
        return pltpu.make_async_remote_copy(
            src_ref=src.at[n],
            dst_ref=dst.at[n],
            send_sem=trace_send.at[n, k],
            recv_sem=trace_recv.at[n, k],
            device_id=device,
            device_id_type=MESH,
        )

    def send_trace(n, k):
        @pl.when(traces[k][0])
        def _():
            trace(n, k).start()

    def await_trace(n, k):
        @pl.when(traces[k][1])
        def _():
            trace(n, k).wait_recv()

    def remote(i, src, dst, device):
        return pltpu.make_async_remote_copy(
            src_ref=src,
            dst_ref=dst,
            send_sem=send_sem.at[i],
            recv_sem=recv_sem.at[i],
            device_id=device,
            device_id_type=MESH,
        )

    def start_copies(which):
        for i in which:
            sends, _, src, dst, device = every[i]

            @pl.when(sends)
            def _(i=i, src=src, dst=dst, device=device):
                remote(i, src, dst, device).start()

    def await_copies(which):
        for i in which:
            _, receives, src, dst, _ = every[i]

            @pl.when(receives)
            def _(i=i, src=src, dst=dst):
                remote(i, src, dst, (iy, ix)).wait_recv()

    y_copies, corner_copies, x_copies = range(2), range(2, 6), range(6, 8)

    for given, fresh, arrived in ((has_xl, left_ids, (left_h, strip_left_h)), (has_xr, right_ids, (right_e, strip_right_e))):
        @pl.when(jnp.logical_not(given))
        def _(fresh=fresh, arrived=arrived):
            for buf in arrived:
                buf[...] = jnp.zeros(buf.shape, f32)
            fresh[...] = jnp.full(fresh.shape, NMAT, jnp.int32)

    for edge, side in ((from_l, has_yl), (from_r, has_yr)):
        @pl.when(jnp.logical_not(side))
        def _(edge=edge):
            edge[pl.ds(0, 6), pl.ds(HALO, CX), :] = jnp.zeros((6, CX, CY), f32)

        for given, rows, count in ((side, 8, 16), (side & has_xl, 0, 8), (side & has_xr, 24, 8)):
            @pl.when(jnp.logical_not(given))
            def _(edge=edge, rows=rows, count=count):
                edge[6, pl.ds(rows, count), :] = jnp.full((count, CY), float(NMAT), f32)

    for fields in ((ef, hf), (se, sh)):
        for field in fields:
            for c in range(3):
                for z in range(field.shape[1]):
                    for rows in (0, PAD + CX):
                        field[c, z, pl.ds(rows, PAD), :] = jnp.zeros((PAD, CY), f32)
    ids[:, pl.ds(0, 8), :] = jnp.full((NZ, 8, CY), NMAT, jnp.int32)
    ids[:, pl.ds(HALO + CX, 8), :] = jnp.full((NZ, 8, CY), NMAT, jnp.int32)
    for field in (ce, ch, de, dh):
        field[...] = jnp.zeros(field.shape, f32)

    pl.semaphore_wait(barrier, partners(around))
    begin_round(0)
    for load in loads:
        load.wait()

    for z in range(NZ):
        spot = pl.ds(z * GHOST, GHOST)
        last_ids[spot, :] = ids[z, pl.ds(HALO + CX - GHOST, GHOST), :]
        first_ids[spot, :] = ids[z, pl.ds(HALO, GHOST), :]
    start_copies(x_copies)
    for i in range(7):
        for g in range(2):
            right = jnp.zeros((8, CY), f32)
            left = jnp.zeros((8, CY), f32)
            for z in range(NZ):
                rows = pl.ds(8 * g + PAD, 8)
                if i < 6:
                    value = (ef, hf)[i // 3][i % 3, z, rows, :]
                else:
                    value = ids[z, pl.ds(8 * g + HALO, 8), :].astype(f32)
                here = (lane >= 8 * z) & (lane < 8 * z + 8)
                right = jnp.where(here, pltpu.roll(value, (8 * z - 120) % CY, 1) if z < 15 else value, right)
                left = jnp.where(here, pltpu.roll(value, 8 * z, 1) if z else value, left)
            edge_r[i, pl.ds(8 * g, 8), :] = right
            edge_l[i, pl.ds(8 * g, 8), :] = left
    start_copies(y_copies)
    start_copies(corner_copies)

    def lookup(here):
        va = jnp.zeros((8, CY), f32)
        vb = jnp.zeros((8, CY), f32)
        for m in range(NMAT):
            chosen = here == m
            va = jnp.where(chosen, ca[m], va)
            vb = jnp.where(chosen, cb[m], vb)
        return va, vb

    def coefficients(groups):
        def one(z, carry):
            for g in groups:
                va, vb = lookup(ids[z, pl.ds(8 * g, 8), :])
                coef_a[z, pl.ds(8 * g, 8), :] = va
                coef_b[z, pl.ds(8 * g, 8), :] = vb
            return carry

        lax.fori_loop(0, NZ, one, 0)

    in_half = lax.rem(lane, CY // 2)

    def strips(groups):
        spots = (
            (0, 8, (lane >= 8) & (lane < 24)),
            (0, 48, (lane >= 32) & (lane < 48)),
            (1, 72, (lane >= 72) & (lane < 88)),
            (1, 112, (lane >= 96) & (lane < 112)),
        )

        def pack(j, values, i, rows, base):
            out = jnp.full((8, CY), base, f32)
            for half, shift, mask in spots:
                out = jnp.where(mask, pltpu.roll(values[half], shift, 1), out)
            before, after = from_l[i, rows, :], from_r[i, rows, :]
            out = jnp.where(in_half < 8, pltpu.roll(before, (CY - 8 * j) % CY, 1) if j else before, out)
            return jnp.where((in_half >= 48) & (in_half < 56), pltpu.roll(after, (CY + 48 - 8 * j) % CY, 1), out)

        for g in groups:
            rows = pl.ds(8 * g, 8)
            padded = pl.ds(PAD + 8 * g - HALO, 8)
            for j in range(HALF):
                for i in range(6 if g in OWN else 0):
                    source, target = ((e_in, se), (h_in, sh))[i // 3]
                    values = [source[i % 3, j + HALF * half, pl.ds(8 * g - HALO, 8), :] for half in range(2)]
                    target[i % 3, j, padded, :] = pack(j, values, i, rows, 0.0)
                values = [ids[j + HALF * half, rows, :].astype(f32) for half in range(2)]
                va, vb = lookup(pack(j, values, 6, rows, float(NMAT)))
                strip_a[j, rows, :] = va
                strip_b[j, rows, :] = vb

    def power(bit, carry):
        pr, pi, br, bi = carry
        take = lax.rem(lax.shift_right_logical(ix, bit), 2) == 1
        nr = pr * br - pi * bi
        ni = pr * bi + pi * br
        return (
            jnp.where(take, nr, pr),
            jnp.where(take, ni, pi),
            br * br - bi * bi,
            2.0 * br * bi,
        )

    coefficients(OWN)
    rows_at_once = 8
    for start in range(0, total, rows_at_once):
        part = pl.ds(start, rows_at_once)
        carry = (
            jnp.full((rows_at_once, CY), scale, jnp.float32),
            jnp.zeros((rows_at_once, CY), jnp.float32),
            block.at(0, start, rows_at_once),
            block.at(1, start, rows_at_once),
        )
        for bit in range(max(1, (nx - 1).bit_length())):
            carry = power(bit, carry)
        phase[part, :] = carry[0]
        phase[pl.ds(total + start, rows_at_once), :] = carry[1]
    start_phase = Rows(phase, (0, total))

    half_y = jnp.where((in_half < 8) & (iy == 0), 0.0, 0.5).astype(f32)
    on_face = [
        (row + 8 * g >= face[0]) & (row + 8 * g < face[1]) & (lane >= face[2]) & (lane < face[3])
        for g in range(2)
    ]

    def at(g, shift=0):
        return pl.ds(PAD + 8 * g + shift, 8)

    zero = jnp.zeros((8, CY), f32)
    low_half = lane < CY // 2

    def new_magnetic(e, h, z, groups, here, above, factor, source):
        out = {}
        for g in groups:
            ex, ey, ez = here[g]
            ex_z, ey_z = above[g]
            ey_x, ez_x = e[1, z, at(g, 1), :], e[2, z, at(g, 1), :]
            if source is not None and g != 1:
                more_y, more_z = source(g, z)
                ey_x, ez_x = ey_x + more_y, ez_x + more_z
            ex_y, ez_y = pltpu.roll(ex, CY - 1, 1), pltpu.roll(ez, CY - 1, 1)
            hx = h[0, z, at(g), :] - factor * ((ez_y - ez) - (ey_z - ey))
            hy = h[1, z, at(g), :] - factor * ((ex_z - ex) - (ez_x - ez))
            hz = h[2, z, at(g), :] - factor * ((ey_x - ey) - (ex_y - ex))
            h[0, z, at(g), :] = hx
            h[1, z, at(g), :] = hy
            h[2, z, at(g), :] = hz
            out[g] = (hx, hy, hz)
        return out

    def new_electric(e, h, a, b, z, groups, base, here, now, below, source):
        out = {}
        for g in groups:
            ex, ey, ez = here[g]
            hx, hy, hz = now[g]
            hx_z, hy_z = below[g]
            hy_x, hz_x = h[1, z, at(g, -1), :], h[2, z, at(g, -1), :]
            if source is not None and g != 1:
                more_y, more_z = source(g, z)
                hy_x, hz_x = hy_x + more_y, hz_x + more_z
            hx_y, hz_y = pltpu.roll(hx, 1, 1), pltpu.roll(hz, 1, 1)
            va, vb = a[z, pl.ds(base + 8 * g, 8), :], b[z, pl.ds(base + 8 * g, 8), :]
            ex = va * ex + vb * ((hz - hz_y) - (hy - hy_z))
            ey = va * ey + vb * ((hx - hx_z) - (hz - hz_x))
            ez = va * ez + vb * ((hy - hy_x) - (hx - hx_y))
            e[0, z, at(g), :] = ex
            e[1, z, at(g), :] = ey
            e[2, z, at(g), :] = ez
            out[g] = (ex, ey)
        return out

    def plane(e, z, groups):
        return {g: tuple(e[c, z, at(g), :] for c in range(3)) for g in groups}

    def two(values):
        return {g: v[:2] for g, v in values.items()}

    def advance(e, h, groups, base, source_e=None, source_h=None):
        here = plane(e, 0, groups)
        nothing = {g: (zero, zero) for g in groups}
        below = nothing
        for z in range(NZ):
            ahead = plane(e, z + 1, groups) if z < NZ - 1 else None
            above = two(ahead) if ahead else nothing
            now = new_magnetic(e, h, z, groups, here, above, 0.5, source_e)
            new_electric(e, h, coef_a, coef_b, z, groups, base, here, now, below, source_h)
            below, here = two(now), ahead

    def advance_strips(e, h, groups, base, source_e=None, source_h=None):
        here = first = plane(e, 0, groups)
        for j in range(HALF):
            if j < HALF - 1:
                ahead = plane(e, j + 1, groups)
                above = two(ahead)
            else:
                ahead = None
                above = {
                    g: tuple(jnp.where(low_half, pltpu.roll(v, CY // 2, 1), 0.0) for v in first[g][:2]) for g in groups
                }
            now = new_magnetic(e, h, j, groups, here, above, half_y, source_e)
            if j:
                new_electric(e, h, strip_a, strip_b, j, groups, base, here, now, below, source_h)
            else:
                start = now
            below, here = two(now), ahead
        below = {g: tuple(jnp.where(low_half, 0.0, pltpu.roll(v, CY // 2, 1)) for v in below[g]) for g in groups}
        new_electric(e, h, strip_a, strip_b, 0, groups, base, plane(e, 0, groups), start, below, source_h)

    def borders(n, e, h, mine_e, mine_h, run, k):
        depth = e.shape[1]
        for c in (1, 2):
            mine_e[n, pl.ds((c - 1) * depth, depth), :] = e[c, :, PAD, :]
        send_trace(n, k + 1)
        run(e, h, (0, 1), HALO)
        for c in (1, 2):
            mine_h[n, pl.ds((c - 1) * depth, depth), :] = h[c, :, PAD + CX - 1, :]
        send_trace(n, k)

    def keep(n, e, h, z, kept, first_row, add):
        for c, (field, part) in enumerate(((e, 0), (e, 1), (h, 0), (h, 1))):
            for k in range(2):
                spot = pl.ds(c * CX + 8 * k, 8)
                value = field[part, z, pl.ds(first_row + 8 * k, 8), :]
                kept[n, spot, :] = kept[n, spot, :] + value if add else value

    def alone(n, carry):
        borders(n, ef, hf, own_e, own_h, advance, 0)
        keep(n, ef, hf, ZF, samples, PAD, False)
        return carry

    def alone_strips(n, carry):
        borders(n, se, sh, strip_own_e, strip_own_h, advance_strips, 2)
        keep(n, se, sh, 0, strip_samples, PAD, False)
        return carry

    def sources(n, left, right, spot, depth):
        masks = {0: (row == spot) & has_xl, 2: row == spot}

        def source(g, z):
            buf = left if g == 0 else right
            return tuple(
                jnp.where(masks[g], jnp.broadcast_to(buf[n, pl.ds(c * depth + z, 1), :], (8, CY)), 0.0) for c in range(2)
            )

        return source

    SHIFT = HALO - GHOST

    def correct(groups, n, carry):
        await_trace(n, 0)
        await_trace(n, 1)
        advance(
            ce, ch, groups, SHIFT,
            sources(n, own_e, right_e, GHOST - 1, NZ), sources(n, left_h, own_h, GHOST, NZ),
        )
        keep(n, ce, ch, ZF, samples, PAD + GHOST, True)
        return carry

    def correct_strips(groups, n, carry):
        await_trace(n, 2)
        await_trace(n, 3)
        advance_strips(
            de, dh, groups, SHIFT,
            sources(n, strip_own_e, strip_right_e, GHOST - 1, HALF), sources(n, strip_left_h, strip_own_h, GHOST, HALF),
        )
        keep(n, de, dh, 0, strip_samples, PAD + GHOST, True)
        return carry

    lax.fori_loop(0, STEPS, alone, 0)
    begin_round(1)
    await_copies(y_copies)
    strips(OWN)
    lax.fori_loop(0, STEPS, alone_strips, 0)
    begin_round(2)
    await_copies(x_copies)
    await_copies(corner_copies)
    for z in range(NZ):
        spot = pl.ds(z * GHOST, GHOST)
        ids[z, pl.ds(HALO - GHOST, GHOST), :] = left_ids[spot, :]
        ids[z, pl.ds(HALO + CX, GHOST), :] = right_ids[spot, :]
    strips((0, 3))
    coefficients((0, 3))
    lax.fori_loop(0, STEPS // 2, functools.partial(correct, (0, 2)), 0)
    lax.fori_loop(STEPS // 2, STEPS, functools.partial(correct, (0, 1, 2)), 0)
    begin_round(3)
    lax.fori_loop(0, STEPS // 2, functools.partial(correct_strips, (0, 2)), 0)
    lax.fori_loop(STEPS // 2, STEPS, functools.partial(correct_strips, (0, 1, 2)), 0)

    for k in range(4, len(rounds)):
        begin_round(k)
    for n in range(STEPS):
        for c in range(4):
            for k in range(2):
                spot = pl.ds(c * CX + 8 * k, 8)
                end = strip_samples[n, spot, :]
                value = jnp.where(lane < 8, pltpu.roll(end, 56, 1), samples[n, spot, :])
                value = jnp.where(lane >= CY - 8, pltpu.roll(end, 16, 1), value)
                sample[pl.ds(n * 4 * CX + c * CX + 8 * k, 8), :] = jnp.where(on_face[k], value, 0.0)
    for part in range(2):
        turned[part] = jnp.dot(
            sample[...],
            table[pl.ds(starts[part], CY), :],
            precision=lax.Precision.HIGHEST,
            preferred_element_type=f32,
        )
    for first in range(0, 4 * CX, 8):
        re, im = zero, zero
        for n in range(STEPS):
            g_re, g_im = (turned[part, pl.ds(n * 4 * CX + first, 8), :] for part in range(2))
            ct, st = time.at(0, n, 1), time.at(1, n, 1)
            re += ct * g_re + st * g_im
            im += ct * g_im - st * g_re
        acc[0, pl.ds(first, 8), :] = re
        acc[1, pl.ds(first, 8), :] = im

    end_round(len(rounds) - 1)
    yr, yi = y_start.at(0, iy, 1), y_start.at(1, iy, 1)
    col_re = acc[0] * yr - acc[1] * yi
    acc[1] = acc[0] * yi + acc[1] * yr
    acc[0] = col_re
    for part in range(2):
        for x in range(CX):
            four = acc[part, pl.ds(x, 4, stride=CX), :]
            cols[part, x, pl.ds(0, 4), :] = four
            cols[part, x, pl.ds(4, 4), :] = four

    upper = lax.broadcasted_iota(jnp.int32, (8, CY), 0) < 4
    at_once = min(8, total)

    def send_far(k):
        other = lax.rem(me + k, total)
        return pltpu.make_async_remote_copy(
            src_ref=f_send.at[k],
            dst_ref=f_recv.at[k - 1],
            send_sem=f_send_sem,
            recv_sem=f_recv_sem,
            device_id=(lax.div(other, nx), lax.rem(other, nx)),
            device_id_type=MESH,
        )

    def project(trip, carry):
        k0 = trip * at_once
        picked = [bands[lax.rem(me + k0 + j, total)] for j in range(at_once)]

        def pair(rows, part, j):
            return jnp.where(upper, rows.at(part, picked[j], 1), rows.at(part, picked[j + 1], 1))

        pairs = range(0, at_once, 2)
        wr = [pair(cell, 0, j) for j in pairs]
        wi = [pair(cell, 1, j) for j in pairs]
        c_re, c_im = cols[0, CX - 1], cols[1, CX - 1]
        re = [c_re for _ in pairs]
        im = [c_im for _ in pairs]
        for x in range(CX - 2, -1, -1):
            c_re, c_im = cols[0, x], cols[1, x]
            re, im = (
                [r * a - i * b + c_re for r, i, a, b in zip(re, im, wr, wi)],
                [r * b + i * a + c_im for r, i, a, b in zip(re, im, wr, wi)],
            )
        for t, j in enumerate(pairs):
            pr, pi = pair(start_phase, 0, j), pair(start_phase, 1, j)
            far_re = re[t] * pr - im[t] * pi
            far_im = re[t] * pi + im[t] * pr
            f_send[k0 + j] = jnp.where(upper, far_re, pltpu.roll(far_im, 4, 0))
            f_send[k0 + j + 1] = jnp.where(upper, pltpu.roll(far_re, 4, 0), far_im)
        for j in range(at_once):
            @pl.when(k0 + j > 0)
            def _(j=j):
                send_far(k0 + j).start()
        return carry

    lax.fori_loop(0, total // at_once, project, 0)

    for field, strip, more, strip_more, out in ((ef, se, ce, de, e_out), (hf, sh, ch, dh, h_out)):
        for c in range(3):
            for z in range(NZ):
                half, j = z // HALF, z % HALF
                for g in range(2):
                    end = strip[c, j, at(g), :] + strip_more[c, j, at(g, GHOST), :]
                    value = field[c, z, at(g), :] + more[c, z, at(g, GHOST), :]
                    value = jnp.where(lane < 8, pltpu.roll(end, (CY - 64 * half - 8) % CY, 1), value)
                    value = jnp.where(lane >= CY - 8, pltpu.roll(end, 80 - 64 * half, 1), value)
                    out[c, z, pl.ds(8 * g, 8), :] = value

    pltpu.make_async_copy(f_recv, f_recv, f_recv_sem).wait()
    if total <= 64:
        terms = [f_send[0]] + [f_recv[k] for k in range(total - 1)]
        while len(terms) > 1:
            terms = [a + b for a, b in zip(terms[::2], terms[1::2])]
        far_out[...] = terms[0]
    else:
        far_out[...] = lax.fori_loop(0, total - 1, lambda k, t: t + f_recv[k], f_send[0])
    pltpu.make_async_copy(f_recv, f_recv, f_send_sem).wait()
    for i, (sends, _, src, dst, device) in enumerate(every):
        @pl.when(sends)
        def _(i=i, src=src, dst=dst, device=device):
            remote(i, src, dst, device).wait_send()

    def sent(n, carry):
        for k in range(4):
            @pl.when(traces[k][0])
            def _(k=k):
                trace(n, k).wait_send()
        return carry

    lax.fori_loop(0, STEPS, sent, 0)


def write_out(e, h, far, e_out, h_out, far_out, sem):
    copies = [
        pltpu.make_async_copy(src, dst, sem.at[i])
        for i, (src, dst) in enumerate(((e, e_out), (h, h_out), (far, far_out)))
    ]
    for copy in copies:
        copy.start()
    for copy in copies:
        copy.wait()


def local(ny, nx, electric, magnetic, material_ids, update_ca, update_cb, face_ranges, band_table):
    total = ny * nx
    bands = band_table.shape[0]
    assert bands == total and electric.shape == (3, NZ, CX, CY)
    scale = 1.0 / math.sqrt(CX * nx * CY * ny)
    f32 = jnp.float32
    vmem = pl.BlockSpec(memory_space=pltpu.VMEM)
    hbm = pl.BlockSpec(memory_space=pltpu.HBM)
    packed, starts = tables(bands, ny)
    e_out, h_out, far = pl.pallas_call(
        functools.partial(kernel, ny, nx, scale, starts),
        out_shape=(
            pltpu.VMEM(electric.shape, f32),
            pltpu.VMEM(electric.shape, f32),
            pltpu.VMEM((8, CY), f32),
        ),
        in_specs=[hbm] * 8,
        out_specs=(vmem,) * 3,
        scratch_shapes=[
            pltpu.VMEM((3, NZ, PITCH, CY), f32),
            pltpu.VMEM((3, NZ, PITCH, CY), f32),
            pltpu.VMEM((NZ, ROWS, CY), jnp.int32),
            pltpu.SMEM((NMAT,), f32),
            pltpu.SMEM((NMAT,), f32),
            pltpu.SMEM((4,), jnp.int32),
            pltpu.SMEM((bands,), jnp.int32),
            pltpu.VMEM(packed.shape, f32),
            pltpu.VMEM((3, NZ, CX, CY), f32),
            pltpu.VMEM((3, NZ, CX, CY), f32),
            pltpu.SemaphoreType.DMA((10,)),
            pltpu.VMEM((NZ, ROWS, CY), f32),
            pltpu.VMEM((NZ, ROWS, CY), f32),
            pltpu.VMEM((3, HALF, PITCH, CY), f32),
            pltpu.VMEM((3, HALF, PITCH, CY), f32),
            pltpu.VMEM((HALF, ROWS, CY), f32),
            pltpu.VMEM((HALF, ROWS, CY), f32),
            pltpu.VMEM((3, NZ, WIDE, CY), f32),
            pltpu.VMEM((3, NZ, WIDE, CY), f32),
            pltpu.VMEM((3, HALF, WIDE, CY), f32),
            pltpu.VMEM((3, HALF, WIDE, CY), f32),
            pltpu.VMEM((7, CX, CY), f32),
            pltpu.VMEM((7, CX, CY), f32),
            pltpu.VMEM((7, ROWS, CY), f32),
            pltpu.VMEM((7, ROWS, CY), f32),
            *[pltpu.VMEM((NZ * GHOST, CY), jnp.int32)] * 4,
            *[pltpu.VMEM((STEPS, 2 * NZ, CY), f32)] * 4,
            *[pltpu.VMEM((STEPS, 2 * HALF, CY), f32)] * 4,
            pltpu.VMEM((STEPS, 4 * CX, CY), f32),
            pltpu.VMEM((STEPS, 4 * CX, CY), f32),
            pltpu.VMEM((STEPS * 4 * CX, CY), f32),
            pltpu.VMEM((2, STEPS * 4 * CX, CY), f32),
            pltpu.VMEM((2, 4 * CX, CY), f32),
            pltpu.VMEM((2, CX, 8, CY), f32),
            pltpu.VMEM((2 * total, CY), f32),
            pltpu.VMEM((total, 8, CY), f32),
            pltpu.VMEM((total - 1, 8, CY), f32),
            pltpu.SemaphoreType.DMA((8,)),
            pltpu.SemaphoreType.DMA((8,)),
            pltpu.SemaphoreType.DMA((STEPS, 4)),
            pltpu.SemaphoreType.DMA((STEPS, 4)),
            pltpu.SemaphoreType.REGULAR((len(round_offsets(ny, nx)),)),
            pltpu.SemaphoreType.DMA,
            pltpu.SemaphoreType.DMA,
        ],
        compiler_params=pltpu.CompilerParams(
            collective_id=0, has_side_effects=True, vmem_limit_bytes=62 * 1024 * 1024
        ),
        name="fdtd",
    )(
        electric,
        magnetic,
        material_ids,
        update_ca,
        update_cb,
        face_ranges.reshape(4),
        band_table,
        packed,
    )
    e_out, h_out, far = pl.pallas_call(
        write_out,
        out_shape=tuple(jax.ShapeDtypeStruct(value.shape, f32) for value in (e_out, h_out, far)),
        in_specs=[vmem] * 3,
        out_specs=(hbm,) * 3,
        scratch_shapes=[pltpu.SemaphoreType.DMA((3,))],
        name="write_out",
    )(e_out, h_out, far)
    return e_out, h_out, far.reshape(1, 8, CY)


def solution(mesh):
    in_specs = (
        P(None, None, "inner", "grp"),
        P(None, None, "inner", "grp"),
        P(None, "inner", "grp"),
        P(),
        P(),
        P("inner", "grp", None),
        P(),
    )
    out_specs = (
        P(None, None, "inner", "grp"),
        P(None, None, "inner", "grp"),
        P(("grp", "inner"), None, None),
    )
    body = functools.partial(local, mesh.shape["grp"], mesh.shape["inner"])
    return jax.shard_map(body, mesh=mesh, in_specs=in_specs, out_specs=out_specs, check_vma=False)
```

```python
import functools
import math

import jax
import jax.numpy as jnp
import numpy as np
from jax import lax
from jax.experimental import pallas as pl
from jax.experimental.pallas import tpu as pltpu
from jax.sharding import PartitionSpec as P

STEPS = 8
FREQS = 32
ANG_BAND = 4
NMAT = 8
ZF = 8
NZ = 16
CX = 16
CY = 128
PAD = 8
HALO = 8
ROWS = CX + 2 * HALO
GHOST = 4
PITCH = CX + 2 * PAD
WIDE = CX + 2 * GHOST + 2 * PAD
OWN = (1, 2)
HALF = NZ // 2
MESH = pl.DeviceIdType.MESH


def tables(bands, groups):
    f = np.tile(np.arange(FREQS, dtype=np.int64) + 1, ANG_BAND)
    b = np.repeat(np.arange(ANG_BAND, dtype=np.int64) * 33 // ANG_BAND - 16, FREQS)
    a = np.arange(bands, dtype=np.int64) - bands // 2

    def both(turns, period):
        angle = (turns % period) * (2.0 * math.pi / period)
        return np.cos(angle).astype(np.float32), np.sin(angle).astype(np.float32)

    y = np.arange(CY, dtype=np.int64)[:, None]
    proj = np.concatenate(both(f * b * y, 4096), axis=1)
    time = np.stack(both(f * np.arange(STEPS, dtype=np.int64)[:, None], 128))
    y_start = np.stack(both(f * b * CY * np.arange(groups, dtype=np.int64)[:, None], 4096))
    cell = np.stack(both(f * a[:, None], 4096))
    block = np.stack(both(f * a[:, None] * CX, 4096))
    flat = [proj[:, :CY], proj[:, CY:]] + [part for table in (time, y_start, cell, block) for part in table]
    starts = np.cumsum([0] + [-(-part.shape[0] // 8) * 8 for part in flat])
    packed = np.zeros((starts[-1], CY), np.float32)
    for start, part in zip(starts, flat):
        packed[start : start + part.shape[0]] = part
    return packed, tuple(int(start) for start in starts[:-1])


def round_offsets(ny, nx):
    rounds, reach = [], 1
    while reach < max(ny, nx) - 1:
        rounds.append(
            [(0, s * reach) for s in (-1, 1) if reach < nx - 1] + [(s * reach, 0) for s in (-1, 1) if reach < ny - 1]
        )
        reach *= 2
    rounds.append([(s * d, 0) for d in range(1, ny) for s in (-1, 1)])
    return rounds


class Rows:
    def __init__(self, ref, starts):
        self.ref, self.starts = ref, starts

    def at(self, part, first, count):
        return self.ref[pl.ds(self.starts[part] + first, count), :]


def kernel(
    ny, nx, scale, starts,
    e_hbm, h_hbm, ids_hbm, ca_hbm, cb_hbm, face_hbm, bands_hbm, table_hbm,
    e_out, h_out, far_out,
    ef, hf, ids, ca, cb, face, bands, table, e_in, h_in, in_sem,
    coef_a, coef_b, se, sh, strip_a, strip_b, ce, ch, de, dh,
    edge_r, edge_l, from_l, from_r, last_ids, first_ids, left_ids, right_ids,
    own_h, own_e, left_h, right_e, strip_own_h, strip_own_e, strip_left_h, strip_right_e,
    samples, strip_samples, sample, turned, acc, cols, phase, f_send, f_recv,
    send_sem, recv_sem, trace_send, trace_recv, round_sem, f_send_sem, f_recv_sem,
):
    iy = lax.axis_index("grp")
    ix = lax.axis_index("inner")
    total = ny * nx
    me = iy * nx + ix
    f32 = jnp.float32
    lane = lax.broadcasted_iota(jnp.int32, (8, CY), 1)
    row = lax.broadcasted_iota(jnp.int32, (8, CY), 0)
    own_rows = pl.ds(PAD, CX)

    loads = [
        pltpu.make_async_copy(src, dst, in_sem.at[i])
        for i, (src, dst) in enumerate(
            (
                (e_hbm, ef.at[:, :, own_rows]),
                (h_hbm, hf.at[:, :, own_rows]),
                (ids_hbm, ids.at[:, pl.ds(HALO, CX)]),
                (ca_hbm, ca),
                (cb_hbm, cb),
                (face_hbm, face),
                (bands_hbm, bands),
                (table_hbm, table),
                (e_hbm, e_in),
                (h_hbm, h_in),
            )
        )
    ]
    for load in loads:
        load.start()
    time, y_start, cell, block = (Rows(table, starts[i : i + 2]) for i in (2, 4, 6, 8))

    barrier = pltpu.get_barrier_semaphore()

    has_xr, has_xl = ix < nx - 1, ix > 0
    has_yr, has_yl = iy < ny - 1, iy > 0

    def within(y, x):
        return (y >= 0) & (y < ny) & (x >= 0) & (x < nx)

    def signal_all(sem, offsets):
        for dy, dx in offsets:
            @pl.when(within(iy + dy, ix + dx))
            def _(dy=dy, dx=dx):
                pl.semaphore_signal(sem, inc=1, device_id=(iy + dy, ix + dx), device_id_type=MESH)

    def partners(offsets):
        return sum(jnp.where(within(iy + dy, ix + dx), 1, 0) for dy, dx in offsets)

    around = [(dy, dx) for dy in (-1, 0, 1) for dx in (-1, 0, 1) if (dy, dx) != (0, 0)]
    signal_all(barrier, around)
    rounds = round_offsets(ny, nx)

    def begin_round(k):
        if k > 0:
            end_round(k - 1)
        signal_all(round_sem.at[k], rounds[k])

    def end_round(k):
        pl.semaphore_wait(round_sem.at[k], partners(rounds[k]))

    low, high = pl.ds(0, 8), pl.ds(8, 8)
    every = (
        (has_yr, has_yl, edge_r, from_l.at[:, pl.ds(HALO, CX)], (iy + 1, ix)),
        (has_yl, has_yr, edge_l, from_r.at[:, pl.ds(HALO, CX)], (iy - 1, ix)),
        (has_yr & has_xr, has_yl & has_xl, edge_r.at[6, high], from_l.at[6, low], (iy + 1, ix + 1)),
        (has_yr & has_xl, has_yl & has_xr, edge_r.at[6, low], from_l.at[6, pl.ds(24, 8)], (iy + 1, ix - 1)),
        (has_yl & has_xr, has_yr & has_xl, edge_l.at[6, high], from_r.at[6, low], (iy - 1, ix + 1)),
        (has_yl & has_xl, has_yr & has_xr, edge_l.at[6, low], from_r.at[6, pl.ds(24, 8)], (iy - 1, ix - 1)),
        (has_xr, has_xl, last_ids, left_ids, (iy, ix + 1)),
        (has_xl, has_xr, first_ids, right_ids, (iy, ix - 1)),
    )
    traces = (
        (has_xr, has_xl, own_h, left_h, (iy, ix + 1)),
        (has_xl, has_xr, own_e, right_e, (iy, ix - 1)),
        (has_xr, has_xl, strip_own_h, strip_left_h, (iy, ix + 1)),
        (has_xl, has_xr, strip_own_e, strip_right_e, (iy, ix - 1)),
    )

    def trace(n, k):
        _, _, src, dst, device = traces[k]
        return pltpu.make_async_remote_copy(
            src_ref=src.at[n],
            dst_ref=dst.at[n],
            send_sem=trace_send.at[n, k],
            recv_sem=trace_recv.at[n, k],
            device_id=device,
            device_id_type=MESH,
        )

    def send_trace(n, k):
        @pl.when(traces[k][0])
        def _():
            trace(n, k).start()

    def await_trace(n, k):
        @pl.when(traces[k][1])
        def _():
            trace(n, k).wait_recv()

    def remote(i, src, dst, device):
        return pltpu.make_async_remote_copy(
            src_ref=src,
            dst_ref=dst,
            send_sem=send_sem.at[i],
            recv_sem=recv_sem.at[i],
            device_id=device,
            device_id_type=MESH,
        )

    def start_copies(which):
        for i in which:
            sends, _, src, dst, device = every[i]

            @pl.when(sends)
            def _(i=i, src=src, dst=dst, device=device):
                remote(i, src, dst, device).start()

    def await_copies(which):
        for i in which:
            _, receives, src, dst, _ = every[i]

            @pl.when(receives)
            def _(i=i, src=src, dst=dst):
                remote(i, src, dst, (iy, ix)).wait_recv()

    y_copies, corner_copies, x_copies = range(2), range(2, 6), range(6, 8)

    for given, fresh, arrived in ((has_xl, left_ids, (left_h, strip_left_h)), (has_xr, right_ids, (right_e, strip_right_e))):
        @pl.when(jnp.logical_not(given))
        def _(fresh=fresh, arrived=arrived):
            for buf in arrived:
                buf[...] = jnp.zeros(buf.shape, f32)
            fresh[...] = jnp.full(fresh.shape, NMAT, jnp.int32)

    for edge, side in ((from_l, has_yl), (from_r, has_yr)):
        @pl.when(jnp.logical_not(side))
        def _(edge=edge):
            edge[pl.ds(0, 6), pl.ds(HALO, CX), :] = jnp.zeros((6, CX, CY), f32)

        for given, rows, count in ((side, 8, 16), (side & has_xl, 0, 8), (side & has_xr, 24, 8)):
            @pl.when(jnp.logical_not(given))
            def _(edge=edge, rows=rows, count=count):
                edge[6, pl.ds(rows, count), :] = jnp.full((count, CY), float(NMAT), f32)

    for fields in ((ef, hf), (se, sh)):
        for field in fields:
            for c in range(3):
                for z in range(field.shape[1]):
                    for rows in (0, PAD + CX):
                        field[c, z, pl.ds(rows, PAD), :] = jnp.zeros((PAD, CY), f32)
    ids[:, pl.ds(0, 8), :] = jnp.full((NZ, 8, CY), NMAT, jnp.int32)
    ids[:, pl.ds(HALO + CX, 8), :] = jnp.full((NZ, 8, CY), NMAT, jnp.int32)
    for field in (ce, ch, de, dh):
        field[...] = jnp.zeros(field.shape, f32)

    pl.semaphore_wait(barrier, partners(around))
    begin_round(0)
    for load in loads:
        load.wait()

    for z in range(NZ):
        spot = pl.ds(z * GHOST, GHOST)
        last_ids[spot, :] = ids[z, pl.ds(HALO + CX - GHOST, GHOST), :]
        first_ids[spot, :] = ids[z, pl.ds(HALO, GHOST), :]
    start_copies(x_copies)
    for i in range(7):
        for g in range(2):
            right = jnp.zeros((8, CY), f32)
            left = jnp.zeros((8, CY), f32)
            for z in range(NZ):
                rows = pl.ds(8 * g + PAD, 8)
                if i < 6:
                    value = (ef, hf)[i // 3][i % 3, z, rows, :]
                else:
                    value = ids[z, pl.ds(8 * g + HALO, 8), :].astype(f32)
                here = (lane >= 8 * z) & (lane < 8 * z + 8)
                right = jnp.where(here, pltpu.roll(value, (8 * z - 120) % CY, 1) if z < 15 else value, right)
                left = jnp.where(here, pltpu.roll(value, 8 * z, 1) if z else value, left)
            edge_r[i, pl.ds(8 * g, 8), :] = right
            edge_l[i, pl.ds(8 * g, 8), :] = left
    start_copies(y_copies)
    start_copies(corner_copies)

    def lookup(here):
        va = jnp.zeros((8, CY), f32)
        vb = jnp.zeros((8, CY), f32)
        for m in range(NMAT):
            chosen = here == m
            va = jnp.where(chosen, ca[m], va)
            vb = jnp.where(chosen, cb[m], vb)
        return va, vb

    def coefficients(groups):
        def one(z, carry):
            for g in groups:
                va, vb = lookup(ids[z, pl.ds(8 * g, 8), :])
                coef_a[z, pl.ds(8 * g, 8), :] = va
                coef_b[z, pl.ds(8 * g, 8), :] = vb
            return carry

        lax.fori_loop(0, NZ, one, 0)

    in_half = lax.rem(lane, CY // 2)

    def strips(groups):
        spots = (
            (0, 8, (lane >= 8) & (lane < 24)),
            (0, 48, (lane >= 32) & (lane < 48)),
            (1, 72, (lane >= 72) & (lane < 88)),
            (1, 112, (lane >= 96) & (lane < 112)),
        )

        def pack(j, values, i, rows, base):
            out = jnp.full((8, CY), base, f32)
            for half, shift, mask in spots:
                out = jnp.where(mask, pltpu.roll(values[half], shift, 1), out)
            before, after = from_l[i, rows, :], from_r[i, rows, :]
            out = jnp.where(in_half < 8, pltpu.roll(before, (CY - 8 * j) % CY, 1) if j else before, out)
            return jnp.where((in_half >= 48) & (in_half < 56), pltpu.roll(after, (CY + 48 - 8 * j) % CY, 1), out)

        for g in groups:
            rows = pl.ds(8 * g, 8)
            padded = pl.ds(PAD + 8 * g - HALO, 8)
            for j in range(HALF):
                for i in range(6 if g in OWN else 0):
                    source, target = ((e_in, se), (h_in, sh))[i // 3]
                    values = [source[i % 3, j + HALF * half, pl.ds(8 * g - HALO, 8), :] for half in range(2)]
                    target[i % 3, j, padded, :] = pack(j, values, i, rows, 0.0)
                values = [ids[j + HALF * half, rows, :].astype(f32) for half in range(2)]
                va, vb = lookup(pack(j, values, 6, rows, float(NMAT)))
                strip_a[j, rows, :] = va
                strip_b[j, rows, :] = vb

    def power(bit, carry):
        pr, pi, br, bi = carry
        take = lax.rem(lax.shift_right_logical(ix, bit), 2) == 1
        nr = pr * br - pi * bi
        ni = pr * bi + pi * br
        return (
            jnp.where(take, nr, pr),
            jnp.where(take, ni, pi),
            br * br - bi * bi,
            2.0 * br * bi,
        )

    coefficients(OWN)
    rows_at_once = 8
    for start in range(0, total, rows_at_once):
        part = pl.ds(start, rows_at_once)
        carry = (
            jnp.full((rows_at_once, CY), scale, jnp.float32),
            jnp.zeros((rows_at_once, CY), jnp.float32),
            block.at(0, start, rows_at_once),
            block.at(1, start, rows_at_once),
        )
        for bit in range(max(1, (nx - 1).bit_length())):
            carry = power(bit, carry)
        phase[part, :] = carry[0]
        phase[pl.ds(total + start, rows_at_once), :] = carry[1]
    start_phase = Rows(phase, (0, total))

    half_y = jnp.where((in_half < 8) & (iy == 0), 0.0, 0.5).astype(f32)
    on_face = [
        (row + 8 * g >= face[0]) & (row + 8 * g < face[1]) & (lane >= face[2]) & (lane < face[3])
        for g in range(2)
    ]

    def at(g, shift=0):
        return pl.ds(PAD + 8 * g + shift, 8)

    zero = jnp.zeros((8, CY), f32)
    low_half = lane < CY // 2

    def new_magnetic(e, h, z, groups, here, above, factor, source):
        out = {}
        for g in groups:
            ex, ey, ez = here[g]
            ex_z, ey_z = above[g]
            ey_x, ez_x = e[1, z, at(g, 1), :], e[2, z, at(g, 1), :]
            if source is not None and g != 1:
                more_y, more_z = source(g, z)
                ey_x, ez_x = ey_x + more_y, ez_x + more_z
            ex_y, ez_y = pltpu.roll(ex, CY - 1, 1), pltpu.roll(ez, CY - 1, 1)
            hx = h[0, z, at(g), :] - factor * ((ez_y - ez) - (ey_z - ey))
            hy = h[1, z, at(g), :] - factor * ((ex_z - ex) - (ez_x - ez))
            hz = h[2, z, at(g), :] - factor * ((ey_x - ey) - (ex_y - ex))
            h[0, z, at(g), :] = hx
            h[1, z, at(g), :] = hy
            h[2, z, at(g), :] = hz
            out[g] = (hx, hy, hz)
        return out

    def new_electric(e, h, a, b, z, groups, base, here, now, below, source):
        out = {}
        for g in groups:
            ex, ey, ez = here[g]
            hx, hy, hz = now[g]
            hx_z, hy_z = below[g]
            hy_x, hz_x = h[1, z, at(g, -1), :], h[2, z, at(g, -1), :]
            if source is not None and g != 1:
                more_y, more_z = source(g, z)
                hy_x, hz_x = hy_x + more_y, hz_x + more_z
            hx_y, hz_y = pltpu.roll(hx, 1, 1), pltpu.roll(hz, 1, 1)
            va, vb = a[z, pl.ds(base + 8 * g, 8), :], b[z, pl.ds(base + 8 * g, 8), :]
            ex = va * ex + vb * ((hz - hz_y) - (hy - hy_z))
            ey = va * ey + vb * ((hx - hx_z) - (hz - hz_x))
            ez = va * ez + vb * ((hy - hy_x) - (hx - hx_y))
            e[0, z, at(g), :] = ex
            e[1, z, at(g), :] = ey
            e[2, z, at(g), :] = ez
            out[g] = (ex, ey)
        return out

    def plane(e, z, groups):
        return {g: tuple(e[c, z, at(g), :] for c in range(3)) for g in groups}

    def two(values):
        return {g: v[:2] for g, v in values.items()}

    def advance(e, h, groups, base, source_e=None, source_h=None):
        here = plane(e, 0, groups)
        nothing = {g: (zero, zero) for g in groups}
        below = nothing
        for z in range(NZ):
            ahead = plane(e, z + 1, groups) if z < NZ - 1 else None
            above = two(ahead) if ahead else nothing
            now = new_magnetic(e, h, z, groups, here, above, 0.5, source_e)
            new_electric(e, h, coef_a, coef_b, z, groups, base, here, now, below, source_h)
            below, here = two(now), ahead

    def advance_strips(e, h, groups, base, source_e=None, source_h=None):
        here = first = plane(e, 0, groups)
        for j in range(HALF):
            if j < HALF - 1:
                ahead = plane(e, j + 1, groups)
                above = two(ahead)
            else:
                ahead = None
                above = {
                    g: tuple(jnp.where(low_half, pltpu.roll(v, CY // 2, 1), 0.0) for v in first[g][:2]) for g in groups
                }
            now = new_magnetic(e, h, j, groups, here, above, half_y, source_e)
            if j:
                new_electric(e, h, strip_a, strip_b, j, groups, base, here, now, below, source_h)
            else:
                start = now
            below, here = two(now), ahead
        below = {g: tuple(jnp.where(low_half, 0.0, pltpu.roll(v, CY // 2, 1)) for v in below[g]) for g in groups}
        new_electric(e, h, strip_a, strip_b, 0, groups, base, plane(e, 0, groups), start, below, source_h)

    def borders(n, e, h, mine_e, mine_h, run, k):
        depth = e.shape[1]
        for c in (1, 2):
            mine_e[n, pl.ds((c - 1) * depth, depth), :] = e[c, :, PAD, :]
        send_trace(n, k + 1)
        run(e, h, (0, 1), HALO)
        for c in (1, 2):
            mine_h[n, pl.ds((c - 1) * depth, depth), :] = h[c, :, PAD + CX - 1, :]
        send_trace(n, k)

    def keep(n, e, h, z, kept, first_row, add):
        for c, (field, part) in enumerate(((e, 0), (e, 1), (h, 0), (h, 1))):
            for k in range(2):
                spot = pl.ds(c * CX + 8 * k, 8)
                value = field[part, z, pl.ds(first_row + 8 * k, 8), :]
                kept[n, spot, :] = kept[n, spot, :] + value if add else value

    def alone(n, carry):
        borders(n, ef, hf, own_e, own_h, advance, 0)
        keep(n, ef, hf, ZF, samples, PAD, False)
        return carry

    def alone_strips(n, carry):
        borders(n, se, sh, strip_own_e, strip_own_h, advance_strips, 2)
        keep(n, se, sh, 0, strip_samples, PAD, False)
        return carry

    def sources(n, left, right, spot, depth):
        masks = {0: (row == spot) & has_xl, 2: row == spot}

        def source(g, z):
            buf = left if g == 0 else right
            return tuple(
                jnp.where(masks[g], jnp.broadcast_to(buf[n, pl.ds(c * depth + z, 1), :], (8, CY)), 0.0) for c in range(2)
            )

        return source

    SHIFT = HALO - GHOST

    def correct(groups, n, carry):
        await_trace(n, 0)
        await_trace(n, 1)
        advance(
            ce, ch, groups, SHIFT,
            sources(n, own_e, right_e, GHOST - 1, NZ), sources(n, left_h, own_h, GHOST, NZ),
        )
        keep(n, ce, ch, ZF, samples, PAD + GHOST, True)
        return carry

    def correct_strips(groups, n, carry):
        await_trace(n, 2)
        await_trace(n, 3)
        advance_strips(
            de, dh, groups, SHIFT,
            sources(n, strip_own_e, strip_right_e, GHOST - 1, HALF), sources(n, strip_left_h, strip_own_h, GHOST, HALF),
        )
        keep(n, de, dh, 0, strip_samples, PAD + GHOST, True)
        return carry

    lax.fori_loop(0, STEPS, alone, 0)
    begin_round(1)
    await_copies(y_copies)
    strips(OWN)
    lax.fori_loop(0, STEPS, alone_strips, 0)
    begin_round(2)
    await_copies(x_copies)
    await_copies(corner_copies)
    for z in range(NZ):
        spot = pl.ds(z * GHOST, GHOST)
        ids[z, pl.ds(HALO - GHOST, GHOST), :] = left_ids[spot, :]
        ids[z, pl.ds(HALO + CX, GHOST), :] = right_ids[spot, :]
    strips((0, 3))
    coefficients((0, 3))
    lax.fori_loop(0, STEPS // 2, functools.partial(correct, (0, 2)), 0)
    lax.fori_loop(STEPS // 2, STEPS, functools.partial(correct, (0, 1, 2)), 0)
    begin_round(3)
    lax.fori_loop(0, STEPS // 2, functools.partial(correct_strips, (0, 2)), 0)
    lax.fori_loop(STEPS // 2, STEPS, functools.partial(correct_strips, (0, 1, 2)), 0)

    for k in range(4, len(rounds)):
        begin_round(k)
    for n in range(STEPS):
        for c in range(4):
            for k in range(2):
                spot = pl.ds(c * CX + 8 * k, 8)
                end = strip_samples[n, spot, :]
                value = jnp.where(lane < 8, pltpu.roll(end, 56, 1), samples[n, spot, :])
                value = jnp.where(lane >= CY - 8, pltpu.roll(end, 16, 1), value)
                sample[pl.ds(n * 4 * CX + c * CX + 8 * k, 8), :] = jnp.where(on_face[k], value, 0.0)
    for part in range(2):
        turned[part] = jnp.dot(
            sample[...],
            table[pl.ds(starts[part], CY), :],
            precision=lax.Precision.HIGHEST,
            preferred_element_type=f32,
        )
    for first in range(0, 4 * CX, 8):
        re, im = zero, zero
        for n in range(STEPS):
            g_re, g_im = (turned[part, pl.ds(n * 4 * CX + first, 8), :] for part in range(2))
            ct, st = time.at(0, n, 1), time.at(1, n, 1)
            re += ct * g_re + st * g_im
            im += ct * g_im - st * g_re
        acc[0, pl.ds(first, 8), :] = re
        acc[1, pl.ds(first, 8), :] = im

    end_round(len(rounds) - 1)
    yr, yi = y_start.at(0, iy, 1), y_start.at(1, iy, 1)
    col_re = acc[0] * yr - acc[1] * yi
    acc[1] = acc[0] * yi + acc[1] * yr
    acc[0] = col_re
    for part in range(2):
        for x in range(CX):
            four = acc[part, pl.ds(x, 4, stride=CX), :]
            cols[part, x, pl.ds(0, 4), :] = four
            cols[part, x, pl.ds(4, 4), :] = four

    upper = lax.broadcasted_iota(jnp.int32, (8, CY), 0) < 4
    at_once = min(8, total)

    def send_far(k):
        other = lax.rem(me + k, total)
        return pltpu.make_async_remote_copy(
            src_ref=f_send.at[k],
            dst_ref=f_recv.at[k - 1],
            send_sem=f_send_sem,
            recv_sem=f_recv_sem,
            device_id=(lax.div(other, nx), lax.rem(other, nx)),
            device_id_type=MESH,
        )

    def project(trip, carry):
        k0 = trip * at_once
        picked = [bands[lax.rem(me + k0 + j, total)] for j in range(at_once)]

        def pair(rows, part, j):
            return jnp.where(upper, rows.at(part, picked[j], 1), rows.at(part, picked[j + 1], 1))

        pairs = range(0, at_once, 2)
        wr = [pair(cell, 0, j) for j in pairs]
        wi = [pair(cell, 1, j) for j in pairs]
        c_re, c_im = cols[0, CX - 1], cols[1, CX - 1]
        re = [c_re for _ in pairs]
        im = [c_im for _ in pairs]
        for x in range(CX - 2, -1, -1):
            c_re, c_im = cols[0, x], cols[1, x]
            re, im = (
                [r * a - i * b + c_re for r, i, a, b in zip(re, im, wr, wi)],
                [r * b + i * a + c_im for r, i, a, b in zip(re, im, wr, wi)],
            )
        for t, j in enumerate(pairs):
            pr, pi = pair(start_phase, 0, j), pair(start_phase, 1, j)
            far_re = re[t] * pr - im[t] * pi
            far_im = re[t] * pi + im[t] * pr
            f_send[k0 + j] = jnp.where(upper, far_re, pltpu.roll(far_im, 4, 0))
            f_send[k0 + j + 1] = jnp.where(upper, pltpu.roll(far_re, 4, 0), far_im)
        for j in range(at_once):
            @pl.when(k0 + j > 0)
            def _(j=j):
                send_far(k0 + j).start()
        return carry

    lax.fori_loop(0, total // at_once, project, 0)

    for field, strip, more, strip_more, out in ((ef, se, ce, de, e_out), (hf, sh, ch, dh, h_out)):
        for c in range(3):
            for z in range(NZ):
                half, j = z // HALF, z % HALF
                for g in range(2):
                    end = strip[c, j, at(g), :] + strip_more[c, j, at(g, GHOST), :]
                    value = field[c, z, at(g), :] + more[c, z, at(g, GHOST), :]
                    value = jnp.where(lane < 8, pltpu.roll(end, (CY - 64 * half - 8) % CY, 1), value)
                    value = jnp.where(lane >= CY - 8, pltpu.roll(end, 80 - 64 * half, 1), value)
                    out[c, z, pl.ds(8 * g, 8), :] = value

    pltpu.make_async_copy(f_recv, f_recv, f_recv_sem).wait()
    if total <= 64:
        terms = [f_send[0]] + [f_recv[k] for k in range(total - 1)]
        while len(terms) > 1:
            terms = [a + b for a, b in zip(terms[::2], terms[1::2])]
        far_out[...] = terms[0]
    else:
        far_out[...] = lax.fori_loop(0, total - 1, lambda k, t: t + f_recv[k], f_send[0])
    pltpu.make_async_copy(f_recv, f_recv, f_send_sem).wait()
    for i, (sends, _, src, dst, device) in enumerate(every):
        @pl.when(sends)
        def _(i=i, src=src, dst=dst, device=device):
            remote(i, src, dst, device).wait_send()

    def sent(n, carry):
        for k in range(4):
            @pl.when(traces[k][0])
            def _(k=k):
                trace(n, k).wait_send()
        return carry

    lax.fori_loop(0, STEPS, sent, 0)


def write_out(e, h, far, e_out, h_out, far_out, sem):
    copies = [
        pltpu.make_async_copy(src, dst, sem.at[i])
        for i, (src, dst) in enumerate(((e, e_out), (h, h_out), (far, far_out)))
    ]
    for copy in copies:
        copy.start()
    for copy in copies:
        copy.wait()


def local(ny, nx, electric, magnetic, material_ids, update_ca, update_cb, face_ranges, band_table):
    total = ny * nx
    bands = band_table.shape[0]
    assert bands == total and electric.shape == (3, NZ, CX, CY)
    scale = 1.0 / math.sqrt(CX * nx * CY * ny)
    f32 = jnp.float32
    vmem = pl.BlockSpec(memory_space=pltpu.VMEM)
    hbm = pl.BlockSpec(memory_space=pltpu.HBM)
    packed, starts = tables(bands, ny)
    e_out, h_out, far = pl.pallas_call(
        functools.partial(kernel, ny, nx, scale, starts),
        out_shape=(
            pltpu.VMEM(electric.shape, f32),
            pltpu.VMEM(electric.shape, f32),
            pltpu.VMEM((8, CY), f32),
        ),
        in_specs=[hbm] * 8,
        out_specs=(vmem,) * 3,
        scratch_shapes=[
            pltpu.VMEM((3, NZ, PITCH, CY), f32),
            pltpu.VMEM((3, NZ, PITCH, CY), f32),
            pltpu.VMEM((NZ, ROWS, CY), jnp.int32),
            pltpu.SMEM((NMAT,), f32),
            pltpu.SMEM((NMAT,), f32),
            pltpu.SMEM((4,), jnp.int32),
            pltpu.SMEM((bands,), jnp.int32),
            pltpu.VMEM(packed.shape, f32),
            pltpu.VMEM((3, NZ, CX, CY), f32),
            pltpu.VMEM((3, NZ, CX, CY), f32),
            pltpu.SemaphoreType.DMA((10,)),
            pltpu.VMEM((NZ, ROWS, CY), f32),
            pltpu.VMEM((NZ, ROWS, CY), f32),
            pltpu.VMEM((3, HALF, PITCH, CY), f32),
            pltpu.VMEM((3, HALF, PITCH, CY), f32),
            pltpu.VMEM((HALF, ROWS, CY), f32),
            pltpu.VMEM((HALF, ROWS, CY), f32),
            pltpu.VMEM((3, NZ, WIDE, CY), f32),
            pltpu.VMEM((3, NZ, WIDE, CY), f32),
            pltpu.VMEM((3, HALF, WIDE, CY), f32),
            pltpu.VMEM((3, HALF, WIDE, CY), f32),
            pltpu.VMEM((7, CX, CY), f32),
            pltpu.VMEM((7, CX, CY), f32),
            pltpu.VMEM((7, ROWS, CY), f32),
            pltpu.VMEM((7, ROWS, CY), f32),
            *[pltpu.VMEM((NZ * GHOST, CY), jnp.int32)] * 4,
            *[pltpu.VMEM((STEPS, 2 * NZ, CY), f32)] * 4,
            *[pltpu.VMEM((STEPS, 2 * HALF, CY), f32)] * 4,
            pltpu.VMEM((STEPS, 4 * CX, CY), f32),
            pltpu.VMEM((STEPS, 4 * CX, CY), f32),
            pltpu.VMEM((STEPS * 4 * CX, CY), f32),
            pltpu.VMEM((2, STEPS * 4 * CX, CY), f32),
            pltpu.VMEM((2, 4 * CX, CY), f32),
            pltpu.VMEM((2, CX, 8, CY), f32),
            pltpu.VMEM((2 * total, CY), f32),
            pltpu.VMEM((total, 8, CY), f32),
            pltpu.VMEM((total - 1, 8, CY), f32),
            pltpu.SemaphoreType.DMA((8,)),
            pltpu.SemaphoreType.DMA((8,)),
            pltpu.SemaphoreType.DMA((STEPS, 4)),
            pltpu.SemaphoreType.DMA((STEPS, 4)),
            pltpu.SemaphoreType.REGULAR((len(round_offsets(ny, nx)),)),
            pltpu.SemaphoreType.DMA,
            pltpu.SemaphoreType.DMA,
        ],
        compiler_params=pltpu.CompilerParams(
            collective_id=0, has_side_effects=True, vmem_limit_bytes=62 * 1024 * 1024
        ),
        name="fdtd",
    )(
        electric,
        magnetic,
        material_ids,
        update_ca,
        update_cb,
        face_ranges.reshape(4),
        band_table,
        packed,
    )
    e_out, h_out, far = pl.pallas_call(
        write_out,
        out_shape=tuple(jax.ShapeDtypeStruct(value.shape, f32) for value in (e_out, h_out, far)),
        in_specs=[vmem] * 3,
        out_specs=(hbm,) * 3,
        scratch_shapes=[pltpu.SemaphoreType.DMA((3,))],
        name="write_out",
    )(*(pltpu.with_memory_space_constraint(value, pltpu.VMEM) for value in (e_out, h_out, far)))
    return e_out, h_out, far.reshape(1, 8, CY)


def solution(mesh):
    in_specs = (
        P(None, None, "inner", "grp"),
        P(None, None, "inner", "grp"),
        P(None, "inner", "grp"),
        P(),
        P(),
        P("inner", "grp", None),
        P(),
    )
    out_specs = (
        P(None, None, "inner", "grp"),
        P(None, None, "inner", "grp"),
        P(("grp", "inner"), None, None),
    )
    body = functools.partial(local, mesh.shape["grp"], mesh.shape["inner"])
    return jax.shard_map(body, mesh=mesh, in_specs=in_specs, out_specs=out_specs, check_vma=False)
```

```python
import functools
import math

import jax
import jax.numpy as jnp
import numpy as np
from jax import lax
from jax.experimental import pallas as pl
from jax.experimental.pallas import tpu as pltpu
from jax.sharding import PartitionSpec as P

STEPS = 8
FREQS = 32
ANG_BAND = 4
NMAT = 8
ZF = 8
NZ = 16
CX = 16
CY = 128
PAD = 8
HALO = 8
ROWS = CX + 2 * HALO
GHOST = 4
EARLY = 2
PITCH = CX + 2 * PAD
WIDE = CX + 2 * GHOST + 2 * PAD
OWN = (1, 2)
HALF = NZ // 2
MESH = pl.DeviceIdType.MESH


def tables(bands, groups):
    f = np.tile(np.arange(FREQS, dtype=np.int64) + 1, ANG_BAND)
    b = np.repeat(np.arange(ANG_BAND, dtype=np.int64) * 33 // ANG_BAND - 16, FREQS)
    a = np.arange(bands, dtype=np.int64) - bands // 2

    def both(turns, period):
        angle = (turns % period) * (2.0 * math.pi / period)
        return np.cos(angle).astype(np.float32), np.sin(angle).astype(np.float32)

    y = np.arange(CY, dtype=np.int64)[:, None]
    proj = np.concatenate(both(f * b * y, 4096), axis=1)
    time = np.stack(both(f * np.arange(STEPS, dtype=np.int64)[:, None], 128))
    y_start = np.stack(both(f * b * CY * np.arange(groups, dtype=np.int64)[:, None], 4096))
    cell = np.stack(both(f * a[:, None], 4096))
    block = np.stack(both(f * a[:, None] * CX, 4096))
    flat = [proj[:, :CY], proj[:, CY:]] + [part for table in (time, y_start, cell, block) for part in table]
    starts = np.cumsum([0] + [-(-part.shape[0] // 8) * 8 for part in flat])
    packed = np.zeros((starts[-1], CY), np.float32)
    for start, part in zip(starts, flat):
        packed[start : start + part.shape[0]] = part
    return packed, tuple(int(start) for start in starts[:-1])


def round_offsets(ny, nx):
    rounds, reach = [], 1
    while reach < max(ny, nx) - 1:
        rounds.append(
            [(0, s * reach) for s in (-1, 1) if reach < nx - 1] + [(s * reach, 0) for s in (-1, 1) if reach < ny - 1]
        )
        reach *= 2
    rounds.append([(s * d, 0) for d in range(1, ny) for s in (-1, 1)])
    return rounds


class Rows:
    def __init__(self, ref, starts):
        self.ref, self.starts = ref, starts

    def at(self, part, first, count):
        return self.ref[pl.ds(self.starts[part] + first, count), :]


def kernel(
    ny, nx, scale, starts,
    e_hbm, h_hbm, ids_hbm, ca_hbm, cb_hbm, face_hbm, bands_hbm, table_hbm,
    e_out, h_out, far_out,
    ef, hf, ids, ca, cb, face, bands, table, e_in, h_in, in_sem,
    coef_a, coef_b, se, sh, strip_a, strip_b, ce, ch, de, dh,
    edge_r, edge_l, from_l, from_r, last_ids, first_ids, left_ids, right_ids,
    own_h, own_e, left_h, right_e, strip_own_h, strip_own_e, strip_left_h, strip_right_e,
    late_own_h, late_own_e, late_left_h, late_right_e,
    samples, strip_samples, sample, turned, acc, cols, phase, f_send, f_recv,
    send_sem, recv_sem, trace_send, trace_recv, round_sem, f_send_sem, f_recv_sem,
):
    iy = lax.axis_index("grp")
    ix = lax.axis_index("inner")
    total = ny * nx
    me = iy * nx + ix
    f32 = jnp.float32
    lane = lax.broadcasted_iota(jnp.int32, (8, CY), 1)
    row = lax.broadcasted_iota(jnp.int32, (8, CY), 0)
    own_rows = pl.ds(PAD, CX)

    loads = [
        pltpu.make_async_copy(src, dst, in_sem.at[i])
        for i, (src, dst) in enumerate(
            (
                (e_hbm, ef.at[:, :, own_rows]),
                (h_hbm, hf.at[:, :, own_rows]),
                (ids_hbm, ids.at[:, pl.ds(HALO, CX)]),
                (ca_hbm, ca),
                (cb_hbm, cb),
                (face_hbm, face),
                (bands_hbm, bands),
                (table_hbm, table),
                (e_hbm, e_in),
                (h_hbm, h_in),
            )
        )
    ]
    for load in loads:
        load.start()
    time, y_start, cell, block = (Rows(table, starts[i : i + 2]) for i in (2, 4, 6, 8))

    barrier = pltpu.get_barrier_semaphore()

    has_xr, has_xl = ix < nx - 1, ix > 0
    has_yr, has_yl = iy < ny - 1, iy > 0

    def within(y, x):
        return (y >= 0) & (y < ny) & (x >= 0) & (x < nx)

    def signal_all(sem, offsets):
        for dy, dx in offsets:
            @pl.when(within(iy + dy, ix + dx))
            def _(dy=dy, dx=dx):
                pl.semaphore_signal(sem, inc=1, device_id=(iy + dy, ix + dx), device_id_type=MESH)

    def partners(offsets):
        return sum(jnp.where(within(iy + dy, ix + dx), 1, 0) for dy, dx in offsets)

    around = [(dy, dx) for dy in (-1, 0, 1) for dx in (-1, 0, 1) if (dy, dx) != (0, 0)]
    signal_all(barrier, around)
    rounds = round_offsets(ny, nx)

    def begin_round(k):
        if k > 0:
            end_round(k - 1)
        signal_all(round_sem.at[k], rounds[k])

    def end_round(k):
        pl.semaphore_wait(round_sem.at[k], partners(rounds[k]))

    low, high = pl.ds(0, 8), pl.ds(8, 8)
    every = (
        (has_yr, has_yl, edge_r, from_l.at[:, pl.ds(HALO, CX)], (iy + 1, ix)),
        (has_yl, has_yr, edge_l, from_r.at[:, pl.ds(HALO, CX)], (iy - 1, ix)),
        (has_yr & has_xr, has_yl & has_xl, edge_r.at[6, high], from_l.at[6, low], (iy + 1, ix + 1)),
        (has_yr & has_xl, has_yl & has_xr, edge_r.at[6, low], from_l.at[6, pl.ds(24, 8)], (iy + 1, ix - 1)),
        (has_yl & has_xr, has_yr & has_xl, edge_l.at[6, high], from_r.at[6, low], (iy - 1, ix + 1)),
        (has_yl & has_xl, has_yr & has_xr, edge_l.at[6, low], from_r.at[6, pl.ds(24, 8)], (iy - 1, ix - 1)),
        (has_xr, has_xl, last_ids, left_ids, (iy, ix + 1)),
        (has_xl, has_xr, first_ids, right_ids, (iy, ix - 1)),
    )
    traces = (
        (has_xr, has_xl, own_h, left_h, (iy, ix + 1)),
        (has_xl, has_xr, own_e, right_e, (iy, ix - 1)),
        (has_xr, has_xl, strip_own_h, strip_left_h, (iy, ix + 1)),
        (has_xl, has_xr, strip_own_e, strip_right_e, (iy, ix - 1)),
        (has_xr, has_xl, late_own_h, late_left_h, (iy, ix + 1)),
        (has_xl, has_xr, late_own_e, late_right_e, (iy, ix - 1)),
    )

    def trace(n, k):
        _, _, src, dst, device = traces[k]
        return pltpu.make_async_remote_copy(
            src_ref=src.at[n - STEPS // 2 if k >= 4 else n],
            dst_ref=dst.at[n - STEPS // 2 if k >= 4 else n],
            send_sem=trace_send.at[n, 2 + k % 2 if k >= 4 else k],
            recv_sem=trace_recv.at[n, 2 + k % 2 if k >= 4 else k],
            device_id=device,
            device_id_type=MESH,
        )

    def send_trace(n, k):
        @pl.when(traces[k][0])
        def _():
            trace(n, k).start()

    def await_trace(n, k):
        @pl.when(traces[k][1])
        def _():
            trace(n, k).wait_recv()

    def remote(i, src, dst, device):
        return pltpu.make_async_remote_copy(
            src_ref=src,
            dst_ref=dst,
            send_sem=send_sem.at[i],
            recv_sem=recv_sem.at[i],
            device_id=device,
            device_id_type=MESH,
        )

    def start_copies(which):
        for i in which:
            sends, _, src, dst, device = every[i]

            @pl.when(sends)
            def _(i=i, src=src, dst=dst, device=device):
                remote(i, src, dst, device).start()

    def await_copies(which):
        for i in which:
            _, receives, src, dst, _ = every[i]

            @pl.when(receives)
            def _(i=i, src=src, dst=dst):
                remote(i, src, dst, (iy, ix)).wait_recv()

    y_copies, corner_copies, x_copies = range(2), range(2, 6), range(6, 8)

    for given, fresh, arrived in (
        (has_xl, left_ids, (left_h, strip_left_h, late_left_h)),
        (has_xr, right_ids, (right_e, strip_right_e, late_right_e)),
    ):
        @pl.when(jnp.logical_not(given))
        def _(fresh=fresh, arrived=arrived):
            for buf in arrived:
                buf[...] = jnp.zeros(buf.shape, f32)
            fresh[...] = jnp.full(fresh.shape, NMAT, jnp.int32)

    for edge, side in ((from_l, has_yl), (from_r, has_yr)):
        @pl.when(jnp.logical_not(side))
        def _(edge=edge):
            edge[pl.ds(0, 6), pl.ds(HALO, CX), :] = jnp.zeros((6, CX, CY), f32)

        for given, rows, count in ((side, 8, 16), (side & has_xl, 0, 8), (side & has_xr, 24, 8)):
            @pl.when(jnp.logical_not(given))
            def _(edge=edge, rows=rows, count=count):
                edge[6, pl.ds(rows, count), :] = jnp.full((count, CY), float(NMAT), f32)

    for fields in ((ef, hf), (se, sh)):
        for field in fields:
            for c in range(3):
                for z in range(field.shape[1]):
                    for rows in (0, PAD + CX):
                        field[c, z, pl.ds(rows, PAD), :] = jnp.zeros((PAD, CY), f32)
    ids[:, pl.ds(0, 8), :] = jnp.full((NZ, 8, CY), NMAT, jnp.int32)
    ids[:, pl.ds(HALO + CX, 8), :] = jnp.full((NZ, 8, CY), NMAT, jnp.int32)
    for field in (ce, ch, de, dh):
        field[...] = jnp.zeros(field.shape, f32)

    pl.semaphore_wait(barrier, partners(around))
    begin_round(0)
    for load in loads:
        load.wait()

    def pack_edges(which):
        for i in which:
            for g in range(2):
                right = jnp.zeros((8, CY), f32)
                left = jnp.zeros((8, CY), f32)
                for z in range(NZ):
                    if i < 6:
                        value = (e_in, h_in)[i // 3][i % 3, z, pl.ds(8 * g, 8), :]
                    else:
                        value = ids[z, pl.ds(8 * g + HALO, 8), :].astype(f32)
                    here = (lane >= 8 * z) & (lane < 8 * z + 8)
                    right = jnp.where(here, pltpu.roll(value, (8 * z - 120) % CY, 1) if z < 15 else value, right)
                    left = jnp.where(here, pltpu.roll(value, 8 * z, 1) if z else value, left)
                edge_r[i, pl.ds(8 * g, 8), :] = right
                edge_l[i, pl.ds(8 * g, 8), :] = left

    for z in range(NZ):
        spot = pl.ds(z * GHOST, GHOST)
        last_ids[spot, :] = ids[z, pl.ds(HALO + CX - GHOST, GHOST), :]
        first_ids[spot, :] = ids[z, pl.ds(HALO, GHOST), :]
    start_copies(x_copies)
    pack_edges((6,))
    start_copies(corner_copies)

    def lookup(here):
        va = jnp.zeros((8, CY), f32)
        vb = jnp.zeros((8, CY), f32)
        for m in range(NMAT):
            chosen = here == m
            va = jnp.where(chosen, ca[m], va)
            vb = jnp.where(chosen, cb[m], vb)
        return va, vb

    def coefficients(groups):
        def one(z, carry):
            for g in groups:
                va, vb = lookup(ids[z, pl.ds(8 * g, 8), :])
                coef_a[z, pl.ds(8 * g, 8), :] = va
                coef_b[z, pl.ds(8 * g, 8), :] = vb
            return carry

        lax.fori_loop(0, NZ, one, 0)

    in_half = lax.rem(lane, CY // 2)

    def strips(groups):
        spots = (
            (0, 8, (lane >= 8) & (lane < 24)),
            (0, 48, (lane >= 32) & (lane < 48)),
            (1, 72, (lane >= 72) & (lane < 88)),
            (1, 112, (lane >= 96) & (lane < 112)),
        )

        def pack(j, values, i, rows, base):
            out = jnp.full((8, CY), base, f32)
            for half, shift, mask in spots:
                out = jnp.where(mask, pltpu.roll(values[half], shift, 1), out)
            before, after = from_l[i, rows, :], from_r[i, rows, :]
            out = jnp.where(in_half < 8, pltpu.roll(before, (CY - 8 * j) % CY, 1) if j else before, out)
            return jnp.where((in_half >= 48) & (in_half < 56), pltpu.roll(after, (CY + 48 - 8 * j) % CY, 1), out)

        for g in groups:
            rows = pl.ds(8 * g, 8)
            padded = pl.ds(PAD + 8 * g - HALO, 8)
            for j in range(HALF):
                for i in range(6 if g in OWN else 0):
                    source, target = ((e_in, se), (h_in, sh))[i // 3]
                    values = [source[i % 3, j + HALF * half, pl.ds(8 * g - HALO, 8), :] for half in range(2)]
                    target[i % 3, j, padded, :] = pack(j, values, i, rows, 0.0)
                values = [ids[j + HALF * half, rows, :].astype(f32) for half in range(2)]
                va, vb = lookup(pack(j, values, 6, rows, float(NMAT)))
                strip_a[j, rows, :] = va
                strip_b[j, rows, :] = vb

    def power(bit, carry):
        pr, pi, br, bi = carry
        take = lax.rem(lax.shift_right_logical(ix, bit), 2) == 1
        nr = pr * br - pi * bi
        ni = pr * bi + pi * br
        return (
            jnp.where(take, nr, pr),
            jnp.where(take, ni, pi),
            br * br - bi * bi,
            2.0 * br * bi,
        )

    coefficients(OWN)
    start_phase = Rows(phase, (0, total))

    half_y = jnp.where((in_half < 8) & (iy == 0), 0.0, 0.5).astype(f32)
    on_face = [
        (row + 8 * g >= face[0]) & (row + 8 * g < face[1]) & (lane >= face[2]) & (lane < face[3])
        for g in range(2)
    ]

    def at(g, shift=0):
        return pl.ds(PAD + 8 * g + shift, 8)

    zero = jnp.zeros((8, CY), f32)
    low_half = lane < CY // 2

    def new_magnetic(e, h, z, groups, here, above, factor, source):
        out = {}
        for g in groups:
            ex, ey, ez = here[g]
            ex_z, ey_z = above[g]
            ey_x, ez_x = e[1, z, at(g, 1), :], e[2, z, at(g, 1), :]
            if source is not None and g != 1:
                more_y, more_z = source(g, z)
                ey_x, ez_x = ey_x + more_y, ez_x + more_z
            ex_y, ez_y = pltpu.roll(ex, CY - 1, 1), pltpu.roll(ez, CY - 1, 1)
            hx = h[0, z, at(g), :] - factor * ((ez_y - ez) - (ey_z - ey))
            hy = h[1, z, at(g), :] - factor * ((ex_z - ex) - (ez_x - ez))
            hz = h[2, z, at(g), :] - factor * ((ey_x - ey) - (ex_y - ex))
            h[0, z, at(g), :] = hx
            h[1, z, at(g), :] = hy
            h[2, z, at(g), :] = hz
            out[g] = (hx, hy, hz)
        return out

    def new_electric(e, h, a, b, z, groups, base, here, now, below, source):
        out = {}
        for g in groups:
            ex, ey, ez = here[g]
            hx, hy, hz = now[g]
            hx_z, hy_z = below[g]
            hy_x, hz_x = h[1, z, at(g, -1), :], h[2, z, at(g, -1), :]
            if source is not None and g != 1:
                more_y, more_z = source(g, z)
                hy_x, hz_x = hy_x + more_y, hz_x + more_z
            hx_y, hz_y = pltpu.roll(hx, 1, 1), pltpu.roll(hz, 1, 1)
            va, vb = a[z, pl.ds(base + 8 * g, 8), :], b[z, pl.ds(base + 8 * g, 8), :]
            ex = va * ex + vb * ((hz - hz_y) - (hy - hy_z))
            ey = va * ey + vb * ((hx - hx_z) - (hz - hz_x))
            ez = va * ez + vb * ((hy - hy_x) - (hx - hx_y))
            e[0, z, at(g), :] = ex
            e[1, z, at(g), :] = ey
            e[2, z, at(g), :] = ez
            out[g] = (ex, ey)
        return out

    def plane(e, z, groups):
        return {g: tuple(e[c, z, at(g), :] for c in range(3)) for g in groups}

    def two(values):
        return {g: v[:2] for g, v in values.items()}

    def advance(e, h, groups, base, source_e=None, source_h=None):
        here = plane(e, 0, groups)
        nothing = {g: (zero, zero) for g in groups}
        below = nothing
        for z in range(NZ):
            ahead = plane(e, z + 1, groups) if z < NZ - 1 else None
            above = two(ahead) if ahead else nothing
            now = new_magnetic(e, h, z, groups, here, above, 0.5, source_e)
            new_electric(e, h, coef_a, coef_b, z, groups, base, here, now, below, source_h)
            below, here = two(now), ahead

    def advance_strips(e, h, groups, base, source_e=None, source_h=None):
        here = first = plane(e, 0, groups)
        for j in range(HALF):
            if j < HALF - 1:
                ahead = plane(e, j + 1, groups)
                above = two(ahead)
            else:
                ahead = None
                above = {
                    g: tuple(jnp.where(low_half, pltpu.roll(v, CY // 2, 1), 0.0) for v in first[g][:2]) for g in groups
                }
            now = new_magnetic(e, h, j, groups, here, above, half_y, source_e)
            if j:
                new_electric(e, h, strip_a, strip_b, j, groups, base, here, now, below, source_h)
            else:
                start = now
            below, here = two(now), ahead
        below = {g: tuple(jnp.where(low_half, 0.0, pltpu.roll(v, CY // 2, 1)) for v in below[g]) for g in groups}
        new_electric(e, h, strip_a, strip_b, 0, groups, base, plane(e, 0, groups), start, below, source_h)

    def border(n, field, x, mine, late, k):
        depth = field.shape[1]
        for c in (1, 2):
            mine[n, pl.ds((c - 1) * depth, depth), :] = field[c, :, PAD + x, :]
        if late is not None:
            first, second = (mine[n, pl.ds(c * depth, depth), :] for c in range(2))
            late[n - STEPS // 2] = jnp.where(in_middle, first, pltpu.roll(second, 16, 1))
        if k < 2:
            send_trace(n, k)

    in_strip = lax.rem(lane, CY // 4)
    in_middle = (in_strip >= 4) & (in_strip < 20)

    def keep(n, e, h, z, kept, first_row, add):
        for c, (field, part) in enumerate(((e, 0), (e, 1), (h, 0), (h, 1))):
            for k in range(2):
                spot = pl.ds(c * CX + 8 * k, 8)
                value = field[part, z, pl.ds(first_row + 8 * k, 8), :]
                kept[n, spot, :] = kept[n, spot, :] + value if add else value

    def alone(n, carry):
        border(n, ef, 0, own_e, None, 1)
        advance(ef, hf, (0, 1), HALO)
        border(n, hf, CX - 1, own_h, None, 0)
        keep(n, ef, hf, ZF, samples, PAD, False)
        return carry

    def alone_strips(is_late, n, carry):
        k = 4 if is_late else 2
        border(n, se, 0, strip_own_e, late_own_e if is_late else None, k + 1)
        advance_strips(se, sh, (0, 1), HALO)
        border(n, sh, CX - 1, strip_own_h, late_own_h if is_late else None, k)
        keep(n, se, sh, 0, strip_samples, PAD, False)
        return carry

    def sources(n, left, right, spot, depth):
        masks = {0: (row == spot) & has_xl, 2: row == spot}

        def source(g, z):
            buf = left if g == 0 else right
            return tuple(
                jnp.where(masks[g], jnp.broadcast_to(buf[n, pl.ds(c * depth + z, 1), :], (8, CY)), 0.0) for c in range(2)
            )

        return source

    SHIFT = HALO - GHOST

    def correct(groups, n, carry):
        await_trace(n, 0)
        await_trace(n, 1)
        advance(
            ce, ch, groups, SHIFT,
            sources(n, own_e, right_e, GHOST - 1, NZ), sources(n, left_h, own_h, GHOST, NZ),
        )
        keep(n, ce, ch, ZF, samples, PAD + GHOST, True)
        return carry

    def correct_strips(groups, is_late, n, carry):
        k = 4 if is_late else 2
        await_trace(n, k)
        await_trace(n, k + 1)
        if is_late:
            for late, buf in ((late_left_h, strip_left_h), (late_right_e, strip_right_e)):
                both = late[n - STEPS // 2]
                buf[n, pl.ds(0, HALF), :] = both
                buf[n, pl.ds(HALF, HALF), :] = pltpu.roll(both, CY - 16, 1)
        advance_strips(
            de, dh, groups, SHIFT,
            sources(n, strip_own_e, strip_right_e, GHOST - 1, HALF), sources(n, strip_left_h, strip_own_h, GHOST, HALF),
        )
        keep(n, de, dh, 0, strip_samples, PAD + GHOST, True)
        return carry

    lax.fori_loop(0, EARLY, alone, 0)
    pack_edges(range(6))
    start_copies(y_copies)
    lax.fori_loop(EARLY, STEPS, alone, 0)
    begin_round(1)
    await_copies(y_copies)
    strips(OWN)
    lax.fori_loop(0, STEPS // 2, functools.partial(alone_strips, False), 0)
    lax.fori_loop(STEPS // 2, STEPS, functools.partial(alone_strips, True), 0)
    begin_round(2)
    rows_at_once = 8
    for start in range(0, total, rows_at_once):
        part = pl.ds(start, rows_at_once)
        carry = (
            jnp.full((rows_at_once, CY), scale, jnp.float32),
            jnp.zeros((rows_at_once, CY), jnp.float32),
            block.at(0, start, rows_at_once),
            block.at(1, start, rows_at_once),
        )
        for bit in range(max(1, (nx - 1).bit_length())):
            carry = power(bit, carry)
        phase[part, :] = carry[0]
        phase[pl.ds(total + start, rows_at_once), :] = carry[1]
    await_copies(x_copies)
    await_copies(corner_copies)
    for z in range(NZ):
        spot = pl.ds(z * GHOST, GHOST)
        ids[z, pl.ds(HALO - GHOST, GHOST), :] = left_ids[spot, :]
        ids[z, pl.ds(HALO + CX, GHOST), :] = right_ids[spot, :]
    strips((0, 3))
    coefficients((0, 3))

    def send_strips(kinds, n, carry):
        for k in kinds:
            send_trace(n, k)
        return carry

    lax.fori_loop(0, STEPS // 2, functools.partial(send_strips, (2, 3)), 0)
    lax.fori_loop(STEPS // 2, STEPS, functools.partial(send_strips, (4, 5)), 0)
    lax.fori_loop(0, STEPS // 2, functools.partial(correct, (0, 2)), 0)
    lax.fori_loop(STEPS // 2, STEPS, functools.partial(correct, (0, 1, 2)), 0)
    begin_round(3)
    lax.fori_loop(0, STEPS // 2, functools.partial(correct_strips, (0, 2), False), 0)
    lax.fori_loop(STEPS // 2, STEPS, functools.partial(correct_strips, (0, 1, 2), True), 0)

    for k in range(4, len(rounds)):
        begin_round(k)
    for n in range(STEPS):
        for c in range(4):
            for k in range(2):
                spot = pl.ds(c * CX + 8 * k, 8)
                end = strip_samples[n, spot, :]
                value = jnp.where(lane < 8, pltpu.roll(end, 56, 1), samples[n, spot, :])
                value = jnp.where(lane >= CY - 8, pltpu.roll(end, 16, 1), value)
                sample[pl.ds(n * 4 * CX + c * CX + 8 * k, 8), :] = jnp.where(on_face[k], value, 0.0)
    for part in range(2):
        turned[part] = jnp.dot(
            sample[...],
            table[pl.ds(starts[part], CY), :],
            precision=lax.Precision.HIGHEST,
            preferred_element_type=f32,
        )
    for first in range(0, 4 * CX, 8):
        re, im = zero, zero
        for n in range(STEPS):
            g_re, g_im = (turned[part, pl.ds(n * 4 * CX + first, 8), :] for part in range(2))
            ct, st = time.at(0, n, 1), time.at(1, n, 1)
            re += ct * g_re + st * g_im
            im += ct * g_im - st * g_re
        acc[0, pl.ds(first, 8), :] = re
        acc[1, pl.ds(first, 8), :] = im

    end_round(len(rounds) - 1)
    yr, yi = y_start.at(0, iy, 1), y_start.at(1, iy, 1)
    col_re = acc[0] * yr - acc[1] * yi
    acc[1] = acc[0] * yi + acc[1] * yr
    acc[0] = col_re
    for part in range(2):
        for x in range(CX):
            four = acc[part, pl.ds(x, 4, stride=CX), :]
            cols[part, x, pl.ds(0, 4), :] = four
            cols[part, x, pl.ds(4, 4), :] = four

    upper = lax.broadcasted_iota(jnp.int32, (8, CY), 0) < 4
    at_once = min(8, total)

    def send_far(k):
        other = lax.rem(me + k, total)
        return pltpu.make_async_remote_copy(
            src_ref=f_send.at[k],
            dst_ref=f_recv.at[k - 1],
            send_sem=f_send_sem,
            recv_sem=f_recv_sem,
            device_id=(lax.div(other, nx), lax.rem(other, nx)),
            device_id_type=MESH,
        )

    def project(trip, carry):
        k0 = trip * at_once
        picked = [bands[lax.rem(me + k0 + j, total)] for j in range(at_once)]

        def pair(rows, part, j):
            return jnp.where(upper, rows.at(part, picked[j], 1), rows.at(part, picked[j + 1], 1))

        pairs = range(0, at_once, 2)
        wr = [pair(cell, 0, j) for j in pairs]
        wi = [pair(cell, 1, j) for j in pairs]
        c_re, c_im = cols[0, CX - 1], cols[1, CX - 1]
        re = [c_re for _ in pairs]
        im = [c_im for _ in pairs]
        for x in range(CX - 2, -1, -1):
            c_re, c_im = cols[0, x], cols[1, x]
            re, im = (
                [r * a - i * b + c_re for r, i, a, b in zip(re, im, wr, wi)],
                [r * b + i * a + c_im for r, i, a, b in zip(re, im, wr, wi)],
            )
        for t, j in enumerate(pairs):
            pr, pi = pair(start_phase, 0, j), pair(start_phase, 1, j)
            far_re = re[t] * pr - im[t] * pi
            far_im = re[t] * pi + im[t] * pr
            f_send[k0 + j] = jnp.where(upper, far_re, pltpu.roll(far_im, 4, 0))
            f_send[k0 + j + 1] = jnp.where(upper, pltpu.roll(far_re, 4, 0), far_im)
        for j in range(at_once):
            @pl.when(k0 + j > 0)
            def _(j=j):
                send_far(k0 + j).start()
        return carry

    lax.fori_loop(0, total // at_once, project, 0)

    for field, strip, more, strip_more, out in ((ef, se, ce, de, e_out), (hf, sh, ch, dh, h_out)):
        for c in range(3):
            for z in range(NZ):
                half, j = z // HALF, z % HALF
                for g in range(2):
                    end = strip[c, j, at(g), :] + strip_more[c, j, at(g, GHOST), :]
                    value = field[c, z, at(g), :] + more[c, z, at(g, GHOST), :]
                    value = jnp.where(lane < 8, pltpu.roll(end, (CY - 64 * half - 8) % CY, 1), value)
                    value = jnp.where(lane >= CY - 8, pltpu.roll(end, 80 - 64 * half, 1), value)
                    out[c, z, pl.ds(8 * g, 8), :] = value

    pltpu.make_async_copy(f_recv, f_recv, f_recv_sem).wait()
    if total <= 64:
        terms = [f_send[0]] + [f_recv[k] for k in range(total - 1)]
        while len(terms) > 1:
            terms = [a + b for a, b in zip(terms[::2], terms[1::2])]
        far_out[...] = terms[0]
    else:
        far_out[...] = lax.fori_loop(0, total - 1, lambda k, t: t + f_recv[k], f_send[0])
    pltpu.make_async_copy(f_recv, f_recv, f_send_sem).wait()
    for i, (sends, _, src, dst, device) in enumerate(every):
        @pl.when(sends)
        def _(i=i, src=src, dst=dst, device=device):
            remote(i, src, dst, device).wait_send()

    def sent(kinds, n, carry):
        for k in kinds:
            @pl.when(traces[k][0])
            def _(k=k):
                trace(n, k).wait_send()
        return carry

    lax.fori_loop(0, STEPS // 2, functools.partial(sent, (0, 1, 2, 3)), 0)
    lax.fori_loop(STEPS // 2, STEPS, functools.partial(sent, (0, 1, 4, 5)), 0)


def write_out(e, h, far, e_out, h_out, far_out, sem):
    copies = [
        pltpu.make_async_copy(src, dst, sem.at[i])
        for i, (src, dst) in enumerate(((e, e_out), (h, h_out), (far, far_out)))
    ]
    for copy in copies:
        copy.start()
    for copy in copies:
        copy.wait()


def local(ny, nx, electric, magnetic, material_ids, update_ca, update_cb, face_ranges, band_table):
    total = ny * nx
    bands = band_table.shape[0]
    assert bands == total and electric.shape == (3, NZ, CX, CY)
    scale = 1.0 / math.sqrt(CX * nx * CY * ny)
    f32 = jnp.float32
    vmem = pl.BlockSpec(memory_space=pltpu.VMEM)
    hbm = pl.BlockSpec(memory_space=pltpu.HBM)
    packed, starts = tables(bands, ny)
    e_out, h_out, far = pl.pallas_call(
        functools.partial(kernel, ny, nx, scale, starts),
        out_shape=(
            pltpu.VMEM(electric.shape, f32),
            pltpu.VMEM(electric.shape, f32),
            pltpu.VMEM((8, CY), f32),
        ),
        in_specs=[hbm] * 8,
        out_specs=(vmem,) * 3,
        scratch_shapes=[
            pltpu.VMEM((3, NZ, PITCH, CY), f32),
            pltpu.VMEM((3, NZ, PITCH, CY), f32),
            pltpu.VMEM((NZ, ROWS, CY), jnp.int32),
            pltpu.SMEM((NMAT,), f32),
            pltpu.SMEM((NMAT,), f32),
            pltpu.SMEM((4,), jnp.int32),
            pltpu.SMEM((bands,), jnp.int32),
            pltpu.VMEM(packed.shape, f32),
            pltpu.VMEM((3, NZ, CX, CY), f32),
            pltpu.VMEM((3, NZ, CX, CY), f32),
            pltpu.SemaphoreType.DMA((10,)),
            pltpu.VMEM((NZ, ROWS, CY), f32),
            pltpu.VMEM((NZ, ROWS, CY), f32),
            pltpu.VMEM((3, HALF, PITCH, CY), f32),
            pltpu.VMEM((3, HALF, PITCH, CY), f32),
            pltpu.VMEM((HALF, ROWS, CY), f32),
            pltpu.VMEM((HALF, ROWS, CY), f32),
            pltpu.VMEM((3, NZ, WIDE, CY), f32),
            pltpu.VMEM((3, NZ, WIDE, CY), f32),
            pltpu.VMEM((3, HALF, WIDE, CY), f32),
            pltpu.VMEM((3, HALF, WIDE, CY), f32),
            pltpu.VMEM((7, CX, CY), f32),
            pltpu.VMEM((7, CX, CY), f32),
            pltpu.VMEM((7, ROWS, CY), f32),
            pltpu.VMEM((7, ROWS, CY), f32),
            *[pltpu.VMEM((NZ * GHOST, CY), jnp.int32)] * 4,
            *[pltpu.VMEM((STEPS, 2 * NZ, CY), f32)] * 4,
            *[pltpu.VMEM((STEPS, 2 * HALF, CY), f32)] * 4,
            *[pltpu.VMEM((STEPS // 2, HALF, CY), f32)] * 4,
            pltpu.VMEM((STEPS, 4 * CX, CY), f32),
            pltpu.VMEM((STEPS, 4 * CX, CY), f32),
            pltpu.VMEM((STEPS * 4 * CX, CY), f32),
            pltpu.VMEM((2, STEPS * 4 * CX, CY), f32),
            pltpu.VMEM((2, 4 * CX, CY), f32),
            pltpu.VMEM((2, CX, 8, CY), f32),
            pltpu.VMEM((2 * total, CY), f32),
            pltpu.VMEM((total, 8, CY), f32),
            pltpu.VMEM((total - 1, 8, CY), f32),
            pltpu.SemaphoreType.DMA((8,)),
            pltpu.SemaphoreType.DMA((8,)),
            pltpu.SemaphoreType.DMA((STEPS, 4)),
            pltpu.SemaphoreType.DMA((STEPS, 4)),
            pltpu.SemaphoreType.REGULAR((len(round_offsets(ny, nx)),)),
            pltpu.SemaphoreType.DMA,
            pltpu.SemaphoreType.DMA,
        ],
        compiler_params=pltpu.CompilerParams(
            collective_id=0, has_side_effects=True, vmem_limit_bytes=62 * 1024 * 1024
        ),
        name="fdtd",
    )(
        electric,
        magnetic,
        material_ids,
        update_ca,
        update_cb,
        face_ranges.reshape(4),
        band_table,
        packed,
    )
    e_out, h_out, far = pl.pallas_call(
        write_out,
        out_shape=tuple(jax.ShapeDtypeStruct(value.shape, f32) for value in (e_out, h_out, far)),
        in_specs=[vmem] * 3,
        out_specs=(hbm,) * 3,
        scratch_shapes=[pltpu.SemaphoreType.DMA((3,))],
        name="write_out",
    )(*(pltpu.with_memory_space_constraint(value, pltpu.VMEM) for value in (e_out, h_out, far)))
    return e_out, h_out, far.reshape(1, 8, CY)


def solution(mesh):
    in_specs = (
        P(None, None, "inner", "grp"),
        P(None, None, "inner", "grp"),
        P(None, "inner", "grp"),
        P(),
        P(),
        P("inner", "grp", None),
        P(),
    )
    out_specs = (
        P(None, None, "inner", "grp"),
        P(None, None, "inner", "grp"),
        P(("grp", "inner"), None, None),
    )
    body = functools.partial(local, mesh.shape["grp"], mesh.shape["inner"])
    return jax.shard_map(body, mesh=mesh, in_specs=in_specs, out_specs=out_specs, check_vma=False)
```

```python
import functools
import math

import jax
import jax.numpy as jnp
import numpy as np
from jax import lax
from jax.experimental import pallas as pl
from jax.experimental.pallas import tpu as pltpu
from jax.sharding import PartitionSpec as P

STEPS = 8
FREQS = 32
ANG_BAND = 4
NMAT = 8
ZF = 8
NZ = 16
CX = 16
CY = 128
PAD = 8
HALO = 8
ROWS = CX + 2 * HALO
GHOST = 4
EARLY = 2
PITCH = CX + 2 * PAD
WIDE = CX + 2 * GHOST + 2 * PAD
OWN = (1, 2)
HALF = NZ // 2
MESH = pl.DeviceIdType.MESH


def tables(bands, groups):
    f = np.tile(np.arange(FREQS, dtype=np.int64) + 1, ANG_BAND)
    b = np.repeat(np.arange(ANG_BAND, dtype=np.int64) * 33 // ANG_BAND - 16, FREQS)
    a = np.arange(bands, dtype=np.int64) - bands // 2

    def both(turns, period):
        angle = (turns % period) * (2.0 * math.pi / period)
        return np.cos(angle).astype(np.float32), np.sin(angle).astype(np.float32)

    y = np.arange(CY, dtype=np.int64)[:, None]
    proj = np.concatenate(both(f * b * y, 4096), axis=1)
    time = np.stack(both(f * np.arange(STEPS, dtype=np.int64)[:, None], 128))
    y_start = np.stack(both(f * b * CY * np.arange(groups, dtype=np.int64)[:, None], 4096))
    cell = np.stack(both(f * a[:, None], 4096))
    block = np.stack(both(f * a[:, None] * CX, 4096))
    flat = [proj[:, :CY], proj[:, CY:]] + [part for table in (time, y_start, cell, block) for part in table]
    starts = np.cumsum([0] + [-(-part.shape[0] // 8) * 8 for part in flat])
    packed = np.zeros((starts[-1], CY), np.float32)
    for start, part in zip(starts, flat):
        packed[start : start + part.shape[0]] = part
    return packed, tuple(int(start) for start in starts[:-1])


def round_offsets(ny, nx):
    rounds, reach = [], 1
    while reach < max(ny, nx) - 1:
        rounds.append(
            [(0, s * reach) for s in (-1, 1) if reach < nx - 1] + [(s * reach, 0) for s in (-1, 1) if reach < ny - 1]
        )
        reach *= 2
    rounds.append([(s * d, 0) for d in range(1, ny) for s in (-1, 1)])
    return rounds


class Rows:
    def __init__(self, ref, starts):
        self.ref, self.starts = ref, starts

    def at(self, part, first, count):
        return self.ref[pl.ds(self.starts[part] + first, count), :]


def kernel(
    ny, nx, scale, starts,
    e_hbm, h_hbm, ids_hbm, ca_hbm, cb_hbm, face_hbm, bands_hbm, table_hbm,
    e_out, h_out, far_out,
    ef, hf, ids, ca, cb, face, bands, table, e_in, h_in, in_sem,
    coef_a, coef_b, se, sh, strip_a, strip_b, ce, ch, de, dh,
    edge_r, edge_l, from_l, from_r, last_ids, first_ids, left_ids, right_ids,
    own_h, own_e, left_h, right_e, strip_own_h, strip_own_e, strip_left_h, strip_right_e,
    late_own_h, late_own_e, late_left_h, late_right_e,
    samples, strip_samples, sample, turned, acc, cols, phase, f_send, f_recv,
    send_sem, recv_sem, trace_send, trace_recv, round_sem, f_send_sem, f_recv_sem,
):
    iy = lax.axis_index("grp")
    ix = lax.axis_index("inner")
    total = ny * nx
    me = iy * nx + ix
    f32 = jnp.float32
    lane = lax.broadcasted_iota(jnp.int32, (8, CY), 1)
    row = lax.broadcasted_iota(jnp.int32, (8, CY), 0)
    own_rows = pl.ds(PAD, CX)

    loads = [
        pltpu.make_async_copy(src, dst, in_sem.at[i])
        for i, (src, dst) in enumerate(
            (
                (e_hbm, ef.at[:, :, own_rows]),
                (h_hbm, hf.at[:, :, own_rows]),
                (ids_hbm, ids.at[:, pl.ds(HALO, CX)]),
                (ca_hbm, ca),
                (cb_hbm, cb),
                (face_hbm, face),
                (bands_hbm, bands),
                (table_hbm, table),
                (e_hbm, e_in),
                (h_hbm, h_in),
            )
        )
    ]
    time, y_start, cell, block = (Rows(table, starts[i : i + 2]) for i in (2, 4, 6, 8))

    barrier = pltpu.get_barrier_semaphore()

    has_xr, has_xl = ix < nx - 1, ix > 0
    has_yr, has_yl = iy < ny - 1, iy > 0

    def within(y, x):
        return (y >= 0) & (y < ny) & (x >= 0) & (x < nx)

    def signal_all(sem, offsets):
        for dy, dx in offsets:
            @pl.when(within(iy + dy, ix + dx))
            def _(dy=dy, dx=dx):
                pl.semaphore_signal(sem, inc=1, device_id=(iy + dy, ix + dx), device_id_type=MESH)

    def partners(offsets):
        return sum(jnp.where(within(iy + dy, ix + dx), 1, 0) for dy, dx in offsets)

    around = [(dy, dx) for dy in (-1, 0, 1) for dx in (-1, 0, 1) if (dy, dx) != (0, 0)]
    signal_all(barrier, around)
    for load in loads:
        load.start()
    rounds = round_offsets(ny, nx)

    def begin_round(k):
        if k > 0:
            end_round(k - 1)
        signal_all(round_sem.at[k], rounds[k])

    def end_round(k):
        pl.semaphore_wait(round_sem.at[k], partners(rounds[k]))

    low, high = pl.ds(0, 8), pl.ds(8, 8)
    every = (
        (has_yr, has_yl, edge_r, from_l.at[:, pl.ds(HALO, CX)], (iy + 1, ix)),
        (has_yl, has_yr, edge_l, from_r.at[:, pl.ds(HALO, CX)], (iy - 1, ix)),
        (has_yr & has_xr, has_yl & has_xl, edge_r.at[6, high], from_l.at[6, low], (iy + 1, ix + 1)),
        (has_yr & has_xl, has_yl & has_xr, edge_r.at[6, low], from_l.at[6, pl.ds(24, 8)], (iy + 1, ix - 1)),
        (has_yl & has_xr, has_yr & has_xl, edge_l.at[6, high], from_r.at[6, low], (iy - 1, ix + 1)),
        (has_yl & has_xl, has_yr & has_xr, edge_l.at[6, low], from_r.at[6, pl.ds(24, 8)], (iy - 1, ix - 1)),
        (has_xr, has_xl, last_ids, left_ids, (iy, ix + 1)),
        (has_xl, has_xr, first_ids, right_ids, (iy, ix - 1)),
    )
    traces = (
        (has_xr, has_xl, own_h, left_h, (iy, ix + 1)),
        (has_xl, has_xr, own_e, right_e, (iy, ix - 1)),
        (has_xr, has_xl, strip_own_h, strip_left_h, (iy, ix + 1)),
        (has_xl, has_xr, strip_own_e, strip_right_e, (iy, ix - 1)),
        (has_xr, has_xl, late_own_h, late_left_h, (iy, ix + 1)),
        (has_xl, has_xr, late_own_e, late_right_e, (iy, ix - 1)),
    )

    def trace(n, k):
        _, _, src, dst, device = traces[k]
        return pltpu.make_async_remote_copy(
            src_ref=src.at[n - STEPS // 2 if k >= 4 else n],
            dst_ref=dst.at[n - STEPS // 2 if k >= 4 else n],
            send_sem=trace_send.at[n, 2 + k % 2 if k >= 4 else k],
            recv_sem=trace_recv.at[n, 2 + k % 2 if k >= 4 else k],
            device_id=device,
            device_id_type=MESH,
        )

    def send_trace(n, k):
        @pl.when(traces[k][0])
        def _():
            trace(n, k).start()

    def await_trace(n, k):
        @pl.when(traces[k][1])
        def _():
            trace(n, k).wait_recv()

    def remote(i, src, dst, device):
        return pltpu.make_async_remote_copy(
            src_ref=src,
            dst_ref=dst,
            send_sem=send_sem.at[i],
            recv_sem=recv_sem.at[i],
            device_id=device,
            device_id_type=MESH,
        )

    def start_copies(which):
        for i in which:
            sends, _, src, dst, device = every[i]

            @pl.when(sends)
            def _(i=i, src=src, dst=dst, device=device):
                remote(i, src, dst, device).start()

    def await_copies(which):
        for i in which:
            _, receives, src, dst, _ = every[i]

            @pl.when(receives)
            def _(i=i, src=src, dst=dst):
                remote(i, src, dst, (iy, ix)).wait_recv()

    y_copies, corner_copies, x_copies = range(2), range(2, 6), range(6, 8)

    for given, fresh, arrived in (
        (has_xl, left_ids, (left_h, strip_left_h, late_left_h)),
        (has_xr, right_ids, (right_e, strip_right_e, late_right_e)),
    ):
        @pl.when(jnp.logical_not(given))
        def _(fresh=fresh, arrived=arrived):
            for buf in arrived:
                buf[...] = jnp.zeros(buf.shape, f32)
            fresh[...] = jnp.full(fresh.shape, NMAT, jnp.int32)

    for edge, side in ((from_l, has_yl), (from_r, has_yr)):
        @pl.when(jnp.logical_not(side))
        def _(edge=edge):
            edge[pl.ds(0, 6), pl.ds(HALO, CX), :] = jnp.zeros((6, CX, CY), f32)

        for given, rows, count in ((side, 8, 16), (side & has_xl, 0, 8), (side & has_xr, 24, 8)):
            @pl.when(jnp.logical_not(given))
            def _(edge=edge, rows=rows, count=count):
                edge[6, pl.ds(rows, count), :] = jnp.full((count, CY), float(NMAT), f32)

    for fields in ((ef, hf), (se, sh)):
        for field in fields:
            for c in range(3):
                for z in range(field.shape[1]):
                    for rows in (0, PAD + CX):
                        field[c, z, pl.ds(rows, PAD), :] = jnp.zeros((PAD, CY), f32)
    ids[:, pl.ds(0, 8), :] = jnp.full((NZ, 8, CY), NMAT, jnp.int32)
    ids[:, pl.ds(HALO + CX, 8), :] = jnp.full((NZ, 8, CY), NMAT, jnp.int32)
    for field in (ce, ch, de, dh):
        field[...] = jnp.zeros(field.shape, f32)

    pl.semaphore_wait(barrier, partners(around))
    begin_round(0)
    for load in loads:
        load.wait()

    def pack_edges(which):
        for i in which:
            for g in range(2):
                right = jnp.zeros((8, CY), f32)
                left = jnp.zeros((8, CY), f32)
                for z in range(NZ):
                    if i < 6:
                        value = (e_in, h_in)[i // 3][i % 3, z, pl.ds(8 * g, 8), :]
                    else:
                        value = ids[z, pl.ds(8 * g + HALO, 8), :].astype(f32)
                    here = (lane >= 8 * z) & (lane < 8 * z + 8)
                    right = jnp.where(here, pltpu.roll(value, (8 * z - 120) % CY, 1) if z < 15 else value, right)
                    left = jnp.where(here, pltpu.roll(value, 8 * z, 1) if z else value, left)
                edge_r[i, pl.ds(8 * g, 8), :] = right
                edge_l[i, pl.ds(8 * g, 8), :] = left

    for z in range(NZ):
        spot = pl.ds(z * GHOST, GHOST)
        last_ids[spot, :] = ids[z, pl.ds(HALO + CX - GHOST, GHOST), :]
        first_ids[spot, :] = ids[z, pl.ds(HALO, GHOST), :]
    start_copies(x_copies)
    pack_edges((6,))
    start_copies(corner_copies)

    def lookup(here):
        va = jnp.zeros((8, CY), f32)
        vb = jnp.zeros((8, CY), f32)
        for m in range(NMAT):
            chosen = here == m
            va = jnp.where(chosen, ca[m], va)
            vb = jnp.where(chosen, cb[m], vb)
        return va, vb

    def coefficients(groups):
        def one(z, carry):
            for g in groups:
                va, vb = lookup(ids[z, pl.ds(8 * g, 8), :])
                coef_a[z, pl.ds(8 * g, 8), :] = va
                coef_b[z, pl.ds(8 * g, 8), :] = vb
            return carry

        lax.fori_loop(0, NZ, one, 0)

    in_half = lax.rem(lane, CY // 2)

    def strips(groups):
        spots = (
            (0, 8, (lane >= 8) & (lane < 24)),
            (0, 48, (lane >= 32) & (lane < 48)),
            (1, 72, (lane >= 72) & (lane < 88)),
            (1, 112, (lane >= 96) & (lane < 112)),
        )

        def pack(j, values, i, rows, base):
            out = jnp.full((8, CY), base, f32)
            for half, shift, mask in spots:
                out = jnp.where(mask, pltpu.roll(values[half], shift, 1), out)
            before, after = from_l[i, rows, :], from_r[i, rows, :]
            out = jnp.where(in_half < 8, pltpu.roll(before, (CY - 8 * j) % CY, 1) if j else before, out)
            return jnp.where((in_half >= 48) & (in_half < 56), pltpu.roll(after, (CY + 48 - 8 * j) % CY, 1), out)

        for g in groups:
            rows = pl.ds(8 * g, 8)
            padded = pl.ds(PAD + 8 * g - HALO, 8)
            for j in range(HALF):
                for i in range(6 if g in OWN else 0):
                    source, target = ((e_in, se), (h_in, sh))[i // 3]
                    values = [source[i % 3, j + HALF * half, pl.ds(8 * g - HALO, 8), :] for half in range(2)]
                    target[i % 3, j, padded, :] = pack(j, values, i, rows, 0.0)
                values = [ids[j + HALF * half, rows, :].astype(f32) for half in range(2)]
                va, vb = lookup(pack(j, values, 6, rows, float(NMAT)))
                strip_a[j, rows, :] = va
                strip_b[j, rows, :] = vb

    def power(bit, carry):
        pr, pi, br, bi = carry
        take = lax.rem(lax.shift_right_logical(ix, bit), 2) == 1
        nr = pr * br - pi * bi
        ni = pr * bi + pi * br
        return (
            jnp.where(take, nr, pr),
            jnp.where(take, ni, pi),
            br * br - bi * bi,
            2.0 * br * bi,
        )

    coefficients(OWN)
    start_phase = Rows(phase, (0, total))

    half_y = jnp.where((in_half < 8) & (iy == 0), 0.0, 0.5).astype(f32)
    on_face = [
        (row + 8 * g >= face[0]) & (row + 8 * g < face[1]) & (lane >= face[2]) & (lane < face[3])
        for g in range(2)
    ]

    def at(g, shift=0):
        return pl.ds(PAD + 8 * g + shift, 8)

    zero = jnp.zeros((8, CY), f32)
    low_half = lane < CY // 2

    def new_magnetic(e, h, z, groups, here, above, factor, source):
        out = {}
        for g in groups:
            ex, ey, ez = here[g]
            ex_z, ey_z = above[g]
            ey_x, ez_x = e[1, z, at(g, 1), :], e[2, z, at(g, 1), :]
            if source is not None and g != 1:
                more_y, more_z = source(g, z)
                ey_x, ez_x = ey_x + more_y, ez_x + more_z
            ex_y, ez_y = pltpu.roll(ex, CY - 1, 1), pltpu.roll(ez, CY - 1, 1)
            hx = h[0, z, at(g), :] - factor * ((ez_y - ez) - (ey_z - ey))
            hy = h[1, z, at(g), :] - factor * ((ex_z - ex) - (ez_x - ez))
            hz = h[2, z, at(g), :] - factor * ((ey_x - ey) - (ex_y - ex))
            h[0, z, at(g), :] = hx
            h[1, z, at(g), :] = hy
            h[2, z, at(g), :] = hz
            out[g] = (hx, hy, hz)
        return out

    def new_electric(e, h, a, b, z, groups, base, here, now, below, source):
        out = {}
        for g in groups:
            ex, ey, ez = here[g]
            hx, hy, hz = now[g]
            hx_z, hy_z = below[g]
            hy_x, hz_x = h[1, z, at(g, -1), :], h[2, z, at(g, -1), :]
            if source is not None and g != 1:
                more_y, more_z = source(g, z)
                hy_x, hz_x = hy_x + more_y, hz_x + more_z
            hx_y, hz_y = pltpu.roll(hx, 1, 1), pltpu.roll(hz, 1, 1)
            va, vb = a[z, pl.ds(base + 8 * g, 8), :], b[z, pl.ds(base + 8 * g, 8), :]
            ex = va * ex + vb * ((hz - hz_y) - (hy - hy_z))
            ey = va * ey + vb * ((hx - hx_z) - (hz - hz_x))
            ez = va * ez + vb * ((hy - hy_x) - (hx - hx_y))
            e[0, z, at(g), :] = ex
            e[1, z, at(g), :] = ey
            e[2, z, at(g), :] = ez
            out[g] = (ex, ey)
        return out

    def plane(e, z, groups):
        return {g: tuple(e[c, z, at(g), :] for c in range(3)) for g in groups}

    def two(values):
        return {g: v[:2] for g, v in values.items()}

    def advance(e, h, groups, base, source_e=None, source_h=None):
        here = plane(e, 0, groups)
        nothing = {g: (zero, zero) for g in groups}
        below = nothing
        for z in range(NZ):
            ahead = plane(e, z + 1, groups) if z < NZ - 1 else None
            above = two(ahead) if ahead else nothing
            now = new_magnetic(e, h, z, groups, here, above, 0.5, source_e)
            new_electric(e, h, coef_a, coef_b, z, groups, base, here, now, below, source_h)
            below, here = two(now), ahead

    def advance_strips(e, h, groups, base, source_e=None, source_h=None):
        here = first = plane(e, 0, groups)
        for j in range(HALF):
            if j < HALF - 1:
                ahead = plane(e, j + 1, groups)
                above = two(ahead)
            else:
                ahead = None
                above = {
                    g: tuple(jnp.where(low_half, pltpu.roll(v, CY // 2, 1), 0.0) for v in first[g][:2]) for g in groups
                }
            now = new_magnetic(e, h, j, groups, here, above, half_y, source_e)
            if j:
                new_electric(e, h, strip_a, strip_b, j, groups, base, here, now, below, source_h)
            else:
                start = now
            below, here = two(now), ahead
        below = {g: tuple(jnp.where(low_half, 0.0, pltpu.roll(v, CY // 2, 1)) for v in below[g]) for g in groups}
        new_electric(e, h, strip_a, strip_b, 0, groups, base, plane(e, 0, groups), start, below, source_h)

    def border(n, field, x, mine, late, k):
        depth = field.shape[1]
        for c in (1, 2):
            mine[n, pl.ds((c - 1) * depth, depth), :] = field[c, :, PAD + x, :]
        if late is not None:
            first, second = (mine[n, pl.ds(c * depth, depth), :] for c in range(2))
            late[n - STEPS // 2] = jnp.where(in_middle, first, pltpu.roll(second, 16, 1))
        if k < 2:
            send_trace(n, k)

    in_strip = lax.rem(lane, CY // 4)
    in_middle = (in_strip >= 4) & (in_strip < 20)

    def keep(n, e, h, z, kept, first_row, add):
        for c, (field, part) in enumerate(((e, 0), (e, 1), (h, 0), (h, 1))):
            for k in range(2):
                spot = pl.ds(c * CX + 8 * k, 8)
                value = field[part, z, pl.ds(first_row + 8 * k, 8), :]
                kept[n, spot, :] = kept[n, spot, :] + value if add else value

    def alone(n, carry):
        border(n, ef, 0, own_e, None, 1)
        advance(ef, hf, (0, 1), HALO)
        border(n, hf, CX - 1, own_h, None, 0)
        keep(n, ef, hf, ZF, samples, PAD, False)
        return carry

    def alone_strips(is_late, n, carry):
        k = 4 if is_late else 2
        border(n, se, 0, strip_own_e, late_own_e if is_late else None, k + 1)
        advance_strips(se, sh, (0, 1), HALO)
        border(n, sh, CX - 1, strip_own_h, late_own_h if is_late else None, k)
        keep(n, se, sh, 0, strip_samples, PAD, False)
        return carry

    def sources(n, left, right, spot, depth):
        masks = {0: (row == spot) & has_xl, 2: row == spot}

        def source(g, z):
            buf = left if g == 0 else right
            return tuple(
                jnp.where(masks[g], jnp.broadcast_to(buf[n, pl.ds(c * depth + z, 1), :], (8, CY)), 0.0) for c in range(2)
            )

        return source

    SHIFT = HALO - GHOST

    def correct(groups, n, carry):
        await_trace(n, 0)
        await_trace(n, 1)
        advance(
            ce, ch, groups, SHIFT,
            sources(n, own_e, right_e, GHOST - 1, NZ), sources(n, left_h, own_h, GHOST, NZ),
        )
        keep(n, ce, ch, ZF, samples, PAD + GHOST, True)
        return carry

    def correct_strips(groups, is_late, n, carry):
        k = 4 if is_late else 2
        await_trace(n, k)
        await_trace(n, k + 1)
        if is_late:
            for late, buf in ((late_left_h, strip_left_h), (late_right_e, strip_right_e)):
                both = late[n - STEPS // 2]
                buf[n, pl.ds(0, HALF), :] = both
                buf[n, pl.ds(HALF, HALF), :] = pltpu.roll(both, CY - 16, 1)
        advance_strips(
            de, dh, groups, SHIFT,
            sources(n, strip_own_e, strip_right_e, GHOST - 1, HALF), sources(n, strip_left_h, strip_own_h, GHOST, HALF),
        )
        keep(n, de, dh, 0, strip_samples, PAD + GHOST, True)
        return carry

    lax.fori_loop(0, EARLY, alone, 0)
    pack_edges(range(6))
    start_copies(y_copies)
    lax.fori_loop(EARLY, STEPS, alone, 0)
    begin_round(1)
    await_copies(y_copies)
    strips(OWN)
    lax.fori_loop(0, STEPS // 2, functools.partial(alone_strips, False), 0)
    lax.fori_loop(STEPS // 2, STEPS, functools.partial(alone_strips, True), 0)
    begin_round(2)
    rows_at_once = 8
    for start in range(0, total, rows_at_once):
        part = pl.ds(start, rows_at_once)
        carry = (
            jnp.full((rows_at_once, CY), scale, jnp.float32),
            jnp.zeros((rows_at_once, CY), jnp.float32),
            block.at(0, start, rows_at_once),
            block.at(1, start, rows_at_once),
        )
        for bit in range(max(1, (nx - 1).bit_length())):
            carry = power(bit, carry)
        phase[part, :] = carry[0]
        phase[pl.ds(total + start, rows_at_once), :] = carry[1]
    await_copies(x_copies)
    await_copies(corner_copies)
    for z in range(NZ):
        spot = pl.ds(z * GHOST, GHOST)
        ids[z, pl.ds(HALO - GHOST, GHOST), :] = left_ids[spot, :]
        ids[z, pl.ds(HALO + CX, GHOST), :] = right_ids[spot, :]
    strips((0, 3))
    coefficients((0, 3))

    def send_strips(kinds, n, carry):
        for k in kinds:
            send_trace(n, k)
        return carry

    lax.fori_loop(0, STEPS // 2, functools.partial(send_strips, (2, 3)), 0)
    lax.fori_loop(STEPS // 2, STEPS, functools.partial(send_strips, (4, 5)), 0)
    lax.fori_loop(0, STEPS // 2, functools.partial(correct, (0, 2)), 0)
    lax.fori_loop(STEPS // 2, STEPS, functools.partial(correct, (0, 1, 2)), 0)
    begin_round(3)
    lax.fori_loop(0, STEPS // 2, functools.partial(correct_strips, (0, 2), False), 0)
    lax.fori_loop(STEPS // 2, STEPS, functools.partial(correct_strips, (0, 1, 2), True), 0)

    for k in range(4, len(rounds)):
        begin_round(k)
    for n in range(STEPS):
        for c in range(4):
            for k in range(2):
                spot = pl.ds(c * CX + 8 * k, 8)
                end = strip_samples[n, spot, :]
                value = jnp.where(lane < 8, pltpu.roll(end, 56, 1), samples[n, spot, :])
                value = jnp.where(lane >= CY - 8, pltpu.roll(end, 16, 1), value)
                sample[pl.ds(n * 4 * CX + c * CX + 8 * k, 8), :] = jnp.where(on_face[k], value, 0.0)
    for part in range(2):
        turned[part] = jnp.dot(
            sample[...],
            table[pl.ds(starts[part], CY), :],
            precision=lax.Precision.HIGHEST,
            preferred_element_type=f32,
        )
    for first in range(0, 4 * CX, 8):
        re, im = zero, zero
        for n in range(STEPS):
            g_re, g_im = (turned[part, pl.ds(n * 4 * CX + first, 8), :] for part in range(2))
            ct, st = time.at(0, n, 1), time.at(1, n, 1)
            re += ct * g_re + st * g_im
            im += ct * g_im - st * g_re
        acc[0, pl.ds(first, 8), :] = re
        acc[1, pl.ds(first, 8), :] = im

    end_round(len(rounds) - 1)
    yr, yi = y_start.at(0, iy, 1), y_start.at(1, iy, 1)
    col_re = acc[0] * yr - acc[1] * yi
    acc[1] = acc[0] * yi + acc[1] * yr
    acc[0] = col_re
    for part in range(2):
        for x in range(CX):
            four = acc[part, pl.ds(x, 4, stride=CX), :]
            cols[part, x, pl.ds(0, 4), :] = four
            cols[part, x, pl.ds(4, 4), :] = four

    upper = lax.broadcasted_iota(jnp.int32, (8, CY), 0) < 4
    at_once = min(8, total)

    def send_far(k):
        other = lax.rem(me + k, total)
        return pltpu.make_async_remote_copy(
            src_ref=f_send.at[k],
            dst_ref=f_recv.at[k - 1],
            send_sem=f_send_sem,
            recv_sem=f_recv_sem,
            device_id=(lax.div(other, nx), lax.rem(other, nx)),
            device_id_type=MESH,
        )

    def project(trip, carry):
        k0 = trip * at_once
        picked = [bands[lax.rem(me + k0 + j, total)] for j in range(at_once)]

        def pair(rows, part, j):
            return jnp.where(upper, rows.at(part, picked[j], 1), rows.at(part, picked[j + 1], 1))

        pairs = range(0, at_once, 2)
        wr = [pair(cell, 0, j) for j in pairs]
        wi = [pair(cell, 1, j) for j in pairs]
        c_re, c_im = cols[0, CX - 1], cols[1, CX - 1]
        re = [c_re for _ in pairs]
        im = [c_im for _ in pairs]
        for x in range(CX - 2, -1, -1):
            c_re, c_im = cols[0, x], cols[1, x]
            re, im = (
                [r * a - i * b + c_re for r, i, a, b in zip(re, im, wr, wi)],
                [r * b + i * a + c_im for r, i, a, b in zip(re, im, wr, wi)],
            )
        for t, j in enumerate(pairs):
            pr, pi = pair(start_phase, 0, j), pair(start_phase, 1, j)
            far_re = re[t] * pr - im[t] * pi
            far_im = re[t] * pi + im[t] * pr
            f_send[k0 + j] = jnp.where(upper, far_re, pltpu.roll(far_im, 4, 0))
            f_send[k0 + j + 1] = jnp.where(upper, pltpu.roll(far_re, 4, 0), far_im)
        for j in range(at_once):
            @pl.when(k0 + j > 0)
            def _(j=j):
                send_far(k0 + j).start()
        return carry

    lax.fori_loop(0, total // at_once, project, 0)

    for field, strip, more, strip_more, out in ((ef, se, ce, de, e_out), (hf, sh, ch, dh, h_out)):
        for c in range(3):
            for z in range(NZ):
                half, j = z // HALF, z % HALF
                for g in range(2):
                    end = strip[c, j, at(g), :] + strip_more[c, j, at(g, GHOST), :]
                    value = field[c, z, at(g), :] + more[c, z, at(g, GHOST), :]
                    value = jnp.where(lane < 8, pltpu.roll(end, (CY - 64 * half - 8) % CY, 1), value)
                    value = jnp.where(lane >= CY - 8, pltpu.roll(end, 80 - 64 * half, 1), value)
                    out[c, z, pl.ds(8 * g, 8), :] = value

    for i, (sends, _, src, dst, device) in enumerate(every):
        @pl.when(sends)
        def _(i=i, src=src, dst=dst, device=device):
            remote(i, src, dst, device).wait_send()

    def sent(kinds, n, carry):
        for k in kinds:
            @pl.when(traces[k][0])
            def _(k=k):
                trace(n, k).wait_send()
        return carry

    lax.fori_loop(0, STEPS // 2, functools.partial(sent, (0, 1, 2, 3)), 0)
    lax.fori_loop(STEPS // 2, STEPS, functools.partial(sent, (0, 1, 4, 5)), 0)
    pltpu.make_async_copy(f_recv, f_recv, f_send_sem).wait()

    pltpu.make_async_copy(f_recv, f_recv, f_recv_sem).wait()
    if total <= 64:
        terms = [f_send[0]] + [f_recv[k] for k in range(total - 1)]
        while len(terms) > 1:
            terms = [a + b for a, b in zip(terms[::2], terms[1::2])]
        far_out[...] = terms[0]
    else:
        far_out[...] = lax.fori_loop(0, total - 1, lambda k, t: t + f_recv[k], f_send[0])


def write_out(e, h, far, e_out, h_out, far_out, sem):
    copies = [
        pltpu.make_async_copy(src, dst, sem.at[i])
        for i, (src, dst) in enumerate(((e, e_out), (h, h_out), (far, far_out)))
    ]
    for copy in copies:
        copy.start()
    for copy in copies:
        copy.wait()


def local(ny, nx, electric, magnetic, material_ids, update_ca, update_cb, face_ranges, band_table):
    total = ny * nx
    bands = band_table.shape[0]
    assert bands == total and electric.shape == (3, NZ, CX, CY)
    scale = 1.0 / math.sqrt(CX * nx * CY * ny)
    f32 = jnp.float32
    vmem = pl.BlockSpec(memory_space=pltpu.VMEM)
    hbm = pl.BlockSpec(memory_space=pltpu.HBM)
    packed, starts = tables(bands, ny)
    e_out, h_out, far = pl.pallas_call(
        functools.partial(kernel, ny, nx, scale, starts),
        out_shape=(
            pltpu.VMEM(electric.shape, f32),
            pltpu.VMEM(electric.shape, f32),
            pltpu.VMEM((8, CY), f32),
        ),
        in_specs=[hbm] * 8,
        out_specs=(vmem,) * 3,
        scratch_shapes=[
            pltpu.VMEM((3, NZ, PITCH, CY), f32),
            pltpu.VMEM((3, NZ, PITCH, CY), f32),
            pltpu.VMEM((NZ, ROWS, CY), jnp.int32),
            pltpu.SMEM((NMAT,), f32),
            pltpu.SMEM((NMAT,), f32),
            pltpu.SMEM((4,), jnp.int32),
            pltpu.SMEM((bands,), jnp.int32),
            pltpu.VMEM(packed.shape, f32),
            pltpu.VMEM((3, NZ, CX, CY), f32),
            pltpu.VMEM((3, NZ, CX, CY), f32),
            pltpu.SemaphoreType.DMA((10,)),
            pltpu.VMEM((NZ, ROWS, CY), f32),
            pltpu.VMEM((NZ, ROWS, CY), f32),
            pltpu.VMEM((3, HALF, PITCH, CY), f32),
            pltpu.VMEM((3, HALF, PITCH, CY), f32),
            pltpu.VMEM((HALF, ROWS, CY), f32),
            pltpu.VMEM((HALF, ROWS, CY), f32),
            pltpu.VMEM((3, NZ, WIDE, CY), f32),
            pltpu.VMEM((3, NZ, WIDE, CY), f32),
            pltpu.VMEM((3, HALF, WIDE, CY), f32),
            pltpu.VMEM((3, HALF, WIDE, CY), f32),
            pltpu.VMEM((7, CX, CY), f32),
            pltpu.VMEM((7, CX, CY), f32),
            pltpu.VMEM((7, ROWS, CY), f32),
            pltpu.VMEM((7, ROWS, CY), f32),
            *[pltpu.VMEM((NZ * GHOST, CY), jnp.int32)] * 4,
            *[pltpu.VMEM((STEPS, 2 * NZ, CY), f32)] * 4,
            *[pltpu.VMEM((STEPS, 2 * HALF, CY), f32)] * 4,
            *[pltpu.VMEM((STEPS // 2, HALF, CY), f32)] * 4,
            pltpu.VMEM((STEPS, 4 * CX, CY), f32),
            pltpu.VMEM((STEPS, 4 * CX, CY), f32),
            pltpu.VMEM((STEPS * 4 * CX, CY), f32),
            pltpu.VMEM((2, STEPS * 4 * CX, CY), f32),
            pltpu.VMEM((2, 4 * CX, CY), f32),
            pltpu.VMEM((2, CX, 8, CY), f32),
            pltpu.VMEM((2 * total, CY), f32),
            pltpu.VMEM((total, 8, CY), f32),
            pltpu.VMEM((total - 1, 8, CY), f32),
            pltpu.SemaphoreType.DMA((8,)),
            pltpu.SemaphoreType.DMA((8,)),
            pltpu.SemaphoreType.DMA((STEPS, 4)),
            pltpu.SemaphoreType.DMA((STEPS, 4)),
            pltpu.SemaphoreType.REGULAR((len(round_offsets(ny, nx)),)),
            pltpu.SemaphoreType.DMA,
            pltpu.SemaphoreType.DMA,
        ],
        compiler_params=pltpu.CompilerParams(
            collective_id=0, has_side_effects=True, vmem_limit_bytes=62 * 1024 * 1024
        ),
        name="fdtd",
    )(
        electric,
        magnetic,
        material_ids,
        update_ca,
        update_cb,
        face_ranges.reshape(4),
        band_table,
        packed,
    )
    e_out, h_out, far = pl.pallas_call(
        write_out,
        out_shape=tuple(jax.ShapeDtypeStruct(value.shape, f32) for value in (e_out, h_out, far)),
        in_specs=[vmem] * 3,
        out_specs=(hbm,) * 3,
        scratch_shapes=[pltpu.SemaphoreType.DMA((3,))],
        name="write_out",
    )(*(pltpu.with_memory_space_constraint(value, pltpu.VMEM) for value in (e_out, h_out, far)))
    return e_out, h_out, far.reshape(1, 8, CY)


def solution(mesh):
    in_specs = (
        P(None, None, "inner", "grp"),
        P(None, None, "inner", "grp"),
        P(None, "inner", "grp"),
        P(),
        P(),
        P("inner", "grp", None),
        P(),
    )
    out_specs = (
        P(None, None, "inner", "grp"),
        P(None, None, "inner", "grp"),
        P(("grp", "inner"), None, None),
    )
    body = functools.partial(local, mesh.shape["grp"], mesh.shape["inner"])
    return jax.shard_map(body, mesh=mesh, in_specs=in_specs, out_specs=out_specs, check_vma=False)
```
